32 devices in a mesh: section: 2 (over core), dp: 4 (over z), tensor: 4 (over y, x).
Axes of the slice: x: 2, y: 2, z: 4, core: 2. Of those that a mesh axis runs over, the one named last changes fastest.
Arguments:
- inputs: float32 [2, 4096, 1024], P(None, ('dp', 'tensor')), may hold values from -6 to 6
- cotangent: float32 [2, 4096, 1024], P(None, ('dp', 'tensor')), may hold values from -6 to 6
- split: int32 [2, 4], P(None, 'dp'), may hold values from 0 to 1, as said below
- query_key_value_weight: bfloat16 [2, 1024, 3, 1024], P('section', 'dp', None, 'tensor'), may hold values from -0.1875 to 0.1875
- output_weight: bfloat16 [2, 1024, 1024], P('section', 'tensor', 'dp'), may hold values from -0.75 to 0.75
- up_weight: bfloat16 [2, 1024, 4096], P('section', 'dp', 'tensor'), may hold values from -0.1875 to 0.1875
- down_weight: bfloat16 [2, 4096, 1024], P('section', 'tensor', 'dp'), may hold values from -0.1875 to 0.1875
- qkv_adapter_input: float32 [2, 1024, 128], P('section'), may hold values from -0.1875 to 0.1875
- qkv_adapter_output: float32 [2, 128, 3, 1024], P('section', None, None, 'tensor'), may hold values from -0.5 to 0.5
- out_adapter_input: float32 [2, 1024, 128], P('section', 'tensor'), may hold values from -0.75 to 0.75
- out_adapter_output: float32 [2, 128, 1024], P('section'), may hold values from -0.5 to 0.5
- up_adapter_input: float32 [2, 1024, 128], P('section'), may hold values from -0.1875 to 0.1875
- up_adapter_output: float32 [2, 128, 4096], P('section', None, 'tensor'), may hold values from -0.5 to 0.5
- down_adapter_input: float32 [2, 4096, 128], P('section', 'tensor'), may hold values from -0.1875 to 0.1875
- down_adapter_output: float32 [2, 128, 1024], P('section'), may hold values from -0.5 to 0.5
- ln_gain: float32 [2, 2, 1024], P('section'), may hold values from 0.5 to 1.5
- ln_bias: float32 [2, 2, 1024], P('section'), may hold values from -2 to 2
Outputs:
- activations: float32 [2, 2, 4096, 1024], P('section', None, ('dp', 'tensor'))
- input_grads: float32 [2, 2, 4096, 1024], P('section', None, ('dp', 'tensor'))
- grad_a_qkv: float32 [2, 1024, 128], P('section')
- qkv_adapter_gradient: float32 [2, 128, 3, 1024], P('section', None, None, 'tensor')
- grad_a_out: float32 [2, 1024, 128], P('section', 'tensor')
- out_adapter_gradient: float32 [2, 128, 1024], P('section')
- grad_a_up: float32 [2, 1024, 128], P('section')
- up_adapter_gradient: float32 [2, 128, 4096], P('section', None, 'tensor')
- grad_a_down: float32 [2, 4096, 128], P('section', 'tensor')
- down_adapter_gradient: float32 [2, 128, 1024], P('section')
- grad_gain: float32 [2, 2, 1024], P('section')
- grad_bias: float32 [2, 2, 1024], P('section')
- combined_qkv_weight: float32 [2, 1024, 3, 1024], P('section', 'dp', None, 'tensor')
- combined_out_weight: float32 [2, 1024, 1024], P('section', 'tensor', 'dp')
- combined_up_weight: float32 [2, 1024, 4096], P('section', 'dp', 'tensor')
- combined_down_weight: float32 [2, 4096, 1024], P('section', 'tensor', 'dp')
The draws below stay inside these ranges and needn't reach their ends.
Inputs may be any that keep to these rules, and one draw needn't show every extreme that they name: `split`: in each micro-batch exactly 2 of the blocks hold two sequences (value 1), the others one (value 0).
All inputs are finite; a program needn't handle non-finite values.
Results may differ from the reference program's by a relative error of at most 0.023.
Values may be sent and summed in bfloat16 or wider, within the bound.
A program may use at most 256 MiB of HBM per device.

```python
from functools import partial
import jax
import jax.numpy as jnp
from jax import lax

D = 1024
HEADS = 16
HEAD = 64
FF = 4096
ROT = 16
RANK = 128
LONG = 1024
MICRO = 2
LAYERS = 2
SHARDS = 4
TOKENS = 4096


def draw_split(key, part):
    key = jax.random.fold_in(key, 7)
    subkeys = jax.random.split(key, MICRO)
    orders = jax.vmap(lambda subkey: jax.random.permutation(subkey, SHARDS))(subkeys)
    return (orders < SHARDS // 2).astype(jnp.int32)


def shard_levels(stream_key, extent, cuts, smallest, largest):
    loudness = 1.0
    for dim, parts in cuts:
        heights = jax.random.uniform(jax.random.fold_in(jax.random.fold_in(stream_key, 6), dim), (parts,), jnp.float32, smallest / len(cuts), largest / len(cuts))
        loudness = loudness * jnp.repeat(jnp.exp(heights), extent[dim] // parts).reshape((-1,) + (1,) * (len(extent) - 1 - dim))
    return loudness


def normal_values(own_key, shape, scale, bound, cuts=(), held_as=jnp.bfloat16):
    entries = jax.random.normal(own_key, shape, jnp.float32) * scale
    if len(cuts) > 0:
        entries = shard_levels(own_key, shape, cuts, -0.22, 0.18) * entries
    return jnp.clip(entries, min=-bound, max=bound).astype(held_as)


def setup_inputs(seed: int = 0) -> dict:
    seeds = jax.random.split(jax.random.key(seed), 18)
    inputs = normal_values(seeds[0], (MICRO, TOKENS, D), 1.0, 6.0, ((1, 16),), jnp.float32)
    cotangent = normal_values(seeds[1], (MICRO, TOKENS, D), 1.0, 6.0, ((1, 16),), jnp.float32)
    split = draw_split(jax.random.fold_in(seeds[17], 71), 0)
    query_key_value_weight = normal_values(seeds[3], (LAYERS, D, 3, D), D ** -0.5, 0.1875, ((0, 2), (1, 4), (3, 4)))
    output_weight = normal_values(seeds[4], (LAYERS, D, D), (D // 16) ** -0.5, 0.75, ((0, 2), (1, 4), (2, 4)))
    up_weight = normal_values(seeds[5], (LAYERS, D, FF), D ** -0.5, 0.1875, ((0, 2), (1, 4), (2, 4)))
    down_weight = normal_values(seeds[6], (LAYERS, FF, D), (FF // 4) ** -0.5, 0.1875, ((0, 2), (1, 4), (2, 4)))
    qkv_adapter_input = normal_values(seeds[7], (LAYERS, D, RANK), D ** -0.5, 0.1875, ((0, 2),), jnp.float32)
    qkv_adapter_output = normal_values(seeds[8], (LAYERS, RANK, 3, D), RANK ** -0.5, 0.5, ((0, 2), (3, 4)), jnp.float32)
    out_adapter_input = normal_values(seeds[9], (LAYERS, D, RANK), (D // 16) ** -0.5, 0.75, ((0, 2), (1, 4)), jnp.float32)
    out_adapter_output = normal_values(seeds[10], (LAYERS, RANK, D), RANK ** -0.5, 0.5, ((0, 2),), jnp.float32)
    up_adapter_input = normal_values(seeds[11], (LAYERS, D, RANK), D ** -0.5, 0.1875, ((0, 2),), jnp.float32)
    up_adapter_output = normal_values(seeds[12], (LAYERS, RANK, FF), RANK ** -0.5, 0.5, ((0, 2), (2, 4)), jnp.float32)
    down_adapter_input = normal_values(seeds[13], (LAYERS, FF, RANK), (FF // 4) ** -0.5, 0.1875, ((0, 2), (1, 4)), jnp.float32)
    down_adapter_output = normal_values(seeds[14], (LAYERS, RANK, D), RANK ** -0.5, 0.5, ((0, 2),), jnp.float32)
    ln_gain = jnp.clip(1.0 + 0.1 * jax.random.normal(seeds[15], (LAYERS, 2, D), jnp.float32), 0.5, 1.5)
    ln_bias = normal_values(seeds[16], (LAYERS, 2, D), 0.3, 2.0, ((0, 2),), jnp.float32)
    return {"inputs": inputs, "cotangent": cotangent, "split": split, "query_key_value_weight": query_key_value_weight, "output_weight": output_weight, "up_weight": up_weight, "down_weight": down_weight, "qkv_adapter_input": qkv_adapter_input, "qkv_adapter_output": qkv_adapter_output, "out_adapter_input": out_adapter_input, "out_adapter_output": out_adapter_output, "up_adapter_input": up_adapter_input, "up_adapter_output": up_adapter_output, "down_adapter_input": down_adapter_input, "down_adapter_output": down_adapter_output, "ln_gain": ln_gain, "ln_bias": ln_bias}


ADAPTER_SCALE = 0.25
EPSILON = 1e-05
MASKED = -1e+30
FULL_PRECISION = lax.Precision.HIGHEST

@jax.custom_vjp
def reduced_product(v):
    return lax.optimization_barrier(v.astype(jnp.bfloat16)).astype(jnp.float32)

@jax.custom_vjp
def reduced_backward(v):
    return v

def low_keep(v):
    return (reduced_product(v), None)

def low_pass(kept, grad):
    return (grad,)

def back_keep(v):
    return (v, None)

def back_low(kept, grad):
    return (reduced_product(grad),)
reduced_product.defvjp(low_keep, low_pass)
reduced_backward.defvjp(back_keep, back_low)

def matrix_multiply(left_side, right_side):
    return jnp.dot(left_side, right_side, precision=FULL_PRECISION, preferred_element_type=jnp.float32)

def layer_norms(source, gain_rows, bias_rows):
    row_mean = lax.optimization_barrier(jnp.mean(source, axis=-1, keepdims=True))
    centred = source - row_mean
    spread = lax.optimization_barrier(jnp.mean(centred * centred, axis=-1, keepdims=True))
    normed = centred * lax.rsqrt(spread + EPSILON)
    return (normed * gain_rows[0] + bias_rows[0], normed * gain_rows[1] + bias_rows[1])

def geometry(split_flag, length):
    token_index = jnp.arange(length, dtype=jnp.int32)
    second_doc = (token_index >= length // 2).astype(jnp.int32) * split_flag
    places = (token_index - length // 2 * second_doc).astype(jnp.float32)
    half_rot = ROT // 2
    inverse = 10000.0 ** (-jnp.arange(half_rot, dtype=jnp.float32) * 2.0 / ROT)
    angles = places[:, None] * inverse[None, :]
    angles = jnp.concatenate([angles, angles], axis=-1)[:, None, :]
    allowed = (token_index[:, None] >= token_index[None, :]) & (second_doc[:, None] == second_doc[None, :])
    return (jnp.cos(angles), jnp.sin(angles), allowed)

def rotate(heads_view, cosine_table, sine_table):
    half_rot = ROT // 2
    leading_part = heads_view[..., :ROT]
    turned = jnp.concatenate([-leading_part[..., half_rot:], leading_part[..., :half_rot]], axis=-1)
    return jnp.concatenate([leading_part * cosine_table + turned * sine_table, heads_view[..., ROT:]], axis=-1)

def weights_of(scores, allowed):
    masked_scores = jnp.where(allowed[None], scores, MASKED)
    row_max = lax.optimization_barrier(jnp.max(masked_scores, axis=-1, keepdims=True))
    exponent = jnp.exp(masked_scores - row_max)
    return exponent / lax.optimization_barrier(jnp.sum(exponent, axis=-1, keepdims=True))

def attend(packed):
    block, split_flag = packed
    cosine_table, sine_table, allowed = geometry(split_flag, block.shape[0])
    queries = reduced_product(rotate(block[:, 0], cosine_table, sine_table))
    key_heads = reduced_product(rotate(block[:, 1], cosine_table, sine_table))
    value_heads = reduced_product(block[:, 2])
    scores = reduced_backward(jnp.einsum('qhd,khd->hqk', queries, key_heads, precision=FULL_PRECISION) * 0.125)
    probabilities = reduced_product(weights_of(scores, allowed))
    attention_result = jnp.einsum('hqk,khd->qhd', probabilities, value_heads, precision=FULL_PRECISION)
    return attention_result.reshape(attention_result.shape[0], -1)

def layer(source, trained, split_flags, frozen):
    qkv_weight_full, output_weight_full, up_weight_full, down_weight_full = frozen
    fac_a_qkv, qkv_output_factor, fac_a_out, out_output_factor, fac_a_up, up_output_factor, fac_a_down, down_output_factor, gain_rows, bias_rows = trained
    first_normalized, second_normalized = layer_norms(source, gain_rows, bias_rows)
    first_normalized = reduced_product(first_normalized)
    second_normalized = reduced_product(second_normalized)
    qkv_reduced = reduced_backward(reduced_product(matrix_multiply(first_normalized, reduced_product(fac_a_qkv))))
    up_reduced = reduced_backward(reduced_product(matrix_multiply(second_normalized, reduced_product(fac_a_up))))
    joined_rows = reduced_backward(matrix_multiply(first_normalized, qkv_weight_full.reshape(qkv_weight_full.shape[0], -1)) + ADAPTER_SCALE * matrix_multiply(qkv_reduced, reduced_product(qkv_output_factor).reshape(qkv_output_factor.shape[0], -1)))
    hidden_rows = reduced_backward(matrix_multiply(second_normalized, up_weight_full) + ADAPTER_SCALE * matrix_multiply(up_reduced, reduced_product(up_output_factor)))
    blocks = joined_rows.reshape(SHARDS, LONG, 3, HEADS, HEAD)
    attention_result = lax.map(jax.checkpoint(attend), (blocks, split_flags)).reshape(SHARDS * LONG, HEADS * HEAD)
    attention_result = reduced_product(reduced_backward(attention_result))
    activated_rows = reduced_product(jax.nn.gelu(hidden_rows, approximate=False))
    out_reduced = reduced_backward(reduced_product(matrix_multiply(attention_result, reduced_product(fac_a_out))))
    down_reduced = reduced_backward(reduced_product(matrix_multiply(activated_rows, reduced_product(fac_a_down))))
    branch_output = matrix_multiply(attention_result, output_weight_full) + matrix_multiply(activated_rows, down_weight_full) + ADAPTER_SCALE * (matrix_multiply(out_reduced, reduced_product(out_output_factor)) + matrix_multiply(down_reduced, reduced_product(down_output_factor)))
    return source + reduced_backward(branch_output)

def merge_weights(query_key_value_weight, output_weight, up_weight, down_weight, qkv_adapter_input, qkv_adapter_output, out_adapter_input, out_adapter_output, up_adapter_input, up_adapter_output, down_adapter_input, down_adapter_output):
    combined_qkv_weight = query_key_value_weight + ADAPTER_SCALE * jnp.einsum('wsv,wvao->wsao', qkv_adapter_input, qkv_adapter_output, precision=FULL_PRECISION)
    combined_out_weight = output_weight + ADAPTER_SCALE * jnp.einsum('zcy,zyj->zcj', out_adapter_input, out_adapter_output, precision=FULL_PRECISION)
    combined_up_weight = up_weight + ADAPTER_SCALE * jnp.einsum('zcy,zyj->zcj', up_adapter_input, up_adapter_output, precision=FULL_PRECISION)
    combined_down_weight = down_weight + ADAPTER_SCALE * jnp.einsum('zcy,zyj->zcj', down_adapter_input, down_adapter_output, precision=FULL_PRECISION)
    return (combined_qkv_weight, combined_out_weight, combined_up_weight, combined_down_weight)

def reference(inputs, cotangent, split, query_key_value_weight, output_weight, up_weight, down_weight, qkv_adapter_input, qkv_adapter_output, out_adapter_input, out_adapter_output, up_adapter_input, up_adapter_output, down_adapter_input, down_adapter_output, ln_gain, ln_bias):
    frozen = [tuple((member[layer_index].astype(jnp.float32) for member in (query_key_value_weight, output_weight, up_weight, down_weight))) for layer_index in range(LAYERS)]
    trained = [tuple((member[layer_index].astype(jnp.float32) for member in (qkv_adapter_input, qkv_adapter_output, out_adapter_input, out_adapter_output, up_adapter_input, up_adapter_output, down_adapter_input, down_adapter_output, ln_gain, ln_bias))) for layer_index in range(LAYERS)]
    totals = [tuple((jnp.zeros_like(member) for member in trained[layer_index])) for layer_index in range(LAYERS)]
    outputs_all = []
    grads_all = []
    for batch_index in range(MICRO):
        current = inputs[batch_index].astype(jnp.float32)
        pullbacks = []
        produced = []
        for layer_index in range(LAYERS):
            current, pullback = jax.vjp(partial(layer, split_flags=split[batch_index], frozen=frozen[layer_index]), current, trained[layer_index])
            pullbacks.append(pullback)
            produced.append(current)
        flowing = cotangent[batch_index].astype(jnp.float32)
        handed = [None] * LAYERS
        for layer_index in reversed(range(LAYERS)):
            flowing, received_grads = pullbacks[layer_index](flowing)
            handed[layer_index] = flowing
            totals[layer_index] = tuple((first_term + second_term for first_term, second_term in zip(totals[layer_index], received_grads)))
        outputs_all.append(produced)
        grads_all.append(handed)
    activations = jnp.stack([jnp.stack([outputs_all[batch_index][layer_index] for batch_index in range(MICRO)]) for layer_index in range(LAYERS)])
    input_grads = jnp.stack([jnp.stack([grads_all[batch_index][layer_index] for batch_index in range(MICRO)]) for layer_index in range(LAYERS)])
    stacked = [jnp.stack([totals[layer_index][position] for layer_index in range(LAYERS)]) for position in range(10)]
    merged, unused_pull = jax.vjp(merge_weights, query_key_value_weight.astype(jnp.float32), output_weight.astype(jnp.float32), up_weight.astype(jnp.float32), down_weight.astype(jnp.float32), qkv_adapter_input.astype(jnp.float32), qkv_adapter_output.astype(jnp.float32), out_adapter_input.astype(jnp.float32), out_adapter_output.astype(jnp.float32), up_adapter_input.astype(jnp.float32), up_adapter_output.astype(jnp.float32), down_adapter_input.astype(jnp.float32), down_adapter_output.astype(jnp.float32))
    combined_qkv_weight, combined_out_weight, combined_up_weight, combined_down_weight = merged
    return (activations, input_grads, stacked[0], stacked[1], stacked[2], stacked[3], stacked[4], stacked[5], stacked[6], stacked[7], stacked[8], stacked[9], combined_qkv_weight, combined_out_weight, combined_up_weight, combined_down_weight)
```

```python
import functools

import jax
import jax.numpy as jnp
from jax import lax
from jax.experimental import pallas as pl
from jax.experimental.pallas import tpu as pltpu
from jax.sharding import PartitionSpec as P

HEAD = 64
ROT = 16
ADAPTER_SCALE = 0.25
EPSILON = 1e-05
MASKED = -1e30
BF = jnp.bfloat16
F32 = jnp.float32
MESH = pl.DeviceIdType.MESH


def nn(a, b):
    return lax.dot_general(a, b, (((1,), (0,)), ((), ())), preferred_element_type=F32)


def nt(a, b):
    return lax.dot_general(a, b, (((1,), (1,)), ((), ())), preferred_element_type=F32)


def make_kernel(T, DP, M, R, D, QC, FFL, RANK):
    L = R * T
    DR = D // DP
    W = D + 2 * RANK
    PAIRS = QC // 128
    HEADS = QC // HEAD
    TILE = 256
    HALF = L // 2

    def kernel(
        x_in, ct_in, wq_in, wup_in, wout_in, wdn_in,
        aq, bq, ao, bo, au, bu, ad, bd, gain, bias, cos_t, sin_t, negb,
        act, ig, ga_out, gr_out, gb_out, h_hbm, dg_hbm,
        wq, wup, wout, wdn, xh, t12t, qh, kp, vp, kT, vT, oT, lse, hw, dg,
        todt, sbuf, rbuf, sxr, sgr, sxs, dz, doh, delta, edot, dk, dv, dqt, dqkv,
        ga, gr, gb, xw, yw,
        w_ls, w_ss, w_rs, x_ss, x_rs, r_ss, r_rs, z_ss, z_rs, c_ss, c_rs, l_s,
    ):
        s = lax.axis_index("section")
        d = lax.axis_index("dp")
        t = lax.axis_index("tensor")
        other = 1 - s

        barrier = pltpu.get_barrier_semaphore()
        for k in range(1, T):
            pl.semaphore_signal(
                barrier, inc=1, device_id={"tensor": lax.rem(t + k, T)}, device_id_type=MESH
            )
        for k in range(1, DP):
            pl.semaphore_signal(
                barrier, inc=1, device_id={"dp": lax.rem(d + k, DP)}, device_id_type=MESH
            )
        pl.semaphore_signal(barrier, inc=1, device_id={"section": other}, device_id_type=MESH)
        pl.semaphore_wait(barrier, T + DP - 1)

        def weight_refs(index, owner):
            if index < 2:
                rows = pl.ds(pl.multiple_of(owner * DR, DR), DR)
                return (wq_in, wup_in)[index], (wq, wup)[index].at[rows]
            return (wout_in, wdn_in)[index - 2], (wout, wdn)[index - 2].at[owner]

        def weight_copy(index, k):
            src, dst = weight_refs(index, d)
            return pltpu.make_async_remote_copy(
                src_ref=src, dst_ref=dst,
                send_sem=w_ss.at[index, k - 1], recv_sem=w_rs.at[index, k - 1],
                device_id={"dp": lax.rem(d + k, DP)}, device_id_type=MESH,
            )

        def weight_local(index):
            src, dst = weight_refs(index, d)
            return pltpu.make_async_copy(src, dst, w_ls.at[index])

        for index in range(4):
            weight_local(index).start()
            for k in range(1, DP):
                weight_copy(index, k).start()

        def weights_ready(index):
            weight_local(index).wait()
            for k in range(1, DP):
                weight_copy(index, k).wait_recv()

        ga[...] = jnp.zeros_like(ga)
        gr[...] = jnp.zeros_like(gr)
        gb[...] = jnp.zeros_like(gb)

        def rows_copy(buf, m, k, ssem, rsem):
            place = m * T + t
            return pltpu.make_async_remote_copy(
                src_ref=buf.at[place], dst_ref=buf.at[place],
                send_sem=ssem.at[k - 1], recv_sem=rsem.at[m * (T - 1) + k - 1],
                device_id={"tensor": lax.rem(t + k, T)}, device_id_type=MESH,
            )

        def rows_wait(buf, m, c, ssem, rsem):
            place = m * T + lax.rem(t - c + T, T)
            pltpu.make_async_remote_copy(
                src_ref=buf.at[place], dst_ref=buf.at[place],
                send_sem=ssem.at[0], recv_sem=rsem.at[m * (T - 1) + c - 1],
                device_id={"tensor": lax.rem(t + 1, T)}, device_id_type=MESH,
            ).wait_recv()

        def block_copy(phase, i):
            k = lax.rem(i - t + T, T)
            slot = phase * (T - 1) + k - 1
            return pltpu.make_async_remote_copy(
                src_ref=sbuf.at[i], dst_ref=rbuf.at[slot],
                send_sem=r_ss.at[i], recv_sem=r_rs.at[slot],
                device_id={"tensor": i}, device_id_type=MESH,
            )

        def block_wait(phase, k):
            slot = phase * (T - 1) + k - 1
            pltpu.make_async_remote_copy(
                src_ref=sbuf.at[0], dst_ref=rbuf.at[slot],
                send_sem=r_ss.at[0], recv_sem=r_rs.at[slot],
                device_id={"tensor": lax.rem(t + k, T)}, device_id_type=MESH,
            ).wait_recv()

        def section_copy(m, phase):
            dst = (sxr, sgr)[phase]
            return pltpu.make_async_remote_copy(
                src_ref=sxs, dst_ref=dst.at[m],
                send_sem=c_ss.at[0], recv_sem=c_rs.at[phase * M + m],
                device_id={"section": other}, device_id_type=MESH,
            )

        def local_copy(src, dst, index):
            return pltpu.make_async_copy(src, dst, l_s.at[index])

        def norm_parts(x):
            mean = jnp.mean(x, axis=-1, keepdims=True)
            centred = x - mean
            spread = jnp.mean(centred * centred, axis=-1, keepdims=True)
            rstd = lax.rsqrt(spread + EPSILON)
            return centred * rstd, rstd

        def load_x(m):
            @pl.when(s == 0)
            def _():
                copy = local_copy(x_in.at[m], xw, 0)
                copy.start()
                copy.wait()

        lane = lax.broadcasted_iota(jnp.int32, (R, 128), 1)
        in_first = lax.rem(lane, HEAD) < ROT // 2
        head_low = lane < HEAD

        def turn(v, cosine, sine):
            swapped = jnp.where(in_first, pltpu.roll(v, 128 - ROT // 2, 1), pltpu.roll(v, ROT // 2, 1))
            return v * cosine + swapped * sine

        causal = lax.broadcasted_iota(jnp.int32, (R, R), 0) <= lax.broadcasted_iota(
            jnp.int32, (R, R), 1
        )

        def scores_t(m, p, i, j, q):
            keys = kp[m * PAIRS + p, j * R:(j + 1) * R, :]
            sc = nt(keys, q)
            if j == i:
                sc = jnp.where(causal, sc, MASKED)
            if i * R >= HALF and j * R < HALF:
                sc = sc + negb[m]
            return sc

        def forward(m, carry):
            load_x(m)

            @pl.when(s == 1)
            def _():
                section_copy(m, 0).wait_recv()
                xw[...] = sxr[m].astype(F32)

            xhat, _ = norm_parts(xw[...])
            xh[m * T + t] = xhat.astype(BF)
            for k in range(1, T):
                rows_copy(xh, m, k, x_ss, x_rs).start()

            @pl.when(m == 0)
            def _():
                weights_ready(0)
                weights_ready(1)

            def chunk(c, carry):
                src = lax.rem(t - c + T, T)

                @pl.when(c > 0)
                def _():
                    rows_wait(xh, m, c, x_ss, x_rs)

                rows = pl.ds(pl.multiple_of(src * R, R), R)
                xhc = xh[m * T + src].astype(F32)
                n1 = (xhc * gain[0:1] + bias[0:1]).astype(BF)
                n2 = (xhc * gain[1:2] + bias[1:2]).astype(BF)
                t1 = nn(n1, aq[...]).astype(BF)
                t2 = nn(n2, au[...]).astype(BF)
                t12t[m, 0:RANK, rows] = t1.T
                t12t[m, RANK:2 * RANK, rows] = t2.T
                cosine = cos_t[m, rows, :]
                sine = sin_t[m, rows, :]
                for part in range(3):
                    cols = slice(part * QC, (part + 1) * QC)
                    val = nn(n1, wq[:, cols]) + nn(t1, bq[:, cols])
                    if part == 2:
                        vb = val.astype(BF)
                        for p in range(PAIRS):
                            vp[m * PAIRS + p, rows, :] = vb[:, p * 128:(p + 1) * 128]
                        vT[:, rows] = vb.T
                    else:
                        for p in range(PAIRS):
                            v = turn(val[:, p * 128:(p + 1) * 128], cosine, sine)
                            if part == 0:
                                v = v * 0.125
                                qh[m * HEADS + 2 * p, rows, :] = jnp.where(head_low, v, 0.0).astype(BF)
                                qh[m * HEADS + 2 * p + 1, rows, :] = jnp.where(head_low, 0.0, v).astype(BF)
                            else:
                                vb = v.astype(BF)
                                kp[m * PAIRS + p, rows, :] = vb
                                kT[m, p * 128:(p + 1) * 128, rows] = vb.T
                for n0 in range(0, FFL, TILE):
                    cols = slice(n0, n0 + TILE)
                    u = nn(n2, wup[:, cols]) + nn(t2, bu[:, cols])
                    phi = 0.5 * (1.0 + lax.erf(u * 0.7071067811865476))
                    hw[rows, cols] = (u * phi).astype(BF)
                    dg[rows, cols] = (
                        phi + u * (0.3989422804014327 * jnp.exp(-0.5 * u * u))
                    ).astype(BF)
                return carry

            lax.fori_loop(0, T, chunk, 0)
            for k in range(1, T):
                rows_copy(xh, m, k, x_ss, x_rs).wait_send()
            local_copy(hw, h_hbm.at[m], 1).start()
            local_copy(dg, dg_hbm.at[m], 2).start()

            @pl.when(m == 0)
            def _():
                weights_ready(2)
                weights_ready(3)

            for i in range(T):
                icols = slice(i * R, (i + 1) * R)

                def pair(p, carry, i=i, icols=icols):
                    for hh in range(2):
                        h = 2 * p + hh
                        q = qh[m * HEADS + h, icols, :]
                        hrows = pl.ds(pl.multiple_of(h * HEAD, HEAD), HEAD)
                        blocks = [scores_t(m, p, i, j, q) for j in range(i + 1)]
                        top = functools.reduce(
                            jnp.maximum, [jnp.max(b, axis=0, keepdims=True) for b in blocks]
                        )
                        total = jnp.zeros_like(top)
                        acc = jnp.zeros((HEAD, R), F32)
                        for j in range(i + 1):
                            e = jnp.exp(blocks[j] - top)
                            total = total + jnp.sum(e, axis=0, keepdims=True)
                            acc = acc + nn(vT[hrows, j * R:(j + 1) * R], e.astype(BF))
                        oT[m, hrows, icols] = (acc * (1.0 / total)).astype(BF)
                        lse[pl.ds(m * HEADS + h, 1), icols] = top + jnp.log(total)
                    return carry

                lax.fori_loop(0, PAIRS, pair, 0)
                o = oT[m, :, icols].T
                hrow = hw[icols, :]
                for j in range(DP):
                    sbuf[i, :, j * DR:(j + 1) * DR] = (nn(o, wout[j]) + nn(hrow, wdn[j])).astype(BF)
                sbuf[i, :, D:D + RANK] = nn(o, ao[...]).astype(BF)
                sbuf[i, :, D + RANK:W] = nn(hrow, ad[...]).astype(BF)

                @pl.when(t != i)
                def _(i=i):
                    block_copy(m, i).start()

            for k in range(1, T):
                block_wait(m, k)

            def summed(lo, hi):
                v = sbuf[t, :, lo:hi].astype(F32)
                for k in range(T - 1):
                    v = v + rbuf[m * (T - 1) + k, :, lo:hi].astype(F32)
                return v

            to = summed(D, D + RANK).astype(BF)
            td = summed(D + RANK, W).astype(BF)
            todt[m, 0:RANK, :] = to.T
            todt[m, RANK:2 * RANK, :] = td.T
            for n0 in range(0, D, TILE):
                cols = slice(n0, n0 + TILE)
                y = xw[:, cols] + summed(n0, n0 + TILE) + nn(to, bo[:, cols]) + nn(td, bd[:, cols])
                xw[:, cols] = y
                sxs[:, cols] = y.astype(BF)

            @pl.when(s == 0)
            def _():
                section_copy(m, 0).start()

            out = local_copy(xw, act.at[m], 3)
            out.start()
            out.wait()
            for i in range(T):
                @pl.when(t != i)
                def _(i=i):
                    block_copy(m, i).wait_send()
            local_copy(hw, h_hbm.at[m], 1).wait()
            local_copy(dg, dg_hbm.at[m], 2).wait()

            @pl.when(s == 0)
            def _():
                section_copy(m, 0).wait_send()
            return carry

        lax.fori_loop(0, M, forward, 0)

        def backward(m, carry):
            local_copy(dg_hbm.at[m], dg, 2).start()
            local_copy(h_hbm.at[m], hw, 1).start()

            @pl.when(s == 1)
            def _():
                copy = local_copy(ct_in.at[m], yw, 3)
                copy.start()
                copy.wait()
                xw[...] = sxr[m].astype(F32)

            @pl.when(s == 0)
            def _():
                section_copy(m, 1).wait_recv()
                yw[...] = sgr[m].astype(F32)

            load_x(m)
            dz[m * T + t] = yw[...].astype(BF)
            for k in range(1, T):
                rows_copy(dz, m, k, z_ss, z_rs).start()
            dk[...] = jnp.zeros_like(dk)
            dv[...] = jnp.zeros_like(dv)
            local_copy(dg_hbm.at[m], dg, 2).wait()

            def chunk(c, carry):
                src = lax.rem(t - c + T, T)

                @pl.when(c > 0)
                def _():
                    rows_wait(dz, m, c, z_ss, z_rs)

                rows = pl.ds(pl.multiple_of(src * R, R), R)
                place = m * T + src
                full = dz[place]
                eo = nt(full, bo[...]).astype(BF)
                ed = nt(full, bd[...]).astype(BF)
                edot[0:RANK, rows] = eo.T
                edot[RANK:2 * RANK, rows] = ed.T
                do = nt(eo, ao[...])
                for j in range(DP):
                    do = do + nt(full[:, j * DR:(j + 1) * DR], wout[j])
                dob = do.astype(BF)
                for p in range(PAIRS):
                    v = dob[:, p * 128:(p + 1) * 128]
                    zero = jnp.zeros_like(v)
                    doh[2 * p, rows, :] = jnp.where(head_low, v, zero)
                    doh[2 * p + 1, rows, :] = jnp.where(head_low, zero, v)
                prod = dob.T.astype(F32) * oT[m, :, rows].astype(F32)
                for h in range(HEADS):
                    delta[h:h + 1, rows] = jnp.sum(
                        prod[h * HEAD:(h + 1) * HEAD], axis=0, keepdims=True
                    )
                for n0 in range(0, FFL, TILE):
                    cols = slice(n0, n0 + TILE)
                    v = nt(ed, ad[cols, :])
                    for j in range(DP):
                        v = v + nt(full[:, j * DR:(j + 1) * DR], wdn[j, cols, :])
                    dg[rows, cols] = (v * dg[rows, cols].astype(F32)).astype(BF)
                return carry

            lax.fori_loop(0, T, chunk, 0)
            for k in range(1, T):
                rows_copy(dz, m, k, z_ss, z_rs).wait_send()

            for i in range(T):
                icols = slice(i * R, (i + 1) * R)

                def pair(p, carry, i=i, icols=icols):
                    for hh in range(2):
                        h = 2 * p + hh
                        q = qh[m * HEADS + h, icols, :]
                        do = doh[h, icols, :]
                        hrows = pl.ds(pl.multiple_of(h * HEAD, HEAD), HEAD)
                        low = lse[pl.ds(m * HEADS + h, 1), icols]
                        dlt = delta[pl.ds(h, 1), icols]
                        acc = jnp.zeros((HEAD, R), F32)
                        for j in range(i + 1):
                            jrows = slice(j * R, (j + 1) * R)
                            prob = jnp.exp(scores_t(m, p, i, j, q) - low)
                            dp_t = nt(vp[m * PAIRS + p, jrows, :], do)
                            ds_t = (prob * (dp_t - dlt)).astype(BF)
                            dv[p, jrows, :] += nn(prob.astype(BF), do)
                            dk[p, jrows, :] += nn(ds_t, q)
                            acc = acc + nn(kT[m, hrows, jrows], ds_t)
                        dqt[hrows, icols] = acc
                    return carry

                lax.fori_loop(0, PAIRS, pair, 0)

            def tail(c, carry):
                i = lax.rem(t + c + 1, T)
                rows = pl.ds(pl.multiple_of(i * R, R), R)
                cosine = cos_t[m, rows, :]
                sine = -sin_t[m, rows, :]
                dq = dqt[:, rows].T * 0.125
                for p in range(PAIRS):
                    lanes = slice(p * 128, (p + 1) * 128)
                    dqkv[rows, p * 128:(p + 1) * 128] = turn(dq[:, lanes], cosine, sine).astype(BF)
                    dqkv[rows, QC + p * 128:QC + (p + 1) * 128] = turn(
                        dk[p, rows, :], cosine, sine
                    ).astype(BF)
                    dqkv[rows, 2 * QC + p * 128:2 * QC + (p + 1) * 128] = dv[p, rows, :].astype(BF)
                dj = dqkv[rows, :]
                du = dg[rows, :]
                for n0 in range(0, D, TILE):
                    cols = slice(n0, n0 + TILE)
                    dn1 = nt(dj, wq[cols, :])
                    dn2 = nt(du, wup[cols, :])
                    xhc = xh[m * T + i, :, cols].astype(F32)
                    gb[0:1, cols] += jnp.sum(dn1 * xhc, axis=0, keepdims=True)
                    gb[1:2, cols] += jnp.sum(dn2 * xhc, axis=0, keepdims=True)
                    gb[2:3, cols] += jnp.sum(dn1, axis=0, keepdims=True)
                    gb[3:4, cols] += jnp.sum(dn2, axis=0, keepdims=True)
                    sbuf[i, :, cols] = (dn1 * gain[0:1, cols] + dn2 * gain[1:2, cols]).astype(BF)
                sbuf[i, :, D:D + RANK] = nt(dj, bq[...]).astype(BF)
                sbuf[i, :, D + RANK:W] = nt(du, bu[...]).astype(BF)

                @pl.when(t != i)
                def _():
                    block_copy(M + m, i).start()
                return carry

            lax.fori_loop(0, T, tail, 0)

            local_copy(h_hbm.at[m], hw, 1).wait()
            base = 0
            ga[:, base:base + 3 * QC] += ADAPTER_SCALE * nn(t12t[m, 0:RANK, :], dqkv[...])
            base += 3 * QC
            ga[:, base:base + FFL] += ADAPTER_SCALE * nn(t12t[m, RANK:2 * RANK, :], dg[...])
            base += FFL
            ga[:, base:base + QC] += nt(edot[0:RANK, :], oT[m])
            base += QC
            ga[:, base:base + FFL] += nn(edot[RANK:2 * RANK, :], hw[...])
            own = dz[m * T + t]
            gr[:, 2 * D:3 * D] += ADAPTER_SCALE * nn(todt[m, 0:RANK, :], own)
            gr[:, 3 * D:4 * D] += ADAPTER_SCALE * nn(todt[m, RANK:2 * RANK, :], own)

            for k in range(1, T):
                block_wait(M + m, k)

            def summed(lo, hi):
                v = sbuf[t, :, lo:hi].astype(F32)
                for k in range(T - 1):
                    v = v + rbuf[(M + m) * (T - 1) + k, :, lo:hi].astype(F32)
                return v

            e1 = summed(D, D + RANK).astype(BF)
            e2 = summed(D + RANK, W).astype(BF)
            xhat, rstd = norm_parts(xw[...])
            xw[...] = xhat
            n1 = (xhat * gain[0:1] + bias[0:1]).astype(BF)
            n2 = (xhat * gain[1:2] + bias[1:2]).astype(BF)
            gr[:, 0:D] += nn(e1.T, n1)
            gr[:, D:2 * D] += nn(e2.T, n2)
            pieces = []
            mean_g = jnp.zeros((R, 1), F32)
            mean_gx = jnp.zeros((R, 1), F32)
            for n0 in range(0, D, TILE):
                cols = slice(n0, n0 + TILE)
                dn1 = nt(e1, aq[cols, :])
                dn2 = nt(e2, au[cols, :])
                xhc = xw[:, cols]
                gb[0:1, cols] += jnp.sum(dn1 * xhc, axis=0, keepdims=True)
                gb[1:2, cols] += jnp.sum(dn2 * xhc, axis=0, keepdims=True)
                gb[2:3, cols] += jnp.sum(dn1, axis=0, keepdims=True)
                gb[3:4, cols] += jnp.sum(dn2, axis=0, keepdims=True)
                g = summed(n0, n0 + TILE) + dn1 * gain[0:1, cols] + dn2 * gain[1:2, cols]
                mean_g = mean_g + jnp.sum(g, axis=1, keepdims=True)
                mean_gx = mean_gx + jnp.sum(g * xhc, axis=1, keepdims=True)
                pieces.append(g)
            mean_g = mean_g * (1.0 / D)
            mean_gx = mean_gx * (1.0 / D)
            for n, n0 in enumerate(range(0, D, TILE)):
                cols = slice(n0, n0 + TILE)
                v = yw[:, cols] + (pieces[n] - mean_g - xw[:, cols] * mean_gx) * rstd
                yw[:, cols] = v
                sxs[:, cols] = v.astype(BF)

            @pl.when(s == 1)
            def _():
                section_copy(m, 1).start()

            out = local_copy(yw, ig.at[m], 3)
            out.start()
            out.wait()
            for i in range(T):
                @pl.when(t != i)
                def _(i=i):
                    block_copy(M + m, i).wait_send()

            @pl.when(s == 1)
            def _():
                section_copy(m, 1).wait_send()
            return carry

        lax.fori_loop(0, M, backward, 0)

        outs = [local_copy(ga, ga_out, 1), local_copy(gr, gr_out, 2), local_copy(gb, gb_out, 3)]
        for copy in outs:
            copy.start()
        for copy in outs:
            copy.wait()
        for index in range(4):
            for k in range(1, DP):
                weight_copy(index, k).wait_send()

    any_spec = pl.BlockSpec(memory_space=pl.ANY)
    vmem_spec = pl.BlockSpec(memory_space=pltpu.VMEM)
    smem_spec = pl.BlockSpec(memory_space=pltpu.SMEM)
    GA = 3 * QC + QC + 2 * FFL
    shapes = jax.ShapeDtypeStruct
    return pl.pallas_call(
        kernel,
        out_shape=(
            shapes((M, R, D), F32), shapes((M, R, D), F32),
            shapes((RANK, GA), F32), shapes((RANK, 4 * D), F32), shapes((8, D), F32),
            shapes((M, L, FFL), BF), shapes((M, L, FFL), BF),
        ),
        in_specs=[any_spec] * 6 + [vmem_spec] * 12 + [smem_spec],
        out_specs=(any_spec,) * 7,
        scratch_shapes=[
            pltpu.VMEM((D, 3 * QC), BF), pltpu.VMEM((D, FFL), BF),
            pltpu.VMEM((DP, QC, DR), BF), pltpu.VMEM((DP, FFL, DR), BF),
            pltpu.VMEM((M * T, R, D), BF),
            pltpu.VMEM((M, 2 * RANK, L), BF),
            pltpu.VMEM((M * HEADS, L, 128), BF),
            pltpu.VMEM((M * PAIRS, L, 128), BF),
            pltpu.VMEM((M * PAIRS, L, 128), BF),
            pltpu.VMEM((M, QC, L), BF),
            pltpu.VMEM((QC, L), BF),
            pltpu.VMEM((M, QC, L), BF),
            pltpu.VMEM((M * HEADS, L), F32),
            pltpu.VMEM((L, FFL), BF),
            pltpu.VMEM((L, FFL), BF),
            pltpu.VMEM((M, 2 * RANK, R), BF),
            pltpu.VMEM((T, R, W), BF),
            pltpu.VMEM((2 * M * (T - 1), R, W), BF),
            pltpu.VMEM((M, R, D), BF),
            pltpu.VMEM((M, R, D), BF),
            pltpu.VMEM((R, D), BF),
            pltpu.VMEM((M * T, R, D), BF),
            pltpu.VMEM((HEADS, L, 128), BF),
            pltpu.VMEM((8, L), F32),
            pltpu.VMEM((2 * RANK, L), BF),
            pltpu.VMEM((PAIRS, L, 128), F32),
            pltpu.VMEM((PAIRS, L, 128), F32),
            pltpu.VMEM((QC, L), F32),
            pltpu.VMEM((L, 3 * QC), BF),
            pltpu.VMEM((RANK, GA), F32),
            pltpu.VMEM((RANK, 4 * D), F32),
            pltpu.VMEM((8, D), F32),
            pltpu.VMEM((R, D), F32),
            pltpu.VMEM((R, D), F32),
            pltpu.SemaphoreType.DMA((4,)),
            pltpu.SemaphoreType.DMA((4, DP - 1)),
            pltpu.SemaphoreType.DMA((4, DP - 1)),
            pltpu.SemaphoreType.DMA((T - 1,)),
            pltpu.SemaphoreType.DMA((M * (T - 1),)),
            pltpu.SemaphoreType.DMA((T,)),
            pltpu.SemaphoreType.DMA((2 * M * (T - 1),)),
            pltpu.SemaphoreType.DMA((T - 1,)),
            pltpu.SemaphoreType.DMA((M * (T - 1),)),
            pltpu.SemaphoreType.DMA((1,)),
            pltpu.SemaphoreType.DMA((2 * M,)),
            pltpu.SemaphoreType.DMA((4,)),
        ],
        compiler_params=pltpu.CompilerParams(
            collective_id=0, has_side_effects=True, vmem_limit_bytes=63 * 2**20
        ),
    )


def rope_tables(split_flags, length):
    half = ROT // 2
    place = jnp.arange(length, dtype=jnp.int32)
    flags = split_flags.astype(jnp.int32)[:, None]
    places = (place[None] - length // 2 * jnp.where(place[None] >= length // 2, flags, 0)).astype(F32)
    inverse = 10000.0 ** (-jnp.arange(half, dtype=F32) * 2.0 / ROT)
    angles = places[:, :, None] * inverse
    cosine, sine = jnp.cos(angles), jnp.sin(angles)
    pad = HEAD - ROT
    rest = angles.shape[:2] + (pad,)
    cos_head = jnp.concatenate([cosine, cosine, jnp.ones(rest, F32)], axis=-1)
    sin_head = jnp.concatenate([-sine, sine, jnp.zeros(rest, F32)], axis=-1)
    return jnp.tile(cos_head, (1, 1, 2)), jnp.tile(sin_head, (1, 1, 2))


def solution(mesh):
    T = mesh.shape["tensor"]
    DP = mesh.shape["dp"]

    def per_device(
        inputs, cotangent, split,
        query_key_value_weight, output_weight, up_weight, down_weight,
        qkv_adapter_input, qkv_adapter_output, out_adapter_input, out_adapter_output,
        up_adapter_input, up_adapter_output, down_adapter_input, down_adapter_output,
        ln_gain, ln_bias,
    ):
        M, R, D = inputs.shape
        QC = output_weight.shape[1]
        FFL = up_weight.shape[2]
        RANK = qkv_adapter_input.shape[2]
        L = R * T
        wq = query_key_value_weight[0].reshape(-1, 3 * QC)
        aq = qkv_adapter_input[0].astype(BF)
        bq = (ADAPTER_SCALE * qkv_adapter_output[0].reshape(RANK, -1)).astype(BF)
        ao = out_adapter_input[0].astype(BF)
        bo = (ADAPTER_SCALE * out_adapter_output[0]).astype(BF)
        au = up_adapter_input[0].astype(BF)
        bu = (ADAPTER_SCALE * up_adapter_output[0]).astype(BF)
        ad = down_adapter_input[0].astype(BF)
        bd = (ADAPTER_SCALE * down_adapter_output[0]).astype(BF)
        flags = split[:, 0]
        cos_t, sin_t = rope_tables(flags, L)
        negb = MASKED * flags.astype(F32)
        kernel = make_kernel(T, DP, M, R, D, QC, FFL, RANK)
        act, ig, ga, gr, gb, _, _ = kernel(
            inputs, cotangent, wq, up_weight[0], output_weight[0], down_weight[0],
            aq, bq, ao, bo, au, bu, ad, bd, ln_gain[0], ln_bias[0], cos_t, sin_t, negb,
        )
        ga = lax.psum(ga.astype(BF), "dp").astype(F32)
        gr = lax.psum(gr.astype(BF), ("dp", "tensor")).astype(F32)
        gb = lax.psum(gb, ("dp", "tensor"))
        cuts = [3 * QC, 3 * QC + FFL, 4 * QC + FFL]
        b_qkv, b_up, a_out, a_down = jnp.split(ga, cuts, axis=1)
        a_qkv, a_up, b_out, b_down = jnp.split(gr, 4, axis=1)

        dp_place = lax.axis_index("dp")
        DR = D // DP
        sl = lax.dynamic_slice_in_dim
        c_qkv = wq.astype(F32) + nn(sl(aq, dp_place * DR, DR, 0), bq)
        c_out = output_weight[0].astype(F32) + nn(ao, sl(bo, dp_place * DR, DR, 1))
        c_up = up_weight[0].astype(F32) + nn(sl(au, dp_place * DR, DR, 0), bu)
        c_down = down_weight[0].astype(F32) + nn(ad, sl(bd, dp_place * DR, DR, 1))
        return (
            act[None], ig[None],
            a_qkv.T[None], b_qkv.reshape(qkv_adapter_output.shape),
            a_out.T[None], b_out[None], a_up.T[None], b_up[None], a_down.T[None], b_down[None],
            gb[0:2][None], gb[2:4][None],
            c_qkv.reshape(query_key_value_weight.shape), c_out[None], c_up[None], c_down[None],
        )

    rows = P(None, ("dp", "tensor"), None)
    whole = P("section", None, None)
    in_specs = (
        rows, rows, P(None, "dp"),
        P("section", "dp", None, "tensor"), P("section", "tensor", "dp"),
        P("section", "dp", "tensor"), P("section", "tensor", "dp"),
        whole, P("section", None, None, "tensor"), P("section", "tensor", None), whole,
        whole, P("section", None, "tensor"), P("section", "tensor", None), whole,
        whole, whole,
    )
    layer_rows = P("section", None, ("dp", "tensor"), None)
    out_specs = (
        layer_rows, layer_rows,
        whole, P("section", None, None, "tensor"), P("section", "tensor", None), whole,
        whole, P("section", None, "tensor"), P("section", "tensor", None), whole,
        whole, whole,
        P("section", "dp", None, "tensor"), P("section", "tensor", "dp"),
        P("section", "dp", "tensor"), P("section", "tensor", "dp"),
    )
    return jax.shard_map(
        per_device, mesh=mesh, in_specs=in_specs, out_specs=out_specs, check_vma=False
    )
```

```python
import functools

import jax
import jax.numpy as jnp
from jax import lax
from jax.experimental import pallas as pl
from jax.experimental.pallas import tpu as pltpu
from jax.sharding import PartitionSpec as P

HEAD = 64
ROT = 16
ADAPTER_SCALE = 0.25
EPSILON = 1e-05
MASKED = -1e30
BF = jnp.bfloat16
F32 = jnp.float32
MESH = pl.DeviceIdType.MESH


def nn(a, b):
    return lax.dot_general(a, b, (((1,), (0,)), ((), ())), preferred_element_type=F32)


def nt(a, b):
    return lax.dot_general(a, b, (((1,), (1,)), ((), ())), preferred_element_type=F32)


def make_kernel(T, DP, M, R, D, QC, FFL, RANK):
    L = R * T
    DR = D // DP
    W = D + 2 * RANK
    PAIRS = QC // 128
    HEADS = QC // HEAD
    TILE = 256
    HALF = L // 2
    GA = 4 * QC + 2 * FFL
    GRW = 4 * D // T
    PW = -(-GA // (DP * 128)) * 128
    SW = -(-GRW // (DP * 128)) * 128

    def kernel(
        x_in, ct_in, wq_in, wup_in, wout_in, wdn_in,
        aq, bq, ao, bo, au, bu, ad, bd, gain, bias, rope, negb,
        act, ig, ga_out, gr_out, gb_out, h_hbm, dg_hbm,
        wq, wup, wout, wdn, xh, t12t, qh, kp, vp, kT, vT, oT, lse, hw, dg,
        todt, sbuf, rbuf, sxr, sgr, sxs, dz, doh, delta, edot, dk, dv, dqt, dqkv,
        ga, gr, gb, xw, yw, pa, pa_in, pa_all, pb, pb_in, pb_all, gb_sum, gb_t, gb_d,
        w_ls, w_ss, w_rs, x_ss, x_rs, r_ss, r_rs, z_ss, z_rs, c_ss, c_rs, l_s,
        go, at_ss, at_rs, ad_ss, ad_rs,
    ):
        s = lax.axis_index("section")
        d = lax.axis_index("dp")
        t = lax.axis_index("tensor")
        other = 1 - s

        barrier = pltpu.get_barrier_semaphore()
        for k in range(1, T):
            pl.semaphore_signal(
                barrier, inc=1, device_id={"tensor": lax.rem(t + k, T)}, device_id_type=MESH
            )
        for k in range(1, DP):
            pl.semaphore_signal(
                barrier, inc=1, device_id={"dp": lax.rem(d + k, DP)}, device_id_type=MESH
            )
        pl.semaphore_signal(barrier, inc=1, device_id={"section": other}, device_id_type=MESH)
        pl.semaphore_wait(barrier, T + DP - 1)

        def gathered(index, owner):
            if index < 2:
                return (wq, wup)[index].at[pl.ds(pl.multiple_of(owner * DR, DR), DR)]
            return (wout, wdn)[index - 2].at[owner]

        def weight_copy(index, way, hop, owner, own):
            place = gathered(index, owner)
            return pltpu.make_async_remote_copy(
                src_ref=(wq_in, wup_in, wout_in, wdn_in)[index] if own else place, dst_ref=place,
                send_sem=w_ss.at[index, way, hop], recv_sem=w_rs.at[index, way, hop],
                device_id={"dp": d + 1 if way == 0 else d - 1}, device_id_type=MESH,
            )

        has_next = (d < DP - 1, d > 0)

        def holds(way, hop):
            return d >= hop + 1 if way == 0 else d + hop + 1 <= DP - 1

        def owner_of(way, hop):
            return d - hop - 1 if way == 0 else d + hop + 1

        def weight_local(index):
            return pltpu.make_async_copy(
                (wq_in, wup_in, wout_in, wdn_in)[index], gathered(index, d), w_ls.at[index]
            )

        def weights_start():
            for index in range(4):
                for way in range(2):
                    @pl.when(has_next[way])
                    def _(index=index, way=way):
                        weight_copy(index, way, 0, d, True).start()

        def weights_pass(indices):
            def step(hop, carry):
                for index in indices:
                    for way in range(2):
                        @pl.when(holds(way, hop))
                        def _(index=index, way=way):
                            weight_copy(index, way, hop, owner_of(way, hop), False).wait_recv()

                            @pl.when(has_next[way])
                            def _():
                                weight_copy(index, way, hop + 1, owner_of(way, hop), False).start()
                return carry

            lax.fori_loop(0, DP - 1, step, 0)

        def weights_sent():
            for index in range(4):
                for way in range(2):
                    @pl.when(has_next[way])
                    def _(index=index, way=way):
                        weight_copy(index, way, 0, d, True).wait_send()

            def step(hop, carry):
                for index in range(4):
                    for way in range(2):
                        @pl.when(jnp.logical_and(has_next[way], holds(way, hop)))
                        def _(index=index, way=way):
                            weight_copy(index, way, hop + 1, owner_of(way, hop), False).wait_send()
                return carry

            lax.fori_loop(0, DP - 1, step, 0)

        for index in range(4):
            weight_local(index).start()

        ga[...] = jnp.zeros_like(ga)
        gr[...] = jnp.zeros_like(gr)
        gb[...] = jnp.zeros_like(gb)

        def rows_copy(buf, m, k, ssem, rsem):
            place = m * T + t
            return pltpu.make_async_remote_copy(
                src_ref=buf.at[place], dst_ref=buf.at[place],
                send_sem=ssem.at[m * (T - 1) + k - 1], recv_sem=rsem.at[m * (T - 1) + k - 1],
                device_id={"tensor": lax.rem(t + k, T)}, device_id_type=MESH,
            )

        def rows_wait(buf, m, c, ssem, rsem):
            place = m * T + lax.rem(t - c + T, T)
            pltpu.make_async_remote_copy(
                src_ref=buf.at[place], dst_ref=buf.at[place],
                send_sem=ssem.at[0], recv_sem=rsem.at[m * (T - 1) + c - 1],
                device_id={"tensor": lax.rem(t + 1, T)}, device_id_type=MESH,
            ).wait_recv()

        def to_peer(axis, size, me, k, src, dst, ssem, rsem):
            return pltpu.make_async_remote_copy(
                src_ref=src, dst_ref=dst, send_sem=ssem, recv_sem=rsem,
                device_id={axis: lax.rem(me + k, size)}, device_id_type=MESH,
            )

        def block_copy(phase, i):
            k = lax.rem(i - t + T, T)
            slot = phase * (T - 1) + k - 1
            return pltpu.make_async_remote_copy(
                src_ref=sbuf.at[i], dst_ref=rbuf.at[slot],
                send_sem=r_ss.at[i], recv_sem=r_rs.at[slot],
                device_id={"tensor": i}, device_id_type=MESH,
            )

        def block_wait(phase, k):
            slot = phase * (T - 1) + k - 1
            pltpu.make_async_remote_copy(
                src_ref=sbuf.at[0], dst_ref=rbuf.at[slot],
                send_sem=r_ss.at[0], recv_sem=r_rs.at[slot],
                device_id={"tensor": lax.rem(t + k, T)}, device_id_type=MESH,
            ).wait_recv()

        def section_copy(m, phase):
            dst = (sxr, sgr)[phase]
            return pltpu.make_async_remote_copy(
                src_ref=sxs, dst_ref=dst.at[m],
                send_sem=c_ss.at[0], recv_sem=c_rs.at[phase * M + m],
                device_id={"section": other}, device_id_type=MESH,
            )

        def local_copy(src, dst, index):
            return pltpu.make_async_copy(src, dst, l_s.at[index])

        def norm_parts(x):
            mean = jnp.mean(x, axis=-1, keepdims=True)
            centred = x - mean
            spread = jnp.mean(centred * centred, axis=-1, keepdims=True)
            rstd = lax.rsqrt(spread + EPSILON)
            return centred * rstd, rstd

        def send_normed(m):
            xhat, _ = norm_parts(xw[m])
            xh[m * T + t] = xhat.astype(BF)
            for k in range(1, T):
                rows_copy(xh, m, k, x_ss, x_rs).start()

        def send_gradient(m):
            for k in range(1, T):
                rows_copy(dz, m, k, z_ss, z_rs).start()

        def take_x(m):
            section_copy(m, 0).wait_recv()
            xw[m] = sxr[m].astype(F32)
            send_normed(m)

        lane = lax.broadcasted_iota(jnp.int32, (R, 128), 1)
        in_first = lax.rem(lane, HEAD) < ROT // 2
        head_low = lane < HEAD

        def turn(v, cosine, sine):
            swapped = jnp.where(in_first, pltpu.roll(v, 128 - ROT // 2, 1), pltpu.roll(v, ROT // 2, 1))
            return v * cosine + swapped * sine

        def rope_of(m, rows):
            table = rope[m, rows, :]
            crossed = pltpu.roll(table, HEAD, 1)
            return jnp.where(head_low, table, crossed), jnp.where(head_low, crossed, table)

        causal = lax.broadcasted_iota(jnp.int32, (R, R), 0) <= lax.broadcasted_iota(
            jnp.int32, (R, R), 1
        )

        def scores_t(m, p, i, j, q):
            keys = kp[m * PAIRS + p, j * R:(j + 1) * R, :]
            sc = nt(keys, q)
            if j == i:
                sc = jnp.where(causal, sc, MASKED)
            if i * R >= HALF and j * R < HALF:
                sc = sc + negb[m]
            return sc

        @pl.when(s == 0)
        def _():
            weights_start()
            loads = [local_copy(x_in.at[m], xw.at[m], m) for m in range(M)]
            for copy in loads:
                copy.start()
            for m in range(M):
                loads[m].wait()
                send_normed(m)
            weights_pass((0, 1, 2, 3))
            weights_sent()
            pl.semaphore_signal(go, inc=1, device_id={"section": other}, device_id_type=MESH)

        @pl.when(s == 1)
        def _():
            loads = [local_copy(ct_in.at[m], xw.at[m], m) for m in range(M)]
            for copy in loads:
                copy.start()
            for m in range(M):
                loads[m].wait()
                dz[m * T + t] = xw[m].astype(BF)
                send_gradient(m)
            pl.semaphore_wait(go, 1)
            weights_start()
            weights_pass((0, 1))
            take_x(0)
            weights_pass((2, 3))
            weights_sent()

        for index in range(4):
            weight_local(index).wait()

        def normed_to_hidden(m):
            @pl.when(m > 0)
            def _():
                local_copy(hw, h_hbm.at[m - 1], 1).wait()
                local_copy(dg, dg_hbm.at[m - 1], 2).wait()

            def chunk(c, carry):
                src = lax.rem(t - c + T, T)

                @pl.when(c > 0)
                def _():
                    rows_wait(xh, m, c, x_ss, x_rs)

                rows = pl.ds(pl.multiple_of(src * R, R), R)
                xhc = xh[m * T + src].astype(F32)
                n1 = (xhc * gain[0:1] + bias[0:1]).astype(BF)
                n2 = (xhc * gain[1:2] + bias[1:2]).astype(BF)
                t1 = nn(n1, aq[...]).astype(BF)
                t2 = nn(n2, au[...]).astype(BF)
                t12t[m, 0:RANK, rows] = t1.T
                t12t[m, RANK:2 * RANK, rows] = t2.T
                cosine, sine = rope_of(m, rows)
                for part in range(3):
                    cols = slice(part * QC, (part + 1) * QC)
                    val = nn(n1, wq[:, cols]) + nn(t1, bq[:, cols])
                    if part == 2:
                        vb = val.astype(BF)
                        for p in range(PAIRS):
                            vp[m * PAIRS + p, rows, :] = vb[:, p * 128:(p + 1) * 128]
                        vT[:, rows] = vb.T
                    else:
                        for p in range(PAIRS):
                            v = turn(val[:, p * 128:(p + 1) * 128], cosine, sine)
                            if part == 0:
                                v = v * 0.125
                                qh[m * HEADS + 2 * p, rows, :] = jnp.where(head_low, v, 0.0).astype(BF)
                                qh[m * HEADS + 2 * p + 1, rows, :] = jnp.where(head_low, 0.0, v).astype(BF)
                            else:
                                vb = v.astype(BF)
                                kp[m * PAIRS + p, rows, :] = vb
                                kT[m, p * 128:(p + 1) * 128, rows] = vb.T
                for n0 in range(0, FFL, TILE):
                    cols = slice(n0, n0 + TILE)
                    u = nn(n2, wup[:, cols]) + nn(t2, bu[:, cols])
                    phi = 0.5 * (1.0 + lax.erf(u * 0.7071067811865476))
                    hw[rows, cols] = (u * phi).astype(BF)
                    dg[rows, cols] = (
                        phi + u * (0.3989422804014327 * jnp.exp(-0.5 * u * u))
                    ).astype(BF)
                return carry

            lax.fori_loop(0, T, chunk, 0)
            local_copy(hw, h_hbm.at[m], 1).start()
            local_copy(dg, dg_hbm.at[m], 2).start()

        def attend_and_project(m):
            for i in range(T):
                icols = slice(i * R, (i + 1) * R)

                def pair(p, carry, i=i, icols=icols):
                    for hh in range(2):
                        h = 2 * p + hh
                        q = qh[m * HEADS + h, icols, :]
                        hrows = pl.ds(pl.multiple_of(h * HEAD, HEAD), HEAD)
                        blocks = [scores_t(m, p, i, j, q) for j in range(i + 1)]
                        top = functools.reduce(
                            jnp.maximum, [jnp.max(b, axis=0, keepdims=True) for b in blocks]
                        )
                        total = jnp.zeros_like(top)
                        acc = jnp.zeros((HEAD, R), F32)
                        for j in range(i + 1):
                            e = jnp.exp(blocks[j] - top)
                            total = total + jnp.sum(e, axis=0, keepdims=True)
                            acc = acc + nn(vT[hrows, j * R:(j + 1) * R], e.astype(BF))
                        oT[m, hrows, icols] = (acc * (1.0 / total)).astype(BF)
                        lse[pl.ds(m * HEADS + h, 1), icols] = top + jnp.log(total)
                    return carry

                lax.fori_loop(0, PAIRS, pair, 0)
                o = oT[m, :, icols].T
                hrow = hw[icols, :]
                for j in range(DP):
                    sbuf[i, :, j * DR:(j + 1) * DR] = (nn(o, wout[j]) + nn(hrow, wdn[j])).astype(BF)
                sbuf[i, :, D:D + RANK] = nn(o, ao[...]).astype(BF)
                sbuf[i, :, D + RANK:W] = nn(hrow, ad[...]).astype(BF)

                @pl.when(t != i)
                def _(i=i):
                    block_copy(m, i).start()

        def finish_forward(m):
            @pl.when(m > 0)
            def _():
                local_copy(yw, act.at[m - 1], 3).wait()

            for k in range(1, T):
                block_wait(m, k)

            def summed(lo, hi):
                v = sbuf[t, :, lo:hi].astype(F32)
                for k in range(T - 1):
                    v = v + rbuf[m * (T - 1) + k, :, lo:hi].astype(F32)
                return v

            to = summed(D, D + RANK).astype(BF)
            td = summed(D + RANK, W).astype(BF)
            todt[m, 0:RANK, :] = to.T
            todt[m, RANK:2 * RANK, :] = td.T
            for n0 in range(0, D, TILE):
                cols = slice(n0, n0 + TILE)
                y = xw[m, :, cols] + summed(n0, n0 + TILE) + nn(to, bo[:, cols]) + nn(td, bd[:, cols])
                yw[:, cols] = y
                sxs[:, cols] = y.astype(BF)

            @pl.when(s == 0)
            def _():
                section_copy(m, 0).start()

            local_copy(yw, act.at[m], 3).start()
            for k in range(1, T):
                rows_copy(xh, m, k, x_ss, x_rs).wait_send()
            for i in range(T):
                @pl.when(t != i)
                def _(i=i):
                    block_copy(m, i).wait_send()

            @pl.when(s == 0)
            def _():
                section_copy(m, 0).wait_send()

        def forward(step, carry):
            @pl.when(step < M)
            def _():
                normed_to_hidden(step)

            @pl.when(step > 0)
            def _():
                finish_forward(step - 1)

            @pl.when(jnp.logical_and(s == 1, step < M - 1))
            def _():
                take_x(step + 1)

            @pl.when(step < M)
            def _():
                attend_and_project(step)
            return carry

        lax.fori_loop(0, M + 1, forward, 0)
        local_copy(hw, h_hbm.at[M - 1], 1).wait()
        local_copy(dg, dg_hbm.at[M - 1], 2).wait()
        local_copy(yw, act.at[M - 1], 3).wait()

        def gradient_to_hidden(m):
            local_copy(dg_hbm.at[m], dg, 2).start()
            local_copy(h_hbm.at[m], hw, 1).start()

            @pl.when(s == 0)
            def _():
                section_copy(m, 1).wait_recv()
                dz[m * T + t] = sgr[m]
                send_gradient(m)

            local_copy(dg_hbm.at[m], dg, 2).wait()

            def chunk(c, carry):
                src = lax.rem(t - c + T, T)

                @pl.when(c > 0)
                def _():
                    rows_wait(dz, m, c, z_ss, z_rs)

                rows = pl.ds(pl.multiple_of(src * R, R), R)
                place = m * T + src
                full = dz[place]
                eo = nt(full, bo[...]).astype(BF)
                ed = nt(full, bd[...]).astype(BF)
                edot[0:RANK, rows] = eo.T
                edot[RANK:2 * RANK, rows] = ed.T
                do = nt(eo, ao[...])
                for j in range(DP):
                    do = do + nt(full[:, j * DR:(j + 1) * DR], wout[j])
                dob = do.astype(BF)
                for p in range(PAIRS):
                    v = dob[:, p * 128:(p + 1) * 128]
                    zero = jnp.zeros_like(v)
                    doh[2 * p, rows, :] = jnp.where(head_low, v, zero)
                    doh[2 * p + 1, rows, :] = jnp.where(head_low, zero, v)
                prod = dob.T.astype(F32) * oT[m, :, rows].astype(F32)
                for h in range(HEADS):
                    delta[h:h + 1, rows] = jnp.sum(
                        prod[h * HEAD:(h + 1) * HEAD], axis=0, keepdims=True
                    )
                for n0 in range(0, FFL, TILE):
                    cols = slice(n0, n0 + TILE)
                    v = nt(ed, ad[cols, :])
                    for j in range(DP):
                        v = v + nt(full[:, j * DR:(j + 1) * DR], wdn[j, cols, :])
                    dg[rows, cols] = (v * dg[rows, cols].astype(F32)).astype(BF)
                return carry

            lax.fori_loop(0, T, chunk, 0)

        def attention_back(m):
            dk[...] = jnp.zeros_like(dk)
            dv[...] = jnp.zeros_like(dv)
            for i in range(T):
                icols = slice(i * R, (i + 1) * R)

                def pair(p, carry, i=i, icols=icols):
                    for hh in range(2):
                        h = 2 * p + hh
                        q = qh[m * HEADS + h, icols, :]
                        do = doh[h, icols, :]
                        hrows = pl.ds(pl.multiple_of(h * HEAD, HEAD), HEAD)
                        low = lse[pl.ds(m * HEADS + h, 1), icols]
                        dlt = delta[pl.ds(h, 1), icols]
                        acc = jnp.zeros((HEAD, R), F32)
                        for j in range(i + 1):
                            jrows = slice(j * R, (j + 1) * R)
                            prob = jnp.exp(scores_t(m, p, i, j, q) - low)
                            dp_t = nt(vp[m * PAIRS + p, jrows, :], do)
                            ds_t = (prob * (dp_t - dlt)).astype(BF)
                            dv[p, jrows, :] += nn(prob.astype(BF), do)
                            dk[p, jrows, :] += nn(ds_t, q)
                            acc = acc + nn(kT[m, hrows, jrows], ds_t)
                        dqt[hrows, icols] = acc
                    return carry

                lax.fori_loop(0, PAIRS, pair, 0)

            def tail(c, carry):
                i = lax.rem(t + c + 1, T)
                rows = pl.ds(pl.multiple_of(i * R, R), R)
                cosine, sine = rope_of(m, rows)
                sine = -sine
                dq = dqt[:, rows].T * 0.125
                for p in range(PAIRS):
                    lanes = slice(p * 128, (p + 1) * 128)
                    dqkv[rows, p * 128:(p + 1) * 128] = turn(dq[:, lanes], cosine, sine).astype(BF)
                    dqkv[rows, QC + p * 128:QC + (p + 1) * 128] = turn(
                        dk[p, rows, :], cosine, sine
                    ).astype(BF)
                    dqkv[rows, 2 * QC + p * 128:2 * QC + (p + 1) * 128] = dv[p, rows, :].astype(BF)
                dj = dqkv[rows, :]
                du = dg[rows, :]
                for n0 in range(0, D, TILE):
                    cols = slice(n0, n0 + TILE)
                    dn1 = nt(dj, wq[cols, :])
                    dn2 = nt(du, wup[cols, :])
                    xhc = xh[m * T + i, :, cols].astype(F32)
                    gb[0:1, cols] += jnp.sum(dn1 * xhc, axis=0, keepdims=True)
                    gb[1:2, cols] += jnp.sum(dn2 * xhc, axis=0, keepdims=True)
                    gb[2:3, cols] += jnp.sum(dn1, axis=0, keepdims=True)
                    gb[3:4, cols] += jnp.sum(dn2, axis=0, keepdims=True)
                    sbuf[i, :, cols] = (dn1 * gain[0:1, cols] + dn2 * gain[1:2, cols]).astype(BF)
                sbuf[i, :, D:D + RANK] = nt(dj, bq[...]).astype(BF)
                sbuf[i, :, D + RANK:W] = nt(du, bu[...]).astype(BF)

                @pl.when(t != i)
                def _():
                    block_copy(M + m, i).start()
                return carry

            lax.fori_loop(0, T, tail, 0)

            @pl.when(m > 0)
            def _():
                local_copy(yw, ig.at[m - 1], 3).wait()

            @pl.when(s == 1)
            def _():
                local_copy(ct_in.at[m], yw, 0).start()

            local_copy(h_hbm.at[m], hw, 1).wait()
            base = 0
            ga[:, base:base + 3 * QC] += ADAPTER_SCALE * nn(t12t[m, 0:RANK, :], dqkv[...])
            base += 3 * QC
            ga[:, base:base + FFL] += ADAPTER_SCALE * nn(t12t[m, RANK:2 * RANK, :], dg[...])
            base += FFL
            ga[:, base:base + QC] += nt(edot[0:RANK, :], oT[m])
            base += QC
            ga[:, base:base + FFL] += nn(edot[RANK:2 * RANK, :], hw[...])
            own = dz[m * T + t]
            gr[:, 2 * D:3 * D] += ADAPTER_SCALE * nn(todt[m, 0:RANK, :], own)
            gr[:, 3 * D:4 * D] += ADAPTER_SCALE * nn(todt[m, RANK:2 * RANK, :], own)

        def finish_backward(m):
            @pl.when(s == 1)
            def _():
                local_copy(ct_in.at[m], yw, 0).wait()

            @pl.when(s == 0)
            def _():
                yw[...] = sgr[m].astype(F32)

            for k in range(1, T):
                block_wait(M + m, k)

            def summed(lo, hi):
                v = sbuf[t, :, lo:hi].astype(F32)
                for k in range(T - 1):
                    v = v + rbuf[(M + m) * (T - 1) + k, :, lo:hi].astype(F32)
                return v

            e1 = summed(D, D + RANK).astype(BF)
            e2 = summed(D + RANK, W).astype(BF)
            xhat, rstd = norm_parts(xw[m])
            xw[m] = xhat
            n1 = (xhat * gain[0:1] + bias[0:1]).astype(BF)
            n2 = (xhat * gain[1:2] + bias[1:2]).astype(BF)
            gr[:, 0:D] += nn(e1.T, n1)
            gr[:, D:2 * D] += nn(e2.T, n2)
            pieces = []
            mean_g = jnp.zeros((R, 1), F32)
            mean_gx = jnp.zeros((R, 1), F32)
            for n0 in range(0, D, TILE):
                cols = slice(n0, n0 + TILE)
                dn1 = nt(e1, aq[cols, :])
                dn2 = nt(e2, au[cols, :])
                xhc = xw[m, :, cols]
                gb[0:1, cols] += jnp.sum(dn1 * xhc, axis=0, keepdims=True)
                gb[1:2, cols] += jnp.sum(dn2 * xhc, axis=0, keepdims=True)
                gb[2:3, cols] += jnp.sum(dn1, axis=0, keepdims=True)
                gb[3:4, cols] += jnp.sum(dn2, axis=0, keepdims=True)
                g = summed(n0, n0 + TILE) + dn1 * gain[0:1, cols] + dn2 * gain[1:2, cols]
                mean_g = mean_g + jnp.sum(g, axis=1, keepdims=True)
                mean_gx = mean_gx + jnp.sum(g * xhc, axis=1, keepdims=True)
                pieces.append(g)
            mean_g = mean_g * (1.0 / D)
            mean_gx = mean_gx * (1.0 / D)
            for n, n0 in enumerate(range(0, D, TILE)):
                cols = slice(n0, n0 + TILE)
                v = yw[:, cols] + (pieces[n] - mean_g - xw[m, :, cols] * mean_gx) * rstd
                yw[:, cols] = v
                sxs[:, cols] = v.astype(BF)

            @pl.when(s == 1)
            def _():
                section_copy(m, 1).start()

            local_copy(yw, ig.at[m], 3).start()
            for k in range(1, T):
                rows_copy(dz, m, k, z_ss, z_rs).wait_send()
            for i in range(T):
                @pl.when(t != i)
                def _(i=i):
                    block_copy(M + m, i).wait_send()

            @pl.when(s == 1)
            def _():
                section_copy(m, 1).wait_send()

        def backward(step, carry):
            @pl.when(step < M)
            def _():
                gradient_to_hidden(step)

            @pl.when(step > 0)
            def _():
                finish_backward(step - 1)

            @pl.when(step < M)
            def _():
                attention_back(step)
            return carry

        lax.fori_loop(0, M + 1, backward, 0)
        local_copy(yw, ig.at[M - 1], 3).wait()

        def scatter_dp(buf, landing, base):
            for k in range(1, DP):
                yield to_peer("dp", DP, d, k, buf.at[lax.rem(d + k, DP)], landing.at[k - 1],
                              ad_ss.at[base, k - 1], ad_rs.at[base, k - 1])

        def gather_dp(buf, base):
            for k in range(1, DP):
                yield to_peer("dp", DP, d, k, buf.at[d], buf.at[d],
                              ad_ss.at[base, k - 1], ad_rs.at[base, k - 1])

        def gather_dp_wait(buf, base):
            for k in range(1, DP):
                place = buf.at[lax.rem(d - k + DP, DP)]
                to_peer("dp", DP, d, k, place, place,
                        ad_ss.at[base, k - 1], ad_rs.at[base, k - 1]).wait_recv()

        def fill(buf, value, width):
            total = value.shape[1]
            for j in range(DP):
                lo, hi = min(j * width, total), min((j + 1) * width, total)
                if hi > lo:
                    buf[j, :, 0:hi - lo] = value[:, lo:hi].astype(BF)
                if hi - lo < width:
                    buf[j, :, hi - lo:width] = jnp.zeros((RANK, width - hi + lo), BF)

        def added(buf, landing):
            v = buf[d].astype(F32)
            for k in range(DP - 1):
                v = v + landing[k].astype(F32)
            return v.astype(BF)

        def tensor_scatter():
            for k in range(1, T):
                yield to_peer("tensor", T, t, k, sbuf.at[lax.rem(t + k, T), 0:RANK, 0:GRW],
                              rbuf.at[k - 1, 0:RANK, 0:GRW], at_ss.at[0, k - 1], at_rs.at[0, k - 1])

        def tensor_gather():
            for k in range(1, T):
                yield to_peer("tensor", T, t, k, sbuf.at[t, 0:RANK, 0:GRW],
                              rbuf.at[T - 1 + k - 1, 0:RANK, 0:GRW],
                              at_ss.at[1, k - 1], at_rs.at[1, k - 1])

        def gb_over_tensor():
            for k in range(1, T):
                yield to_peer("tensor", T, t, k, gb, gb_t.at[k - 1], at_ss.at[2, k - 1], at_rs.at[2, k - 1])

        def gb_over_dp():
            for k in range(1, DP):
                yield to_peer("dp", DP, d, k, gb_sum, gb_d.at[k - 1], ad_ss.at[4, k - 1], ad_rs.at[4, k - 1])

        def start_all(copies):
            for copy in copies:
                copy.start()

        def arrive_all(copies):
            for copy in copies:
                copy.wait_recv()

        def sent_all(copies):
            for copy in copies:
                copy.wait_send()

        for j in range(T):
            sbuf[j, 0:RANK, 0:GRW] = gr[:, j * GRW:(j + 1) * GRW].astype(BF)
        start_all(tensor_scatter())
        start_all(gb_over_tensor())
        fill(pa, ga, PW)
        start_all(scatter_dp(pa, pa_in, 0))

        arrive_all(tensor_scatter())
        part = sbuf[t, 0:RANK, 0:GRW].astype(F32)
        for k in range(T - 1):
            part = part + rbuf[k, 0:RANK, 0:GRW].astype(F32)
        fill(pb, part, SW)
        start_all(scatter_dp(pb, pb_in, 1))
        arrive_all(gb_over_tensor())
        total = gb[...]
        for k in range(T - 1):
            total = total + gb_t[k]
        gb_sum[...] = total
        start_all(gb_over_dp())

        arrive_all(scatter_dp(pb, pb_in, 1))
        pb_all[d] = added(pb, pb_in)
        start_all(gather_dp(pb_all, 3))
        arrive_all(scatter_dp(pa, pa_in, 0))
        pa_all[d] = added(pa, pa_in)
        start_all(gather_dp(pa_all, 2))

        gather_dp_wait(pb_all, 3)
        for j in range(DP):
            lo, hi = min(j * SW, GRW), min((j + 1) * SW, GRW)
            if hi > lo:
                sbuf[t, 0:RANK, lo:hi] = pb_all[j, :, 0:hi - lo]
        start_all(tensor_gather())

        arrive_all(gb_over_dp())
        sent_all(gb_over_tensor())
        total = gb_sum[...]
        for k in range(DP - 1):
            total = total + gb_d[k]
        gb[...] = total
        outs = [local_copy(gb, gb_out, 3)]
        outs[0].start()

        gather_dp_wait(pa_all, 2)
        for j in range(DP):
            lo, hi = min(j * PW, GA), min((j + 1) * PW, GA)
            if hi > lo:
                ga[:, lo:hi] = pa_all[j, :, 0:hi - lo].astype(F32)
        outs.append(local_copy(ga, ga_out, 1))
        outs[1].start()

        arrive_all(tensor_gather())
        gr[:, pl.ds(pl.multiple_of(t * GRW, 128), GRW)] = sbuf[t, 0:RANK, 0:GRW].astype(F32)
        for k in range(1, T):
            place = pl.ds(pl.multiple_of(lax.rem(t - k + T, T) * GRW, 128), GRW)
            gr[:, place] = rbuf[T - 1 + k - 1, 0:RANK, 0:GRW].astype(F32)
        outs.append(local_copy(gr, gr_out, 2))
        outs[2].start()
        for copies in (tensor_scatter(), tensor_gather(), scatter_dp(pa, pa_in, 0),
                       scatter_dp(pb, pb_in, 1), gather_dp(pa_all, 2), gather_dp(pb_all, 3),
                       gb_over_dp()):
            sent_all(copies)
        for copy in outs:
            copy.wait()

    any_spec = pl.BlockSpec(memory_space=pl.ANY)
    vmem_spec = pl.BlockSpec(memory_space=pltpu.VMEM)
    smem_spec = pl.BlockSpec(memory_space=pltpu.SMEM)
    shapes = jax.ShapeDtypeStruct
    return pl.pallas_call(
        kernel,
        out_shape=(
            shapes((M, R, D), F32), shapes((M, R, D), F32),
            shapes((RANK, GA), F32), shapes((RANK, 4 * D), F32), shapes((8, D), F32),
            shapes((M, L, FFL), BF), shapes((M, L, FFL), BF),
        ),
        in_specs=[any_spec] * 6 + [vmem_spec] * 11 + [smem_spec],
        out_specs=(any_spec,) * 7,
        scratch_shapes=[
            pltpu.VMEM((D, 3 * QC), BF), pltpu.VMEM((D, FFL), BF),
            pltpu.VMEM((DP, QC, DR), BF), pltpu.VMEM((DP, FFL, DR), BF),
            pltpu.VMEM((M * T, R, D), BF),
            pltpu.VMEM((M, 2 * RANK, L), BF),
            pltpu.VMEM((M * HEADS, L, 128), BF),
            pltpu.VMEM((M * PAIRS, L, 128), BF),
            pltpu.VMEM((M * PAIRS, L, 128), BF),
            pltpu.VMEM((M, QC, L), BF),
            pltpu.VMEM((QC, L), BF),
            pltpu.VMEM((M, QC, L), BF),
            pltpu.VMEM((M * HEADS, L), F32),
            pltpu.VMEM((L, FFL), BF),
            pltpu.VMEM((L, FFL), BF),
            pltpu.VMEM((M, 2 * RANK, R), BF),
            pltpu.VMEM((T, R, W), BF),
            pltpu.VMEM((2 * M * (T - 1), R, W), BF),
            pltpu.VMEM((M, R, D), BF),
            pltpu.VMEM((M, R, D), BF),
            pltpu.VMEM((R, D), BF),
            pltpu.VMEM((M * T, R, D), BF),
            pltpu.VMEM((HEADS, L, 128), BF),
            pltpu.VMEM((8, L), F32),
            pltpu.VMEM((2 * RANK, L), BF),
            pltpu.VMEM((PAIRS, L, 128), F32),
            pltpu.VMEM((PAIRS, L, 128), F32),
            pltpu.VMEM((QC, L), F32),
            pltpu.VMEM((L, 3 * QC), BF),
            pltpu.VMEM((RANK, GA), F32),
            pltpu.VMEM((RANK, 4 * D), F32),
            pltpu.VMEM((8, D), F32),
            pltpu.VMEM((M, R, D), F32),
            pltpu.VMEM((R, D), F32),
            pltpu.VMEM((DP, RANK, PW), BF),
            pltpu.VMEM((DP - 1, RANK, PW), BF),
            pltpu.VMEM((DP, RANK, PW), BF),
            pltpu.VMEM((DP, RANK, SW), BF),
            pltpu.VMEM((DP - 1, RANK, SW), BF),
            pltpu.VMEM((DP, RANK, SW), BF),
            pltpu.VMEM((8, D), F32),
            pltpu.VMEM((T - 1, 8, D), F32),
            pltpu.VMEM((DP - 1, 8, D), F32),
            pltpu.SemaphoreType.DMA((4,)),
            pltpu.SemaphoreType.DMA((4, 2, DP)),
            pltpu.SemaphoreType.DMA((4, 2, DP)),
            pltpu.SemaphoreType.DMA((M * (T - 1),)),
            pltpu.SemaphoreType.DMA((M * (T - 1),)),
            pltpu.SemaphoreType.DMA((T,)),
            pltpu.SemaphoreType.DMA((2 * M * (T - 1),)),
            pltpu.SemaphoreType.DMA((M * (T - 1),)),
            pltpu.SemaphoreType.DMA((M * (T - 1),)),
            pltpu.SemaphoreType.DMA((1,)),
            pltpu.SemaphoreType.DMA((2 * M,)),
            pltpu.SemaphoreType.DMA((4,)),
            pltpu.SemaphoreType.REGULAR,
            pltpu.SemaphoreType.DMA((3, T - 1)),
            pltpu.SemaphoreType.DMA((3, T - 1)),
            pltpu.SemaphoreType.DMA((5, DP - 1)),
            pltpu.SemaphoreType.DMA((5, DP - 1)),
        ],
        compiler_params=pltpu.CompilerParams(
            collective_id=0, has_side_effects=True, vmem_limit_bytes=63 * 2**20
        ),
    )


def rope_table(split_flags, length):
    half = ROT // 2
    place = jnp.arange(length, dtype=jnp.int32)
    flags = split_flags.astype(jnp.int32)[:, None]
    places = (place[None] - length // 2 * jnp.where(place[None] >= length // 2, flags, 0)).astype(F32)
    inverse = 10000.0 ** (-jnp.arange(half, dtype=F32) * 2.0 / ROT)
    angles = places[:, :, None] * inverse
    cosine, sine = jnp.cos(angles), jnp.sin(angles)
    pad = HEAD - ROT
    rest = angles.shape[:2] + (pad,)
    cos_head = jnp.concatenate([cosine, cosine, jnp.ones(rest, F32)], axis=-1)
    sin_head = jnp.concatenate([-sine, sine, jnp.zeros(rest, F32)], axis=-1)
    return jnp.concatenate([cos_head, sin_head], axis=-1)


def solution(mesh):
    T = mesh.shape["tensor"]
    DP = mesh.shape["dp"]

    def per_device(
        inputs, cotangent, split,
        query_key_value_weight, output_weight, up_weight, down_weight,
        qkv_adapter_input, qkv_adapter_output, out_adapter_input, out_adapter_output,
        up_adapter_input, up_adapter_output, down_adapter_input, down_adapter_output,
        ln_gain, ln_bias,
    ):
        M, R, D = inputs.shape
        QC = output_weight.shape[1]
        FFL = up_weight.shape[2]
        RANK = qkv_adapter_input.shape[2]
        L = R * T
        wq = query_key_value_weight[0].reshape(-1, 3 * QC)
        aq = qkv_adapter_input[0].astype(BF)
        bq = (ADAPTER_SCALE * qkv_adapter_output[0].reshape(RANK, -1)).astype(BF)
        ao = out_adapter_input[0].astype(BF)
        bo = (ADAPTER_SCALE * out_adapter_output[0]).astype(BF)
        au = up_adapter_input[0].astype(BF)
        bu = (ADAPTER_SCALE * up_adapter_output[0]).astype(BF)
        ad = down_adapter_input[0].astype(BF)
        bd = (ADAPTER_SCALE * down_adapter_output[0]).astype(BF)
        flags = split[:, 0]
        rope = rope_table(flags, L)
        negb = MASKED * flags.astype(F32)
        kernel = make_kernel(T, DP, M, R, D, QC, FFL, RANK)
        act, ig, ga, gr, gb, _, _ = kernel(
            inputs, cotangent, wq, up_weight[0], output_weight[0], down_weight[0],
            aq, bq, ao, bo, au, bu, ad, bd, ln_gain[0], ln_bias[0], rope, negb,
        )
        cuts = [3 * QC, 3 * QC + FFL, 4 * QC + FFL]
        b_qkv, b_up, a_out, a_down = jnp.split(ga, cuts, axis=1)
        a_qkv, a_up, b_out, b_down = jnp.split(gr, 4, axis=1)

        dp_place = lax.axis_index("dp")
        DR = D // DP
        sl = lax.dynamic_slice_in_dim
        c_qkv = wq.astype(F32) + nn(sl(aq, dp_place * DR, DR, 0), bq)
        c_out = output_weight[0].astype(F32) + nn(ao, sl(bo, dp_place * DR, DR, 1))
        c_up = up_weight[0].astype(F32) + nn(sl(au, dp_place * DR, DR, 0), bu)
        c_down = down_weight[0].astype(F32) + nn(ad, sl(bd, dp_place * DR, DR, 1))
        return (
            act[None], ig[None],
            a_qkv.T[None], b_qkv.reshape(qkv_adapter_output.shape),
            a_out.T[None], b_out[None], a_up.T[None], b_up[None], a_down.T[None], b_down[None],
            gb[0:2][None], gb[2:4][None],
            c_qkv.reshape(query_key_value_weight.shape), c_out[None], c_up[None], c_down[None],
        )

    rows = P(None, ("dp", "tensor"), None)
    whole = P("section", None, None)
    in_specs = (
        rows, rows, P(None, "dp"),
        P("section", "dp", None, "tensor"), P("section", "tensor", "dp"),
        P("section", "dp", "tensor"), P("section", "tensor", "dp"),
        whole, P("section", None, None, "tensor"), P("section", "tensor", None), whole,
        whole, P("section", None, "tensor"), P("section", "tensor", None), whole,
        whole, whole,
    )
    layer_rows = P("section", None, ("dp", "tensor"), None)
    out_specs = (
        layer_rows, layer_rows,
        whole, P("section", None, None, "tensor"), P("section", "tensor", None), whole,
        whole, P("section", None, "tensor"), P("section", "tensor", None), whole,
        whole, whole,
        P("section", "dp", None, "tensor"), P("section", "tensor", "dp"),
        P("section", "dp", "tensor"), P("section", "tensor", "dp"),
    )
    return jax.shard_map(
        per_device, mesh=mesh, in_specs=in_specs, out_specs=out_specs, check_vma=False
    )
```

```python
import functools

import jax
import jax.numpy as jnp
import numpy as np
from jax import lax
from jax.experimental import pallas as pl
from jax.experimental.pallas import tpu as pltpu
from jax.sharding import PartitionSpec as P

HEAD = 64
ROT = 16
ADAPTER_SCALE = 0.25
EPSILON = 1e-05
MASKED = -1e30
BF = jnp.bfloat16
F32 = jnp.float32
MESH = pl.DeviceIdType.MESH


def nn(a, b):
    return lax.dot_general(a, b, (((1,), (0,)), ((), ())), preferred_element_type=F32)


def nt(a, b):
    return lax.dot_general(a, b, (((1,), (1,)), ((), ())), preferred_element_type=F32)


def make_kernel(T, DP, M, R, D, QC, FFL, RANK):
    L = R * T
    DR = D // DP
    B = R // 2
    PAIRS = QC // 128
    HEADS = QC // HEAD
    TILE = 256
    HALF = L // 2
    GA = 4 * QC + 2 * FFL
    GRW = 2 * D // T
    PW = -(-GA // (DP * 128)) * 128
    SW = -(-GRW // (DP * 128)) * 128

    def kernel(
        x_in, ct_in, wq_in, wup_in, wout_in, wdn_in,
        aq_in, bq_in, ao_in, bo_in, au_in, bu_in, ad_in, bd_in, gain, bias, rope, split,
        act, ig, ga_out, gr_out, gb_out, dg_hbm,
        aq, bq, ao, bo, au, bu, ad, bd,
        wq, wup, wout, wdn, xh, t12t, qp, kp, vp, kT, vT, oT, lse, hw, dg,
        todt, sbuf, rbuf, srec, sxs, dz, dop, delta, edot, dk, dv, dqt, dqkv,
        ga, gr, gb, xw, yw, pa, pa_in, pa_all, pt, pt_in, pt_all, pb, pb_in, pb_all,
        gb_sum, gb_t, gb_d,
        w_ls, w_ss, w_rs, x_ss, x_rs, r_ss, r_rs, z_ss, z_rs, c_ss, c_rs, l_s, f_s,
        go, at_ss, at_rs, ad_ss, ad_rs,
    ):
        s = lax.axis_index("section")
        d = lax.axis_index("dp")
        t = lax.axis_index("tensor")
        other = 1 - s

        barrier = pltpu.get_barrier_semaphore()
        for k in range(1, T):
            pl.semaphore_signal(
                barrier, inc=1, device_id={"tensor": lax.rem(t + k, T)}, device_id_type=MESH
            )
        for k in range(1, DP):
            pl.semaphore_signal(
                barrier, inc=1, device_id={"dp": lax.rem(d + k, DP)}, device_id_type=MESH
            )
        pl.semaphore_signal(barrier, inc=1, device_id={"section": other}, device_id_type=MESH)
        pl.semaphore_wait(barrier, T + DP - 1)

        def gathered(index, owner):
            if index < 2:
                return (wq, wup)[index].at[pl.ds(pl.multiple_of(owner * DR, DR), DR)]
            return (wout, wdn)[index - 2].at[owner]

        def weight_copy(index, way, hop, owner, own):
            place = gathered(index, owner)
            return pltpu.make_async_remote_copy(
                src_ref=(wq_in, wup_in, wout_in, wdn_in)[index] if own else place, dst_ref=place,
                send_sem=w_ss.at[index, way, hop], recv_sem=w_rs.at[index, way, hop],
                device_id={"dp": d + 1 if way == 0 else d - 1}, device_id_type=MESH,
            )

        has_next = (d < DP - 1, d > 0)

        def holds(way, hop):
            return d >= hop + 1 if way == 0 else d + hop + 1 <= DP - 1

        def owner_of(way, hop):
            return d - hop - 1 if way == 0 else d + hop + 1

        def weight_local(index):
            return pltpu.make_async_copy(
                (wq_in, wup_in, wout_in, wdn_in)[index], gathered(index, d), w_ls.at[index]
            )

        def weights_start(indices):
            for index in indices:
                for way in range(2):
                    @pl.when(has_next[way])
                    def _(index=index, way=way):
                        weight_copy(index, way, 0, d, True).start()

        def weights_hop(indices, hop):
            for index in indices:
                for way in range(2):
                    @pl.when(holds(way, hop))
                    def _(index=index, way=way):
                        weight_copy(index, way, hop, owner_of(way, hop), False).wait_recv()

                        @pl.when(has_next[way])
                        def _():
                            weight_copy(index, way, hop + 1, owner_of(way, hop), False).start()

        def weights_pass(indices, first):
            def step(hop, carry):
                weights_hop(indices, hop)
                return carry

            lax.fori_loop(first, DP - 1, step, 0)

        def weights_sent():
            for index in range(4):
                for way in range(2):
                    @pl.when(has_next[way])
                    def _(index=index, way=way):
                        weight_copy(index, way, 0, d, True).wait_send()

            def step(hop, carry):
                for index in range(4):
                    for way in range(2):
                        @pl.when(jnp.logical_and(has_next[way], holds(way, hop)))
                        def _(index=index, way=way):
                            weight_copy(index, way, hop + 1, owner_of(way, hop), False).wait_send()
                return carry

            lax.fori_loop(0, DP - 1, step, 0)

        for index in range(4):
            weight_local(index).start()

        down, wide = 3 * QC, 3 * QC + FFL
        factors = (
            (aq_in, dk.at[0], aq, 1.0), (au_in, dk.at[1], au, 1.0),
            (ad_in, dv.at[0], ad, 1.0), (ao_in, dv.at[1, 0:QC], ao, 1.0),
            (bq_in, ga.at[:, 0:down], bq, ADAPTER_SCALE), (bu_in, ga.at[:, down:wide], bu, ADAPTER_SCALE),
            (bo_in, gr.at[:, 0:D], bo, ADAPTER_SCALE), (bd_in, gr.at[:, D:2 * D], bd, ADAPTER_SCALE),
        )

        def factor_load(index):
            source, stage, _, _ = factors[index]
            return pltpu.make_async_copy(source, stage, f_s.at[index])

        def factors_take():
            for index in range(8):
                factor_load(index).wait()
            for _, stage, place, scale in factors:
                v = stage[...]
                place[...] = (v if scale == 1.0 else v * scale).astype(BF)
            ga[...] = jnp.zeros_like(ga)
            gr[...] = jnp.zeros_like(gr)
            gb[...] = jnp.zeros_like(gb)

        for index in range(8):
            factor_load(index).start()

        def across(c):
            return lax.rem(t + c, 2) + 2 * lax.rem(t // 2 + c // 2, 2)

        def block(i):
            return pl.ds(pl.multiple_of(i * R, R), R)

        def half(i, low):
            return pl.ds(pl.multiple_of(i * R + (B if low else 0), B), B)

        def rows_copy(buf, m, kind, ssem, rsem):
            if kind < 2:
                place = buf.at[m, block(t)]
            elif kind == 2:
                place = buf.at[m, half(across(1), False)]
            else:
                place = buf.at[m, half(across(2), True)]
            return pltpu.make_async_remote_copy(
                src_ref=place, dst_ref=place,
                send_sem=ssem.at[m * 4 + kind], recv_sem=rsem.at[m * 4 + kind],
                device_id={"tensor": across((1, 2, 2, 1)[kind])}, device_id_type=MESH,
            )

        def rows_wait(buf, m, kind, ssem, rsem):
            if kind < 2:
                place = buf.at[m, block(across(1 + kind))]
            else:
                place = buf.at[m, half(across(3), kind == 3)]
            pltpu.make_async_remote_copy(
                src_ref=place, dst_ref=place,
                send_sem=ssem.at[m * 4 + kind], recv_sem=rsem.at[m * 4 + kind],
                device_id={"tensor": across(1)}, device_id_type=MESH,
            ).wait_recv()

        def rows_start(buf, m, ssem, rsem):
            for kind in range(2):
                rows_copy(buf, m, kind, ssem, rsem).start()

        def rows_next(buf, m, c, ssem, rsem):
            @pl.when(c == 1)
            def _():
                for kind in range(2):
                    rows_wait(buf, m, kind, ssem, rsem)
                    rows_copy(buf, m, 2 + kind, ssem, rsem).start()

            @pl.when(c == 3)
            def _():
                for kind in range(2, 4):
                    rows_wait(buf, m, kind, ssem, rsem)

        def rows_sent(buf, m, ssem, rsem):
            for kind in range(4):
                rows_copy(buf, m, kind, ssem, rsem).wait_send()

        def to_peer(axis, size, me, k, src, dst, ssem, rsem):
            return pltpu.make_async_remote_copy(
                src_ref=src, dst_ref=dst, send_sem=ssem, recv_sem=rsem,
                device_id={axis: lax.rem(me + k, size)}, device_id_type=MESH,
            )

        def block_copy(phase, kind):
            place = (
                sbuf.at[across(1), 0:B], sbuf.at[across(3), 0:B],
                sbuf.at[across(2), B:R], sbuf.at[across(3), B:R],
                sbuf.at[across(2), 0:B], sbuf.at[across(1), B:R],
            )[kind]
            return pltpu.make_async_remote_copy(
                src_ref=place, dst_ref=rbuf.at[lax.rem(phase, M) * 6 + kind],
                send_sem=r_ss.at[kind], recv_sem=r_rs.at[phase * 6 + kind],
                device_id={"tensor": across((1, 1, 2, 2, 2, 1)[kind])}, device_id_type=MESH,
            )

        def blocks_next(phase, m, c):
            @pl.when(c == 3)
            def _():
                block_copy(phase, 1).start()
                block_copy(phase, 3).start()

            @pl.when(c == 2)
            def _():
                block_copy(phase, 2).start()

            @pl.when(c == 1)
            def _():
                block_copy(phase, 0).start()
                block_copy(phase, 1).wait_recv()
                place = across(2)
                sbuf[place, 0:B] = (
                    sbuf[place, 0:B].astype(F32) + rbuf[m * 6 + 1].astype(F32)
                ).astype(BF)
                block_copy(phase, 4).start()
                block_copy(phase, 3).wait_recv()
                place = across(1)
                sbuf[place, B:R] = (
                    sbuf[place, B:R].astype(F32) + rbuf[m * 6 + 3].astype(F32)
                ).astype(BF)
                block_copy(phase, 5).start()

        def block_sum(m, low, cols=slice(None)):
            if low:
                own, first, second = sbuf[t, B:R, cols], rbuf[m * 6 + 2, :, cols], rbuf[m * 6 + 5, :, cols]
            else:
                own, first, second = sbuf[t, 0:B, cols], rbuf[m * 6, :, cols], rbuf[m * 6 + 4, :, cols]
            return own.astype(F32) + (first.astype(F32) + second.astype(F32))

        def blocks_arrive(phase):
            for kind in (0, 2, 4, 5):
                block_copy(phase, kind).wait_recv()

        def blocks_sent(phase):
            for kind in range(6):
                block_copy(phase, kind).wait_send()

        def section_copy(m, phase):
            return pltpu.make_async_remote_copy(
                src_ref=sxs, dst_ref=srec.at[m],
                send_sem=c_ss.at[0], recv_sem=c_rs.at[phase * M + m],
                device_id={"section": other}, device_id_type=MESH,
            )

        def local_copy(src, dst, index):
            return pltpu.make_async_copy(src, dst, l_s.at[index])

        def norm_parts(x):
            mean = jnp.mean(x, axis=-1, keepdims=True)
            centred = x - mean
            spread = jnp.mean(centred * centred, axis=-1, keepdims=True)
            rstd = lax.rsqrt(spread + EPSILON)
            return centred * rstd, rstd

        def send_normed(m):
            xhat, _ = norm_parts(xw[m])
            xh[m, block(t)] = xhat.astype(BF)
            rows_start(xh, m, x_ss, x_rs)

        def take_gradient(m):
            section_copy(m, 1).wait_recv()
            dz[m, block(t)] = srec[m]
            rows_start(dz, m, z_ss, z_rs)

        def take_x(m):
            section_copy(m, 0).wait_recv()
            xw[m] = srec[m].astype(F32)
            send_normed(m)

        lane = lax.broadcasted_iota(jnp.int32, (R, 128), 1)
        in_first = lax.rem(lane, HEAD) < ROT // 2
        head_low = lane < HEAD

        def turn(v, cosine, sine):
            swapped = jnp.where(in_first, pltpu.roll(v, 128 - ROT // 2, 1), pltpu.roll(v, ROT // 2, 1))
            return v * cosine + swapped * sine

        def rope_of(m, chunk):
            again = jnp.where(chunk * R >= HALF, chunk * R - HALF, chunk * R)
            plain = rope[pl.ds(pl.multiple_of(chunk * R, R), R), :]
            restarted = rope[pl.ds(pl.multiple_of(again, R), R), :]
            table = jnp.where(split[m] > 0, restarted, plain)
            crossed = pltpu.roll(table, HEAD, 1)
            return jnp.where(head_low, table, crossed), jnp.where(head_low, crossed, table)

        def head_part(v, hh):
            zero = jnp.zeros_like(v)
            return jnp.where(head_low, v, zero) if hh == 0 else jnp.where(head_low, zero, v)

        causal = lax.broadcasted_iota(jnp.int32, (R, R), 0) <= lax.broadcasted_iota(
            jnp.int32, (R, R), 1
        )

        def scores_t(m, p, i, j, q):
            keys = kp[m * PAIRS + p, j * R:(j + 1) * R, :]
            sc = nt(keys, q)
            if j == i:
                sc = jnp.where(causal, sc, MASKED)
            if i * R >= HALF and j * R < HALF:
                sc = sc + MASKED * split[m].astype(F32)
            return sc

        @pl.when(s == 0)
        def _():
            weights_start((0, 1))
            loads = [local_copy(x_in.at[m], xw.at[m], m) for m in range(M)]
            for copy in loads:
                copy.start()
            for m in range(M):
                loads[m].wait()
                send_normed(m)
            factors_take()
            weights_pass((0, 1), 0)
            weights_start((2, 3))

        @pl.when(s == 1)
        def _():
            loads = [local_copy(ct_in.at[m], xw.at[m], m) for m in range(M)]
            for copy in loads:
                copy.start()
            for m in range(M):
                loads[m].wait()
                dz[m, block(t)] = xw[m].astype(BF)
                rows_start(dz, m, z_ss, z_rs)
            factors_take()
            pl.semaphore_wait(go, 1)
            weights_start((0, 1))
            weights_pass((0, 1), 0)
            weights_start((2, 3))
            take_x(0)

        for index in range(4):
            weight_local(index).wait()

        def normed_to_hidden(m):
            @pl.when(m > 0)
            def _():
                local_copy(dg, dg_hbm.at[m - 1], 2).wait()

            def chunk(c, carry):
                src = across(c)
                rows_next(xh, m, c, x_ss, x_rs)

                @pl.when(jnp.logical_and(c == T - 2, m < DP - 1))
                def _():
                    weights_hop((2, 3), 2 * m)

                rows = block(src)
                xhc = xh[m, rows, :].astype(F32)
                n1 = (xhc * gain[0:1] + bias[0:1]).astype(BF)
                n2 = (xhc * gain[1:2] + bias[1:2]).astype(BF)
                t1 = nn(n1, aq[...]).astype(BF)
                t2 = nn(n2, au[...]).astype(BF)
                t12t[m, 0:RANK, rows] = t1.T
                t12t[m, RANK:2 * RANK, rows] = t2.T
                cosine, sine = rope_of(m, src)
                for part in range(3):
                    cols = slice(part * QC, (part + 1) * QC)
                    val = nn(n1, wq[:, cols]) + nn(t1, bq[:, cols])
                    if part == 2:
                        vb = val.astype(BF)
                        for p in range(PAIRS):
                            vp[m * PAIRS + p, rows, :] = vb[:, p * 128:(p + 1) * 128]
                        vT[m, :, rows] = vb.T
                    else:
                        for p in range(PAIRS):
                            v = turn(val[:, p * 128:(p + 1) * 128], cosine, sine)
                            if part == 0:
                                qp[m * PAIRS + p, rows, :] = (v * 0.125).astype(BF)
                            else:
                                vb = v.astype(BF)
                                kp[m * PAIRS + p, rows, :] = vb
                                kT[m, p * 128:(p + 1) * 128, rows] = vb.T
                for n0 in range(0, FFL, TILE):
                    cols = slice(n0, n0 + TILE)
                    u = nn(n2, wup[:, cols]) + nn(t2, bu[:, cols])
                    phi = 0.5 * (1.0 + lax.erf(u * 0.7071067811865476))
                    hw[m, rows, cols] = (u * phi).astype(BF)
                    dg[rows, cols] = (
                        phi + u * (0.3989422804014327 * jnp.exp(-0.5 * u * u))
                    ).astype(BF)
                return carry

            lax.fori_loop(0, T, chunk, 0)
            local_copy(dg, dg_hbm.at[m], 2).start()

        def attend(m):
            for i in range(T):
                icols = slice(i * R, (i + 1) * R)

                def pair(p, carry, i=i, icols=icols):
                    for hh in range(2):
                        h = 2 * p + hh
                        q = head_part(qp[m * PAIRS + p, icols, :], hh)
                        hrows = pl.ds(pl.multiple_of(h * HEAD, HEAD), HEAD)
                        blocks = [scores_t(m, p, i, j, q) for j in range(i + 1)]
                        top = functools.reduce(
                            jnp.maximum, [jnp.max(b, axis=0, keepdims=True) for b in blocks]
                        )
                        total = jnp.zeros_like(top)
                        acc = jnp.zeros((HEAD, R), F32)
                        for j in range(i + 1):
                            e = jnp.exp(blocks[j] - top)
                            total = total + jnp.sum(e, axis=0, keepdims=True)
                            acc = acc + nn(vT[m, hrows, j * R:(j + 1) * R], e.astype(BF))
                        oT[m, hrows, icols] = (acc * (1.0 / total)).astype(BF)
                        lse[pl.ds(m * HEADS + h, 1), icols] = top + jnp.log(total)
                    return carry

                lax.fori_loop(0, PAIRS, pair, 0)

        def project(m):
            def step(n, carry):
                c = T - 1 - n
                i = across(c)
                rows = block(i)
                o = oT[m, :, rows].T
                hrow = hw[m, rows, :]
                to = nn(o, ao[...]).astype(BF)
                td = nn(hrow, ad[...]).astype(BF)
                todt[m, 0:RANK, rows] = to.T
                todt[m, RANK:2 * RANK, rows] = td.T
                for j in range(DP):
                    cols = slice(j * DR, (j + 1) * DR)
                    sbuf[i, :, cols] = (
                        nn(o, wout[j]) + nn(hrow, wdn[j]) + nn(to, bo[:, cols]) + nn(td, bd[:, cols])
                    ).astype(BF)
                blocks_next(m, m, c)
                return carry

            lax.fori_loop(0, T, step, 0)

        def finish_forward(m):
            @pl.when(m > 0)
            def _():
                local_copy(yw, act.at[m - 1], 3).wait()

            blocks_arrive(m)
            for low in range(2):
                rows = slice(low * B, (low + 1) * B)
                y = xw[m, rows, :] + block_sum(m, low)
                yw[rows, :] = y
                sxs[rows, :] = y.astype(BF)

            @pl.when(s == 0)
            def _():
                section_copy(m, 0).start()

            local_copy(yw, act.at[m], 3).start()
            rows_sent(xh, m, x_ss, x_rs)
            blocks_sent(m)

            @pl.when(s == 0)
            def _():
                section_copy(m, 0).wait_send()

        def forward(step, carry):
            @pl.when(step < M)
            def _():
                normed_to_hidden(step)

            @pl.when(step == 1)
            def _():
                weights_pass((2, 3), 3)
                weights_sent()

                @pl.when(s == 0)
                def _():
                    pl.semaphore_signal(go, inc=1, device_id={"section": other}, device_id_type=MESH)

            @pl.when(step > 0)
            def _():
                project(step - 1)

            @pl.when(jnp.logical_and(s == 1, step < M - 1))
            def _():
                take_x(step + 1)

            @pl.when(step < M)
            def _():
                attend(step)

            @pl.when(step == 0)
            def _():
                if DP > 2:
                    weights_hop((2, 3), 1)

            @pl.when(jnp.logical_or(jnp.logical_and(step > 0, step < M), jnp.logical_and(step == M, s == 0)))
            def _():
                finish_forward(step - 1)
            return carry

        lax.fori_loop(0, M + 1, forward, 0)
        local_copy(dg, dg_hbm.at[M - 1], 2).wait()
        local_copy(dg_hbm.at[0], dg, 2).start()

        def gradient_to_hidden(m):
            local_copy(dg_hbm.at[m], dg, 2).wait()

            def chunk(c, carry):
                src = across(c)
                rows_next(dz, m, c, z_ss, z_rs)
                rows = block(src)
                full = dz[m, rows, :]
                eo = nt(full, bo[...]).astype(BF)
                ed = nt(full, bd[...]).astype(BF)
                edot[0:RANK, rows] = eo.T
                edot[RANK:2 * RANK, rows] = ed.T
                do = nt(eo, ao[...])
                for j in range(DP):
                    do = do + nt(full[:, j * DR:(j + 1) * DR], wout[j])
                dob = do.astype(BF)
                for p in range(PAIRS):
                    v = dob[:, p * 128:(p + 1) * 128]
                    dop[p, rows, :] = v
                prod = dob.T.astype(F32) * oT[m, :, rows].astype(F32)
                for h in range(HEADS):
                    delta[h:h + 1, rows] = jnp.sum(
                        prod[h * HEAD:(h + 1) * HEAD], axis=0, keepdims=True
                    )
                for n0 in range(0, FFL, TILE):
                    cols = slice(n0, n0 + TILE)
                    v = nt(ed, ad[cols, :])
                    for j in range(DP):
                        v = v + nt(full[:, j * DR:(j + 1) * DR], wdn[j, cols, :])
                    dg[rows, cols] = (v * dg[rows, cols].astype(F32)).astype(BF)
                return carry

            lax.fori_loop(0, T, chunk, 0)

        def attention_back(m):
            dk[...] = jnp.zeros_like(dk)
            dv[...] = jnp.zeros_like(dv)
            for i in range(T):
                icols = slice(i * R, (i + 1) * R)

                def pair(p, carry, i=i, icols=icols):
                    for hh in range(2):
                        h = 2 * p + hh
                        q = head_part(qp[m * PAIRS + p, icols, :], hh)
                        do = head_part(dop[p, icols, :], hh)
                        hrows = pl.ds(pl.multiple_of(h * HEAD, HEAD), HEAD)
                        low = lse[pl.ds(m * HEADS + h, 1), icols]
                        dlt = delta[pl.ds(h, 1), icols]
                        acc = jnp.zeros((HEAD, R), F32)
                        for j in range(i + 1):
                            jrows = slice(j * R, (j + 1) * R)
                            prob = jnp.exp(scores_t(m, p, i, j, q) - low)
                            dp_t = nt(vp[m * PAIRS + p, jrows, :], do)
                            ds_t = (prob * (dp_t - dlt)).astype(BF)
                            dv[p, jrows, :] += nn(prob.astype(BF), do)
                            dk[p, jrows, :] += nn(ds_t, q)
                            acc = acc + nn(kT[m, hrows, jrows], ds_t)
                        dqt[hrows, icols] = acc
                    return carry

                lax.fori_loop(0, PAIRS, pair, 0)

        def turn_back(m):
            def step(i, carry):
                rows = block(i)
                cosine, sine = rope_of(m, i)
                sine = -sine
                dq = dqt[:, rows].T * 0.125
                for p in range(PAIRS):
                    lanes = slice(p * 128, (p + 1) * 128)
                    dqkv[rows, p * 128:(p + 1) * 128] = turn(dq[:, lanes], cosine, sine).astype(BF)
                    dqkv[rows, QC + p * 128:QC + (p + 1) * 128] = turn(
                        dk[p, rows, :], cosine, sine
                    ).astype(BF)
                    dqkv[rows, 2 * QC + p * 128:2 * QC + (p + 1) * 128] = dv[p, rows, :].astype(BF)
                dop[0, rows, :] = nt(dqkv[rows, :], bq[...]).astype(BF)
                dop[1, rows, :] = nt(dg[rows, :], bu[...]).astype(BF)
                return carry

            lax.fori_loop(0, T, step, 0)

        def project_back(m):
            def tail(n, carry):
                c = T - 1 - n
                i = across(c)
                rows = block(i)
                dj = dqkv[rows, :]
                du = dg[rows, :]
                e1 = dop[0, rows, :]
                e2 = dop[1, rows, :]
                for n0 in range(0, D, TILE):
                    cols = slice(n0, n0 + TILE)
                    dn1 = nt(dj, wq[cols, :]) + nt(e1, aq[cols, :])
                    dn2 = nt(du, wup[cols, :]) + nt(e2, au[cols, :])
                    xhc = xh[m, rows, cols].astype(F32)
                    gb[0:1, cols] += jnp.sum(dn1 * xhc, axis=0, keepdims=True)
                    gb[1:2, cols] += jnp.sum(dn2 * xhc, axis=0, keepdims=True)
                    gb[2:3, cols] += jnp.sum(dn1, axis=0, keepdims=True)
                    gb[3:4, cols] += jnp.sum(dn2, axis=0, keepdims=True)
                    sbuf[i, :, cols] = (dn1 * gain[0:1, cols] + dn2 * gain[1:2, cols]).astype(BF)
                blocks_next(M + m, m, c)
                return carry

            lax.fori_loop(0, T, tail, 0)

            @pl.when(m == 0)
            def _():
                local_copy(yw, act.at[M - 1], 3).wait()

            @pl.when(m > 0)
            def _():
                local_copy(yw, ig.at[m - 1], 3).wait()

            @pl.when(s == 1)
            def _():
                local_copy(ct_in.at[m], yw, 0).start()

        def factor_gradients(m):
            base = 0
            ga[:, base:base + 3 * QC] += ADAPTER_SCALE * nn(t12t[m, 0:RANK, :], dqkv[...])
            base += 3 * QC
            ga[:, base:base + FFL] += ADAPTER_SCALE * nn(t12t[m, RANK:2 * RANK, :], dg[...])
            base += FFL
            ga[:, base:base + QC] += nt(edot[0:RANK, :], oT[m])
            base += QC
            ga[:, base:base + FFL] += nn(edot[RANK:2 * RANK, :], hw[m])
            gr[:, 2 * D:3 * D] += ADAPTER_SCALE * nn(todt[m, 0:RANK, :], dz[m])
            gr[:, 3 * D:4 * D] += ADAPTER_SCALE * nn(todt[m, RANK:2 * RANK, :], dz[m])

            def step(i, carry):
                rows = block(i)
                xhc = xh[m, rows, :].astype(F32)
                n1 = (xhc * gain[0:1] + bias[0:1]).astype(BF)
                gr[:, 0:D] += nn(dop[0, rows, :].T, n1)
                n2 = (xhc * gain[1:2] + bias[1:2]).astype(BF)
                gr[:, D:2 * D] += nn(dop[1, rows, :].T, n2)
                return carry

            lax.fori_loop(0, T, step, 0)

        def next_hidden(m):
            @pl.when(m < M - 1)
            def _():
                local_copy(dg_hbm.at[m + 1], dg, 2).start()

        def finish_backward(m):
            @pl.when(s == 1)
            def _():
                local_copy(ct_in.at[m], yw, 0).wait()

            @pl.when(s == 0)
            def _():
                yw[...] = srec[m].astype(F32)

            blocks_arrive(M + m)
            for low in range(2):
                rows = slice(low * B, (low + 1) * B)
                xhat, rstd = norm_parts(xw[m, rows, :])
                g = block_sum(m, low)
                mean_g = jnp.mean(g, axis=1, keepdims=True)
                mean_gx = jnp.mean(g * xhat, axis=1, keepdims=True)
                v = yw[rows, :] + (g - mean_g - xhat * mean_gx) * rstd
                yw[rows, :] = v
                sxs[rows, :] = v.astype(BF)

            @pl.when(s == 1)
            def _():
                section_copy(m, 1).start()

            local_copy(yw, ig.at[m], 3).start()
            rows_sent(dz, m, z_ss, z_rs)
            blocks_sent(M + m)

            @pl.when(s == 1)
            def _():
                section_copy(m, 1).wait_send()

        def over_dp(index, source, landing):
            for k in range(1, DP):
                yield to_peer("dp", DP, d, k, source(lax.rem(d + k, DP)), landing(k - 1),
                              ad_ss.at[index, k - 1], ad_rs.at[index, k - 1])

        def over_tensor(index, source, landing):
            for k in range(1, T):
                yield to_peer("tensor", T, t, k, source(lax.rem(t + k, T)), landing(k - 1),
                              at_ss.at[index, k - 1], at_rs.at[index, k - 1])

        def pa_scatter():
            return over_dp(0, lambda j: pa.at[j], lambda k: pa_in.at[k])

        def pa_gather():
            return over_dp(1, lambda j: pa_all.at[d], lambda k: pa_all.at[d])

        def pb_scatter(part):
            return over_dp(2 + part, lambda j: pb.at[part * DP + j], lambda k: pb_in.at[part * (DP - 1) + k])

        def pb_gather(part):
            place = pb_all.at[part * DP + d]
            return over_dp(4 + part, lambda j: place, lambda k: place)

        def pt_scatter(part):
            return over_tensor(part, lambda j: pt.at[part * T + j], lambda k: pt_in.at[part * (T - 1) + k])

        def pt_gather(part):
            return over_tensor(2 + part, lambda j: pt.at[part * T + t], lambda k: pt_all.at[part * (T - 1) + k])

        def gb_tensor():
            return over_tensor(4, lambda j: gb, lambda k: gb_t.at[k])

        def gb_dp():
            return over_dp(6, lambda j: gb_sum, lambda k: gb_d.at[k])

        def gathered_wait(index, buf, base):
            for k in range(1, DP):
                place = buf.at[base + lax.rem(d - k + DP, DP)]
                to_peer("dp", DP, d, k, place, place,
                        ad_ss.at[index, k - 1], ad_rs.at[index, k - 1]).wait_recv()

        def start_all(copies):
            for copy in copies:
                copy.start()

        def arrive_all(copies):
            for copy in copies:
                copy.wait_recv()

        def sent_all(copies):
            for copy in copies:
                copy.wait_send()

        def fill(buf, base, value, width):
            total = value.shape[1]
            for j in range(DP):
                lo, hi = min(j * width, total), min((j + 1) * width, total)
                if hi > lo:
                    buf[base + j, :, 0:hi - lo] = value[:, lo:hi].astype(BF)
                if hi - lo < width:
                    buf[base + j, :, hi - lo:width] = jnp.zeros((RANK, width - hi + lo), BF)

        def pt_fill(part):
            for j in range(T):
                lo = part * 2 * D + j * GRW
                pt[part * T + j] = gr[:, lo:lo + GRW].astype(BF)

        def pt_to_pb(part):
            arrive_all(pt_scatter(part))
            v = pt[part * T + t].astype(F32)
            for k in range(T - 1):
                v = v + pt_in[part * (T - 1) + k].astype(F32)
            fill(pb, part * DP, v, SW)
            start_all(pb_scatter(part))

        def pb_add(part):
            arrive_all(pb_scatter(part))
            v = pb[part * DP + d].astype(F32)
            for k in range(DP - 1):
                v = v + pb_in[part * (DP - 1) + k].astype(F32)
            pb_all[part * DP + d] = v.astype(BF)
            start_all(pb_gather(part))

        def pb_to_pt(part):
            gathered_wait(4 + part, pb_all, part * DP)
            for j in range(DP):
                lo, hi = min(j * SW, GRW), min((j + 1) * SW, GRW)
                if hi > lo:
                    pt[part * T + t, :, lo:hi] = pb_all[part * DP + j, :, 0:hi - lo]
            start_all(pt_gather(part))

        def gr_place(part, owner):
            return gr_out.at[:, pl.ds(pl.multiple_of(part * 2 * D + owner * GRW, 128), GRW)]

        def gr_store(part, k):
            if k == 0:
                return pltpu.make_async_copy(pt.at[part * T + t], gr_place(part, t), f_s.at[part * T])
            return pltpu.make_async_copy(
                pt_all.at[part * (T - 1) + k - 1], gr_place(part, lax.rem(t - k + T, T)),
                f_s.at[part * T + k],
            )

        def backward(step, carry):
            gradient_to_hidden(step)

            @pl.when(jnp.logical_and(s == 1, step == 0))
            def _():
                finish_forward(M - 1)

            @pl.when(jnp.logical_and(s == 0, step > 0))
            def _():
                finish_backward(step - 1)

            attention_back(step)
            turn_back(step)

            @pl.when(step < M - 1)
            def _():
                project_back(step)

                @pl.when(s == 0)
                def _():
                    take_gradient(step + 1)

                factor_gradients(step)
                next_hidden(step)

            @pl.when(step == M - 1)
            def _():
                factor_gradients(step)
                for part in range(2):
                    pt_fill(part)
                    start_all(pt_scatter(part))
                fill(pa, 0, ga, PW)
                start_all(pa_scatter())
                project_back(step)
                start_all(gb_tensor())
                for part in range(2):
                    pt_to_pb(part)
                arrive_all(pa_scatter())
                v = pa[d].astype(F32)
                for k in range(DP - 1):
                    v = v + pa_in[k].astype(F32)
                pa_all[d] = v.astype(BF)
                start_all(pa_gather())
                for part in range(2):
                    pb_add(part)

            @pl.when(jnp.logical_or(s == 1, step == M - 1))
            def _():
                finish_backward(step)
            return carry

        @pl.when(s == 0)
        def _():
            take_gradient(0)

        lax.fori_loop(0, M, backward, 0)

        arrive_all(gb_tensor())
        total = gb[...]
        for k in range(T - 1):
            total = total + gb_t[k]
        gb_sum[...] = total
        start_all(gb_dp())
        for part in range(2):
            pb_to_pt(part)
        arrive_all(gb_dp())
        sent_all(gb_tensor())
        total = gb_sum[...]
        for k in range(DP - 1):
            total = total + gb_d[k]
        gb[...] = total
        outs = [local_copy(gb, gb_out, 0)]
        outs[0].start()
        gathered_wait(1, pa_all, 0)
        for j in range(DP):
            copy = pltpu.make_async_copy(
                pa_all.at[j], ga_out.at[:, j * PW:(j + 1) * PW], w_ls.at[4 + j]
            )
            copy.start()
            outs.append(copy)
        for part in range(2):
            arrive_all(pt_gather(part))
            for k in range(T):
                copy = gr_store(part, k)
                copy.start()
                outs.append(copy)
        for copies in (pa_scatter(), pa_gather(), gb_dp(), pt_scatter(0), pt_scatter(1),
                       pt_gather(0), pt_gather(1), pb_scatter(0), pb_scatter(1),
                       pb_gather(0), pb_gather(1)):
            sent_all(copies)
        for copy in outs:
            copy.wait()
        local_copy(yw, ig.at[M - 1], 3).wait()

    any_spec = pl.BlockSpec(memory_space=pl.ANY)
    vmem_spec = pl.BlockSpec(memory_space=pltpu.VMEM)
    smem_spec = pl.BlockSpec(memory_space=pltpu.SMEM)
    shapes = jax.ShapeDtypeStruct
    return pl.pallas_call(
        kernel,
        out_shape=(
            shapes((M, R, D), F32), shapes((M, R, D), F32),
            shapes((RANK, DP * PW), BF), shapes((RANK, 4 * D), BF), shapes((8, D), F32),
            shapes((M, L, FFL), BF),
        ),
        in_specs=[any_spec] * 14 + [vmem_spec] * 3 + [smem_spec],
        out_specs=(any_spec,) * 6,
        scratch_shapes=[
            pltpu.VMEM((D, RANK), BF), pltpu.VMEM((RANK, 3 * QC), BF),
            pltpu.VMEM((QC, RANK), BF), pltpu.VMEM((RANK, D), BF),
            pltpu.VMEM((D, RANK), BF), pltpu.VMEM((RANK, FFL), BF),
            pltpu.VMEM((FFL, RANK), BF), pltpu.VMEM((RANK, D), BF),
            pltpu.VMEM((D, 3 * QC), BF), pltpu.VMEM((D, FFL), BF),
            pltpu.VMEM((DP, QC, DR), BF), pltpu.VMEM((DP, FFL, DR), BF),
            pltpu.VMEM((M, L, D), BF),
            pltpu.VMEM((M, 2 * RANK, L), BF),
            pltpu.VMEM((M * PAIRS, L, 128), BF),
            pltpu.VMEM((M * PAIRS, L, 128), BF),
            pltpu.VMEM((M * PAIRS, L, 128), BF),
            pltpu.VMEM((M, QC, L), BF),
            pltpu.VMEM((M, QC, L), BF),
            pltpu.VMEM((M, QC, L), BF),
            pltpu.VMEM((M * HEADS, L), F32),
            pltpu.VMEM((M, L, FFL), BF),
            pltpu.VMEM((L, FFL), BF),
            pltpu.VMEM((M, 2 * RANK, L), BF),
            pltpu.VMEM((T, R, D), BF),
            pltpu.VMEM((M * 6, B, D), BF),
            pltpu.VMEM((M, R, D), BF),
            pltpu.VMEM((R, D), BF),
            pltpu.VMEM((M, L, D), BF),
            pltpu.VMEM((PAIRS, L, 128), BF),
            pltpu.VMEM((8, L), F32),
            pltpu.VMEM((2 * RANK, L), BF),
            pltpu.VMEM((PAIRS, L, 128), F32),
            pltpu.VMEM((PAIRS, L, 128), F32),
            pltpu.VMEM((QC, L), F32),
            pltpu.VMEM((L, 3 * QC), BF),
            pltpu.VMEM((RANK, GA), F32),
            pltpu.VMEM((RANK, 4 * D), F32),
            pltpu.VMEM((8, D), F32),
            pltpu.VMEM((M, R, D), F32),
            pltpu.VMEM((R, D), F32),
            pltpu.VMEM((DP, RANK, PW), BF),
            pltpu.VMEM((DP - 1, RANK, PW), BF),
            pltpu.VMEM((DP, RANK, PW), BF),
            pltpu.VMEM((2 * T, RANK, GRW), BF),
            pltpu.VMEM((2 * (T - 1), RANK, GRW), BF),
            pltpu.VMEM((2 * (T - 1), RANK, GRW), BF),
            pltpu.VMEM((2 * DP, RANK, SW), BF),
            pltpu.VMEM((2 * (DP - 1), RANK, SW), BF),
            pltpu.VMEM((2 * DP, RANK, SW), BF),
            pltpu.VMEM((8, D), F32),
            pltpu.VMEM((T - 1, 8, D), F32),
            pltpu.VMEM((DP - 1, 8, D), F32),
            pltpu.SemaphoreType.DMA((4 + DP,)),
            pltpu.SemaphoreType.DMA((4, 2, DP)),
            pltpu.SemaphoreType.DMA((4, 2, DP)),
            pltpu.SemaphoreType.DMA((M * 4,)),
            pltpu.SemaphoreType.DMA((M * 4,)),
            pltpu.SemaphoreType.DMA((6,)),
            pltpu.SemaphoreType.DMA((2 * M * 6,)),
            pltpu.SemaphoreType.DMA((M * 4,)),
            pltpu.SemaphoreType.DMA((M * 4,)),
            pltpu.SemaphoreType.DMA((1,)),
            pltpu.SemaphoreType.DMA((2 * M,)),
            pltpu.SemaphoreType.DMA((4,)),
            pltpu.SemaphoreType.DMA((2 * max(T, 4),)),
            pltpu.SemaphoreType.REGULAR,
            pltpu.SemaphoreType.DMA((5, T - 1)),
            pltpu.SemaphoreType.DMA((5, T - 1)),
            pltpu.SemaphoreType.DMA((7, DP - 1)),
            pltpu.SemaphoreType.DMA((7, DP - 1)),
        ],
        compiler_params=pltpu.CompilerParams(
            collective_id=0, has_side_effects=True, vmem_limit_bytes=63 * 2**20
        ),
    )


def rope_table(length):
    half = ROT // 2
    inverse = np.float32(10000.0) ** (-np.arange(half, dtype=np.float32) * np.float32(2.0 / ROT))
    angles = np.arange(length, dtype=np.float32)[:, None] * inverse[None, :]
    cosine, sine = np.cos(angles.astype(np.float64)), np.sin(angles.astype(np.float64))
    rest = np.zeros((length, HEAD - ROT))
    return np.concatenate(
        [cosine, cosine, rest + 1.0, -sine, sine, rest], axis=-1
    ).astype(np.float32)


def solution(mesh):
    T = mesh.shape["tensor"]
    DP = mesh.shape["dp"]

    def per_device(
        inputs, cotangent, split,
        query_key_value_weight, output_weight, up_weight, down_weight,
        qkv_adapter_input, qkv_adapter_output, out_adapter_input, out_adapter_output,
        up_adapter_input, up_adapter_output, down_adapter_input, down_adapter_output,
        ln_gain, ln_bias,
    ):
        M, R, D = inputs.shape
        QC = output_weight.shape[1]
        FFL = up_weight.shape[2]
        RANK = qkv_adapter_input.shape[2]
        L = R * T
        wq = query_key_value_weight[0].reshape(-1, 3 * QC)
        aq = qkv_adapter_input[0].astype(BF)
        bq = (ADAPTER_SCALE * qkv_adapter_output[0].reshape(RANK, -1)).astype(BF)
        ao = out_adapter_input[0].astype(BF)
        bo = (ADAPTER_SCALE * out_adapter_output[0]).astype(BF)
        au = up_adapter_input[0].astype(BF)
        bu = (ADAPTER_SCALE * up_adapter_output[0]).astype(BF)
        ad = down_adapter_input[0].astype(BF)
        bd = (ADAPTER_SCALE * down_adapter_output[0]).astype(BF)
        kernel = make_kernel(T, DP, M, R, D, QC, FFL, RANK)
        act, ig, ga, gr, gb, _ = kernel(
            inputs, cotangent, wq, up_weight[0], output_weight[0], down_weight[0],
            qkv_adapter_input[0], qkv_adapter_output[0].reshape(RANK, -1),
            out_adapter_input[0], out_adapter_output[0],
            up_adapter_input[0], up_adapter_output[0],
            down_adapter_input[0], down_adapter_output[0],
            ln_gain[0], ln_bias[0], jnp.asarray(rope_table(L)), split[:, 0],
        )
        ga = ga.astype(F32)
        gr = gr.astype(F32)
        cuts = [3 * QC, 3 * QC + FFL, 4 * QC + FFL, 4 * QC + 2 * FFL]
        b_qkv, b_up, a_out, a_down, _ = jnp.split(ga, cuts, axis=1)
        a_qkv, a_up, b_out, b_down = jnp.split(gr, 4, axis=1)

        dp_place = lax.axis_index("dp")
        DR = D // DP
        sl = lax.dynamic_slice_in_dim
        c_qkv = wq.astype(F32) + nn(sl(aq, dp_place * DR, DR, 0), bq)
        c_out = output_weight[0].astype(F32) + nn(ao, sl(bo, dp_place * DR, DR, 1))
        c_up = up_weight[0].astype(F32) + nn(sl(au, dp_place * DR, DR, 0), bu)
        c_down = down_weight[0].astype(F32) + nn(ad, sl(bd, dp_place * DR, DR, 1))
        return (
            act[None], ig[None],
            a_qkv.T[None], b_qkv.reshape(qkv_adapter_output.shape),
            a_out.T[None], b_out[None], a_up.T[None], b_up[None], a_down.T[None], b_down[None],
            gb[0:2][None], gb[2:4][None],
            c_qkv.reshape(query_key_value_weight.shape), c_out[None], c_up[None], c_down[None],
        )

    rows = P(None, ("dp", "tensor"), None)
    whole = P("section", None, None)
    in_specs = (
        rows, rows, P(None, "dp"),
        P("section", "dp", None, "tensor"), P("section", "tensor", "dp"),
        P("section", "dp", "tensor"), P("section", "tensor", "dp"),
        whole, P("section", None, None, "tensor"), P("section", "tensor", None), whole,
        whole, P("section", None, "tensor"), P("section", "tensor", None), whole,
        whole, whole,
    )
    layer_rows = P("section", None, ("dp", "tensor"), None)
    out_specs = (
        layer_rows, layer_rows,
        whole, P("section", None, None, "tensor"), P("section", "tensor", None), whole,
        whole, P("section", None, "tensor"), P("section", "tensor", None), whole,
        whole, whole,
        P("section", "dp", None, "tensor"), P("section", "tensor", "dp"),
        P("section", "dp", "tensor"), P("section", "tensor", "dp"),
    )
    return jax.shard_map(
        per_device, mesh=mesh, in_specs=in_specs, out_specs=out_specs, check_vma=False
    )
```

```python
import functools

import jax
import jax.numpy as jnp
import numpy as np
from jax import lax
from jax.experimental import pallas as pl
from jax.experimental.pallas import tpu as pltpu
from jax.sharding import PartitionSpec as P

HEAD = 64
ROT = 16
ADAPTER_SCALE = 0.25
EPSILON = 1e-05
MASKED = -1e30
BF = jnp.bfloat16
F32 = jnp.float32
MESH = pl.DeviceIdType.MESH


def nn(a, b):
    return lax.dot_general(a, b, (((1,), (0,)), ((), ())), preferred_element_type=F32)


def nt(a, b):
    return lax.dot_general(a, b, (((1,), (1,)), ((), ())), preferred_element_type=F32)


def make_kernel(T, DP, M, R, D, QC, FFL, RANK):
    L = R * T
    DR = D // DP
    B = R // 2
    PAIRS = QC // 128
    HEADS = QC // HEAD
    TILE = 256
    HALF = L // 2
    GA = 4 * QC + 2 * FFL
    GRW = 2 * D // T
    PW = -(-GA // (DP * 128)) * 128
    SW = -(-GRW // (DP * 128)) * 128
    NA, NB = -(-GA // PW), -(-GRW // SW)

    def kernel(
        x_in, ct_in, wq_in, wup_in, wout_in, wdn_in,
        aq_in, bq_in, ao_in, bo_in, au_in, bu_in, ad_in, bd_in, gain_in, bias_in, rope, split,
        act, ig, ga_out, gr_out, gb_out, h_hbm, dg_hbm,
        aq, bq, ao, bo, au, bu, ad, bd, norms,
        wq, wup, wout, wdn, xh, t12t, qp, kp, vp, kT, vT, oT, lse, hw, dg,
        todt, sbuf, rbuf, dz, dop, delta, edot, dk, dv, dqt, dqkv,
        acc, gb, xw, yw, pa, pa_x, pa_in, pa_sum, pt, pt_x, pt_in, pb, pb_in, pb_all,
        gb_x, gb_sum, gb_t, gb_d,
        w_ls, w_ss, w_rs, v_ss, v_rs, x_ss, x_rs, r_ss, r_rs, z_ss, z_rs, c_ss, c_rs, l_s, f_s,
        go, at_ss, at_rs, ad_ss, ad_rs,
    ):
        s = lax.axis_index("section")
        d = lax.axis_index("dp")
        t = lax.axis_index("tensor")
        other = 1 - s

        barrier = pltpu.get_barrier_semaphore()
        for k in range(1, T):
            pl.semaphore_signal(
                barrier, inc=1, device_id={"tensor": lax.rem(t + k, T)}, device_id_type=MESH
            )
        for k in range(1, DP):
            pl.semaphore_signal(
                barrier, inc=1, device_id={"dp": lax.rem(d + k, DP)}, device_id_type=MESH
            )
        pl.semaphore_signal(barrier, inc=1, device_id={"section": other}, device_id_type=MESH)
        pl.semaphore_wait(barrier, T + DP - 1)

        def to_other(src, dst, ssem, rsem):
            return pltpu.make_async_remote_copy(
                src_ref=src, dst_ref=dst, send_sem=ssem, recv_sem=rsem,
                device_id={"section": other}, device_id_type=MESH,
            )

        shards = (wq_in, wup_in, wout_in, wdn_in)

        def gathered(index, layer, owner):
            return (wq, wup, wout, wdn)[index].at[layer, pl.ds(pl.multiple_of(owner * DR, DR), DR)]

        def weight_copy(index, way, hop, owner, own):
            place = gathered(index, s, owner)
            return pltpu.make_async_remote_copy(
                src_ref=shards[index] if own else place, dst_ref=place,
                send_sem=w_ss.at[index, way, hop], recv_sem=w_rs.at[index, way, hop],
                device_id={"dp": d + 1 if way == 0 else d - 1}, device_id_type=MESH,
            )

        def weight_over(index, layer, owner, own):
            place = gathered(index, layer, owner)
            return to_other(
                shards[index] if own else place, place, v_ss.at[index, owner], v_rs.at[index, owner]
            )

        has_next = (d < DP - 1, d > 0)

        def holds(way, hop):
            return d >= hop + 1 if way == 0 else d + hop + 1 <= DP - 1

        def owner_of(way, hop):
            return d - hop - 1 if way == 0 else d + hop + 1

        def weight_local(index):
            return pltpu.make_async_copy(shards[index], gathered(index, s, d), w_ls.at[index])

        def weights_start(indices):
            for index in indices:
                for way in range(2):
                    @pl.when(has_next[way])
                    def _(index=index, way=way):
                        weight_copy(index, way, 0, d, True).start()
                weight_over(index, s, d, True).start()

        def weights_hop(indices, hop):
            for index in indices:
                for way in range(2):
                    @pl.when(holds(way, hop))
                    def _(index=index, way=way):
                        owner = owner_of(way, hop)
                        weight_copy(index, way, hop, owner, False).wait_recv()

                        @pl.when(has_next[way])
                        def _():
                            weight_copy(index, way, hop + 1, owner, False).start()

                        weight_over(index, s, owner, False).start()

        def weights_pass(indices, first, last):
            if last > first:
                def step(hop, carry):
                    weights_hop(indices, hop)
                    return carry

                lax.fori_loop(first, last, step, 0)

        def weights_sent():
            for index in range(4):
                for way in range(2):
                    @pl.when(has_next[way])
                    def _(index=index, way=way):
                        weight_copy(index, way, 0, d, True).wait_send()

            def step(hop, carry):
                for index in range(4):
                    for way in range(2):
                        @pl.when(jnp.logical_and(has_next[way], holds(way, hop)))
                        def _(index=index, way=way):
                            weight_copy(index, way, hop + 1, owner_of(way, hop), False).wait_send()
                return carry

            lax.fori_loop(0, DP - 1, step, 0)

        def weights_from_other(indices, layer):
            def step(owner, carry):
                for index in indices:
                    weight_over(index, layer, owner, False).wait_recv()
                return carry

            lax.fori_loop(0, DP, step, 0)

        for index in range(4):
            weight_local(index).start()

        factors = (
            (aq_in, dk.at[0], aq, 1.0), (au_in, dk.at[1], au, 1.0),
            (ad_in, dv.at[0], ad, 1.0), (ao_in, dv.at[1, 0:QC], ao, 1.0),
            (bq_in, acc.at[0:RANK, 0:3 * QC], bq, ADAPTER_SCALE), (bu_in, acc.at[RANK:, 0:FFL], bu, ADAPTER_SCALE),
            (bo_in, dqt.at[0:RANK, 0:D], bo, ADAPTER_SCALE), (bd_in, dqt.at[RANK:2 * RANK, 0:D], bd, ADAPTER_SCALE),
        )

        def factor_load(index):
            source, stage, _, _ = factors[index]
            return pltpu.make_async_copy(source, stage, f_s.at[index])

        def factor_over(index, layer):
            place = norms.at[layer] if index == 8 else factors[index][2].at[layer]
            return to_other(place, place, c_ss.at[index], c_rs.at[index])

        def factors_give():
            norms[s, 0:2, :] = gain_in[...]
            norms[s, 2:4, :] = bias_in[...]
            factor_over(8, s).start()
            for index, (_, stage, place, scale) in enumerate(factors):
                factor_load(index).wait()
                v = stage[...]
                place[s] = (v if scale == 1.0 else v * scale).astype(BF)
                factor_over(index, s).start()

        for index in range(8):
            factor_load(index).start()

        def across(c):
            return lax.rem(t + c, 2) + 2 * lax.rem(t // 2 + c // 2, 2)

        def block(i):
            return pl.ds(pl.multiple_of(i * R, R), R)

        def half(i, low):
            return pl.ds(pl.multiple_of(i * R + (B if low else 0), B), B)

        def rows_copy(buf, m, kind, ssem, rsem):
            if kind < 2:
                place = buf.at[m, block(t)]
            elif kind == 2:
                place = buf.at[m, half(across(1), False)]
            else:
                place = buf.at[m, half(across(2), True)]
            return pltpu.make_async_remote_copy(
                src_ref=place, dst_ref=place,
                send_sem=ssem.at[m * 4 + kind], recv_sem=rsem.at[m * 4 + kind],
                device_id={"tensor": across((1, 2, 2, 1)[kind])}, device_id_type=MESH,
            )

        def rows_wait(buf, m, kind, ssem, rsem):
            if kind < 2:
                place = buf.at[m, block(across(1 + kind))]
            else:
                place = buf.at[m, half(across(3), kind == 3)]
            pltpu.make_async_remote_copy(
                src_ref=place, dst_ref=place,
                send_sem=ssem.at[m * 4 + kind], recv_sem=rsem.at[m * 4 + kind],
                device_id={"tensor": across(1)}, device_id_type=MESH,
            ).wait_recv()

        def rows_start(buf, m, ssem, rsem):
            for kind in range(2):
                rows_copy(buf, m, kind, ssem, rsem).start()

        def rows_next(buf, m, c, ssem, rsem):
            @pl.when(c == 1)
            def _():
                for kind in range(2):
                    rows_wait(buf, m, kind, ssem, rsem)
                    rows_copy(buf, m, 2 + kind, ssem, rsem).start()

            @pl.when(c == 3)
            def _():
                for kind in range(2, 4):
                    rows_wait(buf, m, kind, ssem, rsem)

        def rows_sent(buf, m, ssem, rsem):
            for kind in range(4):
                rows_copy(buf, m, kind, ssem, rsem).wait_send()

        def to_peer(axis, size, me, k, src, dst, ssem, rsem):
            return pltpu.make_async_remote_copy(
                src_ref=src, dst_ref=dst, send_sem=ssem, recv_sem=rsem,
                device_id={axis: lax.rem(me + k, size)}, device_id_type=MESH,
            )

        def block_copy(phase, kind):
            place = (
                sbuf.at[across(1), 0:B], sbuf.at[across(3), 0:B],
                sbuf.at[across(2), B:R], sbuf.at[across(3), B:R],
                sbuf.at[across(2), 0:B], sbuf.at[across(1), B:R],
            )[kind]
            return pltpu.make_async_remote_copy(
                src_ref=place, dst_ref=rbuf.at[lax.rem(phase, 2) * 6 + kind],
                send_sem=r_ss.at[kind], recv_sem=r_rs.at[phase * 6 + kind],
                device_id={"tensor": across((1, 1, 2, 2, 2, 1)[kind])}, device_id_type=MESH,
            )

        def blocks_next(phase, c):
            @pl.when(c == 3)
            def _():
                block_copy(phase, 1).start()
                block_copy(phase, 3).start()

            @pl.when(c == 2)
            def _():
                block_copy(phase, 2).start()

            @pl.when(c == 1)
            def _():
                block_copy(phase, 0).start()
                block_copy(phase, 1).wait_recv()
                place = across(2)
                sbuf[place, 0:B] = (
                    sbuf[place, 0:B].astype(F32) + rbuf[lax.rem(phase, 2) * 6 + 1].astype(F32)
                ).astype(BF)
                block_copy(phase, 4).start()
                block_copy(phase, 3).wait_recv()
                place = across(1)
                sbuf[place, B:R] = (
                    sbuf[place, B:R].astype(F32) + rbuf[lax.rem(phase, 2) * 6 + 3].astype(F32)
                ).astype(BF)
                block_copy(phase, 5).start()

        def block_sum(phase, low):
            base = lax.rem(phase, 2) * 6
            if low:
                own, first, second = sbuf[t, B:R], rbuf[base + 2], rbuf[base + 5]
            else:
                own, first, second = sbuf[t, 0:B], rbuf[base], rbuf[base + 4]
            return own.astype(F32) + (first.astype(F32) + second.astype(F32))

        def blocks_arrive(phase):
            for kind in (0, 2, 4, 5):
                block_copy(phase, kind).wait_recv()

        def blocks_sent(phase):
            for kind in range(6):
                block_copy(phase, kind).wait_send()

        def rows_out(src, out, layer, index):
            class Out:
                def start(self):
                    @pl.when(s == layer)
                    def _():
                        local_copy(src, out.at[s], 3 + index).start()

                    @pl.when(s != layer)
                    def _():
                        to_other(src, out.at[s], c_ss.at[9 + index], c_rs.at[9 + index]).start()

                def sent(self):
                    @pl.when(s == layer)
                    def _():
                        local_copy(src, out.at[s], 3 + index).wait()

                    @pl.when(s != layer)
                    def _():
                        to_other(src, out.at[s], c_ss.at[9 + index], c_rs.at[9 + index]).wait_send()

                def arrive(self):
                    @pl.when(s == layer)
                    def _():
                        to_other(src, out.at[other], c_ss.at[9 + index], c_rs.at[9 + index]).wait_recv()

            return Out()

        def act_out(layer):
            return rows_out(yw if layer else xw.at[1], act, layer, layer)

        def ig_out(layer):
            return rows_out(yw, ig, layer, 2 + layer)

        def local_copy(src, dst, index):
            return pltpu.make_async_copy(src, dst, l_s.at[index])

        def norm_parts(x):
            mean = jnp.mean(x, axis=-1, keepdims=True)
            centred = x - mean
            spread = jnp.mean(centred * centred, axis=-1, keepdims=True)
            rstd = lax.rsqrt(spread + EPSILON)
            return centred * rstd, rstd

        def send_normed(layer):
            xhat, _ = norm_parts(xw[layer])
            xh[layer, block(t)] = xhat.astype(BF)
            rows_start(xh, layer, x_ss, x_rs)

        lane = lax.broadcasted_iota(jnp.int32, (R, 128), 1)
        in_first = lax.rem(lane, HEAD) < ROT // 2
        head_low = lane < HEAD

        def turn(v, cosine, sine):
            swapped = jnp.where(in_first, pltpu.roll(v, 128 - ROT // 2, 1), pltpu.roll(v, ROT // 2, 1))
            return v * cosine + swapped * sine

        def rope_of(chunk):
            again = jnp.where(chunk * R >= HALF, chunk * R - HALF, chunk * R)
            plain = rope[pl.ds(pl.multiple_of(chunk * R, R), R), :]
            restarted = rope[pl.ds(pl.multiple_of(again, R), R), :]
            table = jnp.where(split[s] > 0, restarted, plain)
            crossed = pltpu.roll(table, HEAD, 1)
            return jnp.where(head_low, table, crossed), jnp.where(head_low, crossed, table)

        def head_part(v, hh):
            zero = jnp.zeros_like(v)
            return jnp.where(head_low, v, zero) if hh == 0 else jnp.where(head_low, zero, v)

        causal = lax.broadcasted_iota(jnp.int32, (R, R), 0) <= lax.broadcasted_iota(
            jnp.int32, (R, R), 1
        )

        def scores_t(m, p, i, j, q):
            keys = kp[m * PAIRS + p, j * R:(j + 1) * R, :]
            sc = nt(keys, q)
            if j == i:
                sc = jnp.where(causal, sc, MASKED)
            if i * R >= HALF and j * R < HALF:
                sc = sc + MASKED * split[s].astype(F32)
            return sc

        loads = [local_copy(x_in.at[s], xw.at[0], 0), local_copy(ct_in.at[s], yw, 1)]
        for copy in loads:
            copy.start()

        @pl.when(s == 0)
        def _():
            weights_start((0, 1))

        loads[0].wait()
        send_normed(0)
        loads[1].wait()
        dz[1, block(t)] = yw[...].astype(BF)
        rows_start(dz, 1, z_ss, z_rs)
        factors_give()
        gb[...] = jnp.zeros_like(gb)

        @pl.when(s == 0)
        def _():
            weights_pass((0, 1), 0, DP - 2)
            weights_start((2, 3))
            weights_pass((0, 1), DP - 2, DP - 1)

        for index in range(9):
            factor_over(index, other).wait_recv()
        for index in range(4):
            weight_local(index).wait()

        def gain_of(layer, j, cols=slice(None)):
            return norms[layer, j:j + 1, cols]

        def bias_of(layer, j):
            return norms[layer, 2 + j:3 + j, :]

        def normed_to_hidden(m):
            @pl.when(s != m)
            def _():
                weights_from_other((0, 1), m)

            @pl.when(m > 0)
            def _():
                local_copy(hw, h_hbm, 1).wait()
                local_copy(dg, dg_hbm, 2).wait()

            def chunk(c, carry):
                src = across(c)
                rows_next(xh, m, c, x_ss, x_rs)

                @pl.when(jnp.logical_and(c == 2, s == m))
                def _():
                    weights_hop((2, 3), 0)

                rows = block(src)
                xhc = xh[m, rows, :].astype(F32)
                n1 = (xhc * gain_of(m, 0) + bias_of(m, 0)).astype(BF)
                n2 = (xhc * gain_of(m, 1) + bias_of(m, 1)).astype(BF)
                t1 = nn(n1, aq[m]).astype(BF)
                t2 = nn(n2, au[m]).astype(BF)
                t12t[m, 0:RANK, rows] = t1.T
                t12t[m, RANK:2 * RANK, rows] = t2.T
                cosine, sine = rope_of(src)
                for part in range(3):
                    cols = slice(part * QC, (part + 1) * QC)
                    val = nn(n1, wq[m, :, cols]) + nn(t1, bq[m, :, cols])
                    if part == 2:
                        vb = val.astype(BF)
                        for p in range(PAIRS):
                            vp[m * PAIRS + p, rows, :] = vb[:, p * 128:(p + 1) * 128]
                        vT[:, rows] = vb.T
                    else:
                        for p in range(PAIRS):
                            v = turn(val[:, p * 128:(p + 1) * 128], cosine, sine)
                            if part == 0:
                                qp[m * PAIRS + p, rows, :] = (v * 0.125).astype(BF)
                            else:
                                vb = v.astype(BF)
                                kp[m * PAIRS + p, rows, :] = vb
                                kT[m, p * 128:(p + 1) * 128, rows] = vb.T
                for n0 in range(0, FFL, TILE):
                    cols = slice(n0, n0 + TILE)
                    u = nn(n2, wup[m, :, cols]) + nn(t2, bu[m, :, cols])
                    phi = 0.5 * (1.0 + lax.erf(u * 0.7071067811865476))
                    hw[rows, cols] = (u * phi).astype(BF)
                    dg[rows, cols] = (
                        phi + u * (0.3989422804014327 * jnp.exp(-0.5 * u * u))
                    ).astype(BF)
                return carry

            lax.fori_loop(0, T, chunk, 0)
            @pl.when(m == 0)
            def _():
                local_copy(hw, h_hbm, 1).start()
                local_copy(dg, dg_hbm, 2).start()

        def attend(m):
            for i in range(T):
                icols = slice(i * R, (i + 1) * R)

                def pair(p, carry, i=i, icols=icols):
                    for hh in range(2):
                        h = 2 * p + hh
                        q = head_part(qp[m * PAIRS + p, icols, :], hh)
                        hrows = pl.ds(pl.multiple_of(h * HEAD, HEAD), HEAD)
                        blocks = [scores_t(m, p, i, j, q) for j in range(i + 1)]
                        top = functools.reduce(
                            jnp.maximum, [jnp.max(b, axis=0, keepdims=True) for b in blocks]
                        )
                        total = jnp.zeros_like(top)
                        acc = jnp.zeros((HEAD, R), F32)
                        for j in range(i + 1):
                            e = jnp.exp(blocks[j] - top)
                            total = total + jnp.sum(e, axis=0, keepdims=True)
                            acc = acc + nn(vT[hrows, j * R:(j + 1) * R], e.astype(BF))
                        oT[m, hrows, icols] = (acc * (1.0 / total)).astype(BF)
                        lse[pl.ds(m * HEADS + h, 1), icols] = top + jnp.log(total)
                    return carry

                lax.fori_loop(0, PAIRS, pair, 0)

        def project(m):
            @pl.when(s != m)
            def _():
                weights_from_other((2, 3), m)

            def step(n, carry):
                c = T - 1 - n
                i = across(c)
                rows = block(i)
                o = oT[m, :, rows].T
                hrow = hw[rows, :]
                to = nn(o, ao[m]).astype(BF)
                td = nn(hrow, ad[m]).astype(BF)
                todt[m, 0:RANK, rows] = to.T
                todt[m, RANK:2 * RANK, rows] = td.T
                for n0 in range(0, D, TILE):
                    cols = slice(n0, n0 + TILE)
                    sbuf[i, :, cols] = (
                        nt(o, wout[m, cols, :]) + nt(hrow, wdn[m, cols, :])
                        + nn(to, bo[m, :, cols]) + nn(td, bd[m, :, cols])
                    ).astype(BF)
                blocks_next(m, c)
                return carry

            lax.fori_loop(0, T, step, 0)

        def finish_forward(m):
            blocks_arrive(m)
            for low in range(2):
                rows = slice(low * B, (low + 1) * B)
                y = xw[m, rows, :] + block_sum(m, low)

                @pl.when(m == 0)
                def _(y=y, rows=rows):
                    xw[1, rows, :] = y

                @pl.when(m == 1)
                def _(y=y, rows=rows):
                    yw[rows, :] = y

            @pl.when(m == 0)
            def _():
                send_normed(1)
                act_out(0).start()

            @pl.when(m == 1)
            def _():
                act_out(1).start()

            rows_sent(xh, m, x_ss, x_rs)
            blocks_sent(m)

        def forward(m, carry):
            normed_to_hidden(m)

            @pl.when(s == m)
            def _():
                weights_pass((2, 3), 1, DP - 2)

            attend(m)

            @pl.when(s == m)
            def _():
                weights_pass((2, 3), max(1, DP - 2), DP - 1)
                weights_sent()

            @pl.when(jnp.logical_and(s == 0, m == 0))
            def _():
                pl.semaphore_signal(go, inc=1, device_id={"section": other}, device_id_type=MESH)

            @pl.when(jnp.logical_and(s == 1, m == 0))
            def _():
                pl.semaphore_wait(go, 1)
                weights_start((0, 1))

            project(m)

            @pl.when(jnp.logical_and(s == 1, m == 0))
            def _():
                weights_pass((0, 1), 0, DP - 2)
                weights_start((2, 3))

            finish_forward(m)

            @pl.when(jnp.logical_and(s == 1, m == 0))
            def _():
                weights_pass((0, 1), DP - 2, DP - 1)
            return carry

        lax.fori_loop(0, 2, forward, 0)

        def gradient_to_hidden(m):
            @pl.when(m == 0)
            def _():
                local_copy(dg_hbm, dg, 2).wait()

            def chunk(c, carry):
                src = across(c)
                rows_next(dz, m, c, z_ss, z_rs)
                rows = block(src)
                full = dz[m, rows, :]
                eo = nt(full, bo[m]).astype(BF)
                ed = nt(full, bd[m]).astype(BF)
                edot[0:RANK, rows] = eo.T
                edot[RANK:2 * RANK, rows] = ed.T
                do = nt(eo, ao[m]) + nn(full, wout[m])
                dob = do.astype(BF)
                for p in range(PAIRS):
                    v = dob[:, p * 128:(p + 1) * 128]
                    dop[p, rows, :] = v
                prod = dob.T.astype(F32) * oT[m, :, rows].astype(F32)
                for h in range(HEADS):
                    delta[h:h + 1, rows] = jnp.sum(
                        prod[h * HEAD:(h + 1) * HEAD], axis=0, keepdims=True
                    )
                for n0 in range(0, FFL, TILE):
                    cols = slice(n0, n0 + TILE)
                    v = nt(ed, ad[m, cols, :]) + nn(full, wdn[m, :, cols])
                    dg[rows, cols] = (v * dg[rows, cols].astype(F32)).astype(BF)
                return carry

            lax.fori_loop(0, T, chunk, 0)

        def attention_back(m):
            dk[...] = jnp.zeros_like(dk)
            dv[...] = jnp.zeros_like(dv)
            for i in range(T):
                icols = slice(i * R, (i + 1) * R)

                def pair(p, carry, i=i, icols=icols):
                    for hh in range(2):
                        h = 2 * p + hh
                        q = head_part(qp[m * PAIRS + p, icols, :], hh)
                        do = head_part(dop[p, icols, :], hh)
                        hrows = pl.ds(pl.multiple_of(h * HEAD, HEAD), HEAD)
                        low = lse[pl.ds(m * HEADS + h, 1), icols]
                        dlt = delta[pl.ds(h, 1), icols]
                        acc = jnp.zeros((HEAD, R), F32)
                        for j in range(i + 1):
                            jrows = slice(j * R, (j + 1) * R)
                            prob = jnp.exp(scores_t(m, p, i, j, q) - low)
                            dp_t = nt(vp[m * PAIRS + p, jrows, :], do)
                            ds_t = (prob * (dp_t - dlt)).astype(BF)
                            dv[p, jrows, :] += nn(prob.astype(BF), do)
                            dk[p, jrows, :] += nn(ds_t, q)
                            acc = acc + nn(kT[m, hrows, jrows], ds_t)
                        dqt[hrows, icols] = acc
                    return carry

                lax.fori_loop(0, PAIRS, pair, 0)

        def turn_back(m):
            def step(i, carry):
                rows = block(i)
                cosine, sine = rope_of(i)
                sine = -sine
                dq = dqt[:, rows].T * 0.125
                for p in range(PAIRS):
                    lanes = slice(p * 128, (p + 1) * 128)
                    dqkv[rows, p * 128:(p + 1) * 128] = turn(dq[:, lanes], cosine, sine).astype(BF)
                    dqkv[rows, QC + p * 128:QC + (p + 1) * 128] = turn(
                        dk[p, rows, :], cosine, sine
                    ).astype(BF)
                    dqkv[rows, 2 * QC + p * 128:2 * QC + (p + 1) * 128] = dv[p, rows, :].astype(BF)
                dop[0, rows, :] = nt(dqkv[rows, :], bq[m]).astype(BF)
                dop[1, rows, :] = nt(dg[rows, :], bu[m]).astype(BF)
                return carry

            lax.fori_loop(0, T, step, 0)

        def project_back(m):
            def tail(n, carry):
                c = T - 1 - n
                i = across(c)
                rows = block(i)
                dj = dqkv[rows, :]
                du = dg[rows, :]
                e1 = dop[0, rows, :]
                e2 = dop[1, rows, :]
                for n0 in range(0, D, TILE):
                    cols = slice(n0, n0 + TILE)
                    dn1 = nt(dj, wq[m, cols, :]) + nt(e1, aq[m, cols, :])
                    dn2 = nt(du, wup[m, cols, :]) + nt(e2, au[m, cols, :])
                    xhc = xh[m, rows, cols].astype(F32)
                    gb[0:1, cols] += jnp.sum(dn1 * xhc, axis=0, keepdims=True)
                    gb[1:2, cols] += jnp.sum(dn2 * xhc, axis=0, keepdims=True)
                    gb[2:3, cols] += jnp.sum(dn1, axis=0, keepdims=True)
                    gb[3:4, cols] += jnp.sum(dn2, axis=0, keepdims=True)
                    sbuf[i, :, cols] = (dn1 * gain_of(m, 0, cols) + dn2 * gain_of(m, 1, cols)).astype(BF)
                blocks_next(3 - m, c)
                return carry

            lax.fori_loop(0, T, tail, 0)

            @pl.when(m == 1)
            def _():
                act_out(1).sent()
                local_copy(ct_in.at[s], yw, 0).start()

        def put(buf, base, width, col, value):
            lo = 0
            while lo < value.shape[1]:
                j, at = divmod(col + lo, width)
                n = min(width - at, value.shape[1] - lo)
                buf[base + j, :, at:at + n] = value[:, lo:lo + n].astype(BF)
                lo += n

        def factor_gradients(m):
            put(pa, 0, PW, 0, ADAPTER_SCALE * nn(t12t[m, 0:RANK, :], dqkv[...]))
            put(pa, 0, PW, 3 * QC, ADAPTER_SCALE * nn(t12t[m, RANK:2 * RANK, :], dg[...]))
            put(pa, 0, PW, 3 * QC + FFL, nt(edot[0:RANK, :], oT[m]))
            put(pa, 0, PW, 4 * QC + FFL, nn(edot[RANK:2 * RANK, :], hw[...]))
            if NA * PW > GA:
                put(pa, 0, PW, GA, jnp.zeros((RANK, NA * PW - GA), F32))
            put(pt, 0, GRW, 2 * D, ADAPTER_SCALE * nn(todt[m, 0:RANK, :], dz[m]))
            put(pt, 0, GRW, 3 * D, ADAPTER_SCALE * nn(todt[m, RANK:2 * RANK, :], dz[m]))
            acc[...] = jnp.zeros_like(acc)

            def step(i, carry):
                rows = block(i)
                xhc = xh[m, rows, :].astype(F32)
                n1 = (xhc * gain_of(m, 0) + bias_of(m, 0)).astype(BF)
                acc[0:RANK, :] += nn(dop[0, rows, :].T, n1)
                n2 = (xhc * gain_of(m, 1) + bias_of(m, 1)).astype(BF)
                acc[RANK:2 * RANK, :] += nn(dop[1, rows, :].T, n2)
                return carry

            lax.fori_loop(0, T, step, 0)
            put(pt, 0, GRW, 0, acc[0:RANK, :])
            put(pt, 0, GRW, D, acc[RANK:2 * RANK, :])

        def finish_backward(m):
            @pl.when(m == 1)
            def _():
                local_copy(ct_in.at[s], yw, 0).wait()

            @pl.when(m == 0)
            def _():
                ig_out(1).sent()

            blocks_arrive(3 - m)
            for low in range(2):
                rows = slice(low * B, (low + 1) * B)
                xhat, rstd = norm_parts(xw[m, rows, :])
                g = block_sum(3 - m, low)
                mean_g = jnp.mean(g, axis=1, keepdims=True)
                mean_gx = jnp.mean(g * xhat, axis=1, keepdims=True)
                v = yw[rows, :] + (g - mean_g - xhat * mean_gx) * rstd
                yw[rows, :] = v

                @pl.when(m == 1)
                def _(v=v, low=low):
                    dz[0, half(t, low == 1)] = v.astype(BF)

            @pl.when(m == 1)
            def _():
                rows_start(dz, 0, z_ss, z_rs)
                ig_out(1).start()

            @pl.when(m == 0)
            def _():
                ig_out(0).start()

            rows_sent(dz, m, z_ss, z_rs)
            blocks_sent(3 - m)

        def guarded(full, condition, action):
            if full:
                action()
            else:
                pl.when(condition)(action)

        class Exchange:
            def __init__(self, index, k, pieces, gather, source, landing):
                self.args = index, k, source, landing
                self.full = pieces >= DP
                to, come = lax.rem(d + k, DP), lax.rem(d - k + DP, DP)
                self.sends = d < pieces if gather else to < pieces
                self.hears = come < pieces if gather else d < pieces

            def copy(self):
                index, k, source, landing = self.args
                return to_peer("dp", DP, d, k, source(lax.rem(d + k, DP)), landing(k - 1),
                               ad_ss.at[index, k - 1], ad_rs.at[index, k - 1])

            def start(self):
                guarded(self.full, self.sends, lambda: self.copy().start())

            def wait_send(self):
                guarded(self.full, self.sends, lambda: self.copy().wait_send())

            def wait_recv(self):
                guarded(self.full, self.hears, lambda: self.copy().wait_recv())

        def over_dp(index, source, landing, pieces=DP, gather=False):
            for k in range(1, DP):
                yield Exchange(index, k, pieces, gather, source, landing)

        def over_tensor(index, source, landing):
            for k in range(1, T):
                yield to_peer("tensor", T, t, k, source(lax.rem(t + k, T)), landing(k - 1),
                              at_ss.at[index, k - 1], at_rs.at[index, k - 1])

        def pa_scatter():
            return over_dp(0, lambda j: pa.at[j], lambda k: pa_in.at[k], NA)

        def ga_place(owner):
            return ga_out.at[:, pl.ds(pl.multiple_of(owner * PW, 128), PW)]

        def pa_gather():
            return over_dp(1, lambda j: pa_sum, lambda k: ga_place(d), NA, True)

        def pb_scatter(part):
            return over_dp(
                2 + part, lambda j: pb.at[part * NB + j], lambda k: pb_in.at[part * (DP - 1) + k], NB
            )

        def pb_gather(part):
            return over_dp(
                4 + part, lambda j: pb_all.at[part * NB + d], lambda k: pb_all.at[part * NB + d], NB, True
            )

        def pt_scatter(part):
            return over_tensor(part, lambda j: pt.at[part * T + j], lambda k: pt_in.at[part * (T - 1) + k])

        def pt_gather(part):
            return over_tensor(2 + part, lambda j: pt.at[part * T + t], lambda k: gr_place(part, t))

        def gb_tensor():
            return over_tensor(4, lambda j: gb, lambda k: gb_t.at[k])

        def gb_dp():
            return over_dp(6, lambda j: gb_sum, lambda k: gb_d.at[k])

        def pb_gathered(part):
            for k in range(1, DP):
                owner = lax.rem(d - k + DP, DP)

                def wait(k=k, owner=owner):
                    place = pb_all.at[part * NB + owner]
                    to_peer("dp", DP, d, k, place, place,
                            ad_ss.at[4 + part, k - 1], ad_rs.at[4 + part, k - 1]).wait_recv()

                guarded(NB >= DP, owner < NB, wait)

        def start_all(copies):
            for copy in copies:
                copy.start()

        def arrive_all(copies):
            for copy in copies:
                copy.wait_recv()

        def sent_all(copies):
            for copy in copies:
                copy.wait_send()

        def fill(buf, base, value, width):
            put(buf, base, width, 0, value)
            spare = -value.shape[1] % width
            if spare > 0:
                put(buf, base, width, value.shape[1], jnp.zeros((RANK, spare), F32))

        def pt_to_pb(part):
            arrive_all(pt_scatter(part))
            v = pt[part * T + t].astype(F32)
            for k in range(T - 1):
                v = v + pt_in[part * (T - 1) + k].astype(F32)
            fill(pb, part * NB, v, SW)
            start_all(pb_scatter(part))

        def pb_add(part):
            arrive_all(pb_scatter(part))

            def add():
                v = pb[part * NB + d].astype(F32)
                for k in range(DP - 1):
                    v = v + pb_in[part * (DP - 1) + k].astype(F32)
                pb_all[part * NB + d] = v.astype(BF)

            guarded(NB >= DP, d < NB, add)
            start_all(pb_gather(part))

        def pb_to_pt(part):
            pb_gathered(part)
            for j in range(NB):
                lo, hi = j * SW, min((j + 1) * SW, GRW)
                pt[part * T + t, :, lo:hi] = pb_all[part * NB + j, :, 0:hi - lo]
            start_all(pt_gather(part))

        def gr_place(part, owner):
            return gr_out.at[:, pl.ds(pl.multiple_of(part * 2 * D + owner * GRW, 128), GRW)]

        def parts_over():
            yield to_other(pt, pt_x, c_ss.at[13], c_rs.at[13])
            yield to_other(pa, pa_x, c_ss.at[14], c_rs.at[14])

        def gb_over():
            return to_other(gb, gb_x, c_ss.at[15], c_rs.at[15])

        def sums_start():
            arrive_all(parts_over())
            for j in range(2 * T):
                pt[j] = (pt[j].astype(F32) + pt_x[j].astype(F32)).astype(BF)
            for part in range(2):
                start_all(pt_scatter(part))
            for j in range(NA):
                pa[j] = (pa[j].astype(F32) + pa_x[j].astype(F32)).astype(BF)
            start_all(pa_scatter())

        def sums_next():
            gb_over().wait_recv()
            gb[...] = gb[...] + gb_x[...]
            start_all(gb_tensor())
            for part in range(2):
                pt_to_pb(part)
            arrive_all(pa_scatter())

            def add():
                v = pa[d].astype(F32)
                for k in range(DP - 1):
                    v = v + pa_in[k].astype(F32)
                pa_sum[...] = v.astype(BF)

            guarded(NA >= DP, d < NA, add)
            start_all(pa_gather())

        def ga_store():
            return pltpu.make_async_copy(pa_sum, ga_place(d), f_s.at[0])

        def gr_store(part):
            return pltpu.make_async_copy(pt.at[part * T + t], gr_place(part, t), f_s.at[1 + part])

        def gb_store():
            return pltpu.make_async_copy(gb, gb_out, f_s.at[3])

        def sums_add():
            for part in range(2):
                pb_add(part)
            arrive_all(gb_tensor())
            total = gb[...]
            for k in range(T - 1):
                total = total + gb_t[k]
            gb_sum[...] = total
            start_all(gb_dp())
            guarded(NA >= DP, d < NA, lambda: ga_store().start())

        def sums_spread():
            for part in range(2):
                pb_to_pt(part)
                gr_store(part).start()
            arrive_all(gb_dp())
            sent_all(gb_tensor())
            total = gb_sum[...]
            for k in range(DP - 1):
                total = total + gb_d[k]
            gb[...] = total
            gb_store().start()

        def sums_end():
            for copies in (pa_gather(), pt_gather(0), pt_gather(1)):
                arrive_all(copies)
            for copies in (pa_scatter(), pa_gather(), gb_dp(), pt_scatter(0), pt_scatter(1),
                           pt_gather(0), pt_gather(1), pb_scatter(0), pb_scatter(1),
                           pb_gather(0), pb_gather(1)):
                sent_all(copies)
            guarded(NA >= DP, d < NA, lambda: ga_store().wait())
            for part in range(2):
                gr_store(part).wait()
            gb_store().wait()

        gradient_to_hidden(1)
        attention_back(1)
        turn_back(1)
        project_back(1)
        factor_gradients(1)
        local_copy(h_hbm, hw, 1).start()
        local_copy(dg_hbm, dg, 2).start()

        @pl.when(s == 0)
        def _():
            start_all(parts_over())
            gb_over().start()

        finish_backward(1)

        @pl.when(s == 1)
        def _():
            sums_start()

        gradient_to_hidden(0)

        @pl.when(s == 1)
        def _():
            sums_next()

        attention_back(0)

        @pl.when(s == 1)
        def _():
            sums_add()

        turn_back(0)

        @pl.when(s == 0)
        def _():
            sent_all(parts_over())
            gb_over().wait_send()

        @pl.when(s == 1)
        def _():
            sums_spread()
            sums_end()

        gb[...] = jnp.zeros_like(gb)
        local_copy(h_hbm, hw, 1).wait()
        factor_gradients(0)

        @pl.when(s == 1)
        def _():
            start_all(parts_over())

        @pl.when(s == 0)
        def _():
            sums_start()

        project_back(0)

        @pl.when(s == 1)
        def _():
            gb_over().start()

        @pl.when(s == 0)
        def _():
            sums_next()

        finish_backward(0)

        @pl.when(s == 0)
        def _():
            sums_add()
            sums_spread()
            sums_end()

        @pl.when(s == 1)
        def _():
            sent_all(parts_over())
            gb_over().wait_send()

        ig_out(0).sent()
        act_out(0).sent()
        for layer in range(2):
            act_out(layer).arrive()
            ig_out(layer).arrive()
        for index in range(9):
            factor_over(index, s).wait_send()
        for index in range(4):
            for owner in range(DP):
                weight_over(index, s, owner, False).wait_send()

    any_spec = pl.BlockSpec(memory_space=pl.ANY)
    vmem_spec = pl.BlockSpec(memory_space=pltpu.VMEM)
    smem_spec = pl.BlockSpec(memory_space=pltpu.SMEM)
    shapes = jax.ShapeDtypeStruct
    return pl.pallas_call(
        kernel,
        out_shape=(
            shapes((M, R, D), F32), shapes((M, R, D), F32),
            shapes((RANK, NA * PW), BF), shapes((RANK, 4 * D), BF), shapes((8, D), F32),
            shapes((L, FFL), BF), shapes((L, FFL), BF),
        ),
        in_specs=[any_spec] * 14 + [vmem_spec] * 3 + [smem_spec],
        out_specs=(any_spec,) * 7,
        scratch_shapes=[
            pltpu.VMEM((2, D, RANK), BF), pltpu.VMEM((2, RANK, 3 * QC), BF),
            pltpu.VMEM((2, QC, RANK), BF), pltpu.VMEM((2, RANK, D), BF),
            pltpu.VMEM((2, D, RANK), BF), pltpu.VMEM((2, RANK, FFL), BF),
            pltpu.VMEM((2, FFL, RANK), BF), pltpu.VMEM((2, RANK, D), BF),
            pltpu.VMEM((2, 8, D), F32),
            pltpu.VMEM((2, D, 3 * QC), BF), pltpu.VMEM((2, D, FFL), BF),
            pltpu.VMEM((2, D, QC), BF), pltpu.VMEM((2, D, FFL), BF),
            pltpu.VMEM((M, L, D), BF),
            pltpu.VMEM((M, 2 * RANK, L), BF),
            pltpu.VMEM((M * PAIRS, L, 128), BF),
            pltpu.VMEM((M * PAIRS, L, 128), BF),
            pltpu.VMEM((M * PAIRS, L, 128), BF),
            pltpu.VMEM((M, QC, L), BF),
            pltpu.VMEM((QC, L), BF),
            pltpu.VMEM((M, QC, L), BF),
            pltpu.VMEM((M * HEADS, L), F32),
            pltpu.VMEM((L, FFL), BF),
            pltpu.VMEM((L, FFL), BF),
            pltpu.VMEM((M, 2 * RANK, L), BF),
            pltpu.VMEM((T, R, D), BF),
            pltpu.VMEM((2 * 6, B, D), BF),
            pltpu.VMEM((M, L, D), BF),
            pltpu.VMEM((PAIRS, L, 128), BF),
            pltpu.VMEM((8, L), F32),
            pltpu.VMEM((2 * RANK, L), BF),
            pltpu.VMEM((PAIRS, L, 128), F32),
            pltpu.VMEM((PAIRS, L, 128), F32),
            pltpu.VMEM((QC, L), F32),
            pltpu.VMEM((L, 3 * QC), BF),
            pltpu.VMEM((2 * RANK, D), F32),
            pltpu.VMEM((8, D), F32),
            pltpu.VMEM((M, R, D), F32),
            pltpu.VMEM((R, D), F32),
            pltpu.VMEM((NA, RANK, PW), BF),
            pltpu.VMEM((NA, RANK, PW), BF),
            pltpu.VMEM((DP - 1, RANK, PW), BF),
            pltpu.VMEM((RANK, PW), BF),
            pltpu.VMEM((2 * T, RANK, GRW), BF),
            pltpu.VMEM((2 * T, RANK, GRW), BF),
            pltpu.VMEM((2 * (T - 1), RANK, GRW), BF),
            pltpu.VMEM((2 * NB, RANK, SW), BF),
            pltpu.VMEM((2 * (DP - 1), RANK, SW), BF),
            pltpu.VMEM((2 * NB, RANK, SW), BF),
            pltpu.VMEM((8, D), F32),
            pltpu.VMEM((8, D), F32),
            pltpu.VMEM((T - 1, 8, D), F32),
            pltpu.VMEM((DP - 1, 8, D), F32),
            pltpu.SemaphoreType.DMA((4,)),
            pltpu.SemaphoreType.DMA((4, 2, DP)),
            pltpu.SemaphoreType.DMA((4, 2, DP)),
            pltpu.SemaphoreType.DMA((4, DP)),
            pltpu.SemaphoreType.DMA((4, DP)),
            pltpu.SemaphoreType.DMA((2 * 4,)),
            pltpu.SemaphoreType.DMA((2 * 4,)),
            pltpu.SemaphoreType.DMA((6,)),
            pltpu.SemaphoreType.DMA((4 * 6,)),
            pltpu.SemaphoreType.DMA((2 * 4,)),
            pltpu.SemaphoreType.DMA((2 * 4,)),
            pltpu.SemaphoreType.DMA((16,)),
            pltpu.SemaphoreType.DMA((16,)),
            pltpu.SemaphoreType.DMA((7,)),
            pltpu.SemaphoreType.DMA((8,)),
            pltpu.SemaphoreType.REGULAR,
            pltpu.SemaphoreType.DMA((5, T - 1)),
            pltpu.SemaphoreType.DMA((5, T - 1)),
            pltpu.SemaphoreType.DMA((7, DP - 1)),
            pltpu.SemaphoreType.DMA((7, DP - 1)),
        ],
        compiler_params=pltpu.CompilerParams(
            collective_id=0, has_side_effects=True, vmem_limit_bytes=63 * 2**20
        ),
    )


def rope_table(length):
    half = ROT // 2
    inverse = np.float32(10000.0) ** (-np.arange(half, dtype=np.float32) * np.float32(2.0 / ROT))
    angles = np.arange(length, dtype=np.float32)[:, None] * inverse[None, :]
    cosine, sine = np.cos(angles.astype(np.float64)), np.sin(angles.astype(np.float64))
    rest = np.zeros((length, HEAD - ROT))
    return np.concatenate(
        [cosine, cosine, rest + 1.0, -sine, sine, rest], axis=-1
    ).astype(np.float32)


def solution(mesh):
    T = mesh.shape["tensor"]
    DP = mesh.shape["dp"]

    def per_device(
        inputs, cotangent, split,
        query_key_value_weight, output_weight, up_weight, down_weight,
        qkv_adapter_input, qkv_adapter_output, out_adapter_input, out_adapter_output,
        up_adapter_input, up_adapter_output, down_adapter_input, down_adapter_output,
        ln_gain, ln_bias,
    ):
        M, R, D = inputs.shape
        QC = output_weight.shape[1]
        FFL = up_weight.shape[2]
        RANK = qkv_adapter_input.shape[2]
        L = R * T
        wq = query_key_value_weight[0].reshape(-1, 3 * QC)
        aq = qkv_adapter_input[0].astype(BF)
        bq = (ADAPTER_SCALE * qkv_adapter_output[0].reshape(RANK, -1)).astype(BF)
        ao = out_adapter_input[0].astype(BF)
        bo = (ADAPTER_SCALE * out_adapter_output[0]).astype(BF)
        au = up_adapter_input[0].astype(BF)
        bu = (ADAPTER_SCALE * up_adapter_output[0]).astype(BF)
        ad = down_adapter_input[0].astype(BF)
        bd = (ADAPTER_SCALE * down_adapter_output[0]).astype(BF)
        kernel = make_kernel(T, DP, M, R, D, QC, FFL, RANK)
        act, ig, ga, gr, gb, _, _ = kernel(
            inputs, cotangent, wq, up_weight[0], output_weight[0].T, down_weight[0].T,
            qkv_adapter_input[0], qkv_adapter_output[0].reshape(RANK, -1),
            out_adapter_input[0], out_adapter_output[0],
            up_adapter_input[0], up_adapter_output[0],
            down_adapter_input[0], down_adapter_output[0],
            ln_gain[0], ln_bias[0], jnp.asarray(rope_table(L)), split[:, 0],
        )
        ga = ga.astype(F32)
        gr = gr.astype(F32)
        cuts = [3 * QC, 3 * QC + FFL, 4 * QC + FFL, 4 * QC + 2 * FFL]
        b_qkv, b_up, a_out, a_down, _ = jnp.split(ga, cuts, axis=1)
        a_qkv, a_up, b_out, b_down = jnp.split(gr, 4, axis=1)

        dp_place = lax.axis_index("dp")
        DR = D // DP
        sl = lax.dynamic_slice_in_dim
        c_qkv = wq.astype(F32) + nn(sl(aq, dp_place * DR, DR, 0), bq)
        c_out = output_weight[0].astype(F32) + nn(ao, sl(bo, dp_place * DR, DR, 1))
        c_up = up_weight[0].astype(F32) + nn(sl(au, dp_place * DR, DR, 0), bu)
        c_down = down_weight[0].astype(F32) + nn(ad, sl(bd, dp_place * DR, DR, 1))
        return (
            act[None], ig[None],
            a_qkv.T[None], b_qkv.reshape(qkv_adapter_output.shape),
            a_out.T[None], b_out[None], a_up.T[None], b_up[None], a_down.T[None], b_down[None],
            gb[0:2][None], gb[2:4][None],
            c_qkv.reshape(query_key_value_weight.shape), c_out[None], c_up[None], c_down[None],
        )

    rows = P(None, ("dp", "tensor"), None)
    whole = P("section", None, None)
    in_specs = (
        rows, rows, P(None, "dp"),
        P("section", "dp", None, "tensor"), P("section", "tensor", "dp"),
        P("section", "dp", "tensor"), P("section", "tensor", "dp"),
        whole, P("section", None, None, "tensor"), P("section", "tensor", None), whole,
        whole, P("section", None, "tensor"), P("section", "tensor", None), whole,
        whole, whole,
    )
    layer_rows = P("section", None, ("dp", "tensor"), None)
    out_specs = (
        layer_rows, layer_rows,
        whole, P("section", None, None, "tensor"), P("section", "tensor", None), whole,
        whole, P("section", None, "tensor"), P("section", "tensor", None), whole,
        whole, whole,
        P("section", "dp", None, "tensor"), P("section", "tensor", "dp"),
        P("section", "dp", "tensor"), P("section", "tensor", "dp"),
    )
    return jax.shard_map(
        per_device, mesh=mesh, in_specs=in_specs, out_specs=out_specs, check_vma=False
    )
```

```python
import functools

import jax
import jax.numpy as jnp
import numpy as np
from jax import lax
from jax.experimental import pallas as pl
from jax.experimental.pallas import tpu as pltpu
from jax.sharding import PartitionSpec as P

HEAD = 64
ROT = 16
ADAPTER_SCALE = 0.25
EPSILON = 1e-05
MASKED = -1e30
BF = jnp.bfloat16
F32 = jnp.float32
MESH = pl.DeviceIdType.MESH


def nn(a, b):
    return lax.dot_general(a, b, (((1,), (0,)), ((), ())), preferred_element_type=F32)


def nt(a, b):
    return lax.dot_general(a, b, (((1,), (1,)), ((), ())), preferred_element_type=F32)


class Sizes:
    def __init__(self, T, DP, alone, both):
        self.alone, self.both = alone, both
        self.PW = -(-alone // (DP * 128)) * 128
        self.GRW = both // T
        self.SW = -(-self.GRW // (DP * 128)) * 128
        self.NA, self.NB = -(-alone // self.PW), -(-self.GRW // self.SW)


def group_sizes(T, DP, D, QC, FFL):
    return Sizes(T, DP, QC + 2 * FFL, 3 * D), Sizes(T, DP, 3 * QC, D)


def make_kernel(T, DP, M, R, D, QC, FFL, RANK):
    L = R * T
    DR = D // DP
    B = R // 2
    PAIRS = QC // 128
    HEADS = QC // HEAD
    TILE = 256
    HALF = L // 2
    EARLY, LATE = group_sizes(T, DP, D, QC, FFL)

    def kernel(
        x_in, ct_in, wq_in, wup_in, wout_in, wdn_in,
        aq_in, bq_in, ao_in, bo_in, au_in, bu_in, ad_in, bd_in, gain_in, bias_in, rope, split,
        act, ig, gb_out, h_hbm, dg_hbm, ga_early, gr_early, ga_late, gr_late,
        aq, bq, ao, bo, au, bu, ad, bd, norms, wout_raw, wdn_raw,
        wq, wup, wout, wdn, xh, t12t, qp, kp, vp, kT, vT, oT, lse, hw, dg,
        todt, sbuf, rbuf, dz, dop, delta, edot, dk, dv, dqt, dqkv,
        acc, gb, xw, yw, gb_x, gb_sum, gb_t, gb_d,
        pa_e, pa_x_e, pa_in_e, pa_sum_e, pt_e, pt_x_e, pt_in_e, pb_e, pb_in_e, pb_all_e,
        pa_l, pa_x_l, pa_in_l, pa_sum_l, pt_l, pt_x_l, pt_in_l, pb_l, pb_in_l, pb_all_l,
        w_ls, w_ss, w_rs, v_ss, v_rs, x_ss, x_rs, r_ss, r_rs, z_ss, z_rs, c_ss, c_rs, l_s, f_s,
        go, at_ss, at_rs, ad_ss, ad_rs,
    ):
        s = lax.axis_index("section")
        d = lax.axis_index("dp")
        t = lax.axis_index("tensor")
        other = 1 - s

        barrier = pltpu.get_barrier_semaphore()
        for k in range(1, T):
            pl.semaphore_signal(
                barrier, inc=1, device_id={"tensor": lax.rem(t + k, T)}, device_id_type=MESH
            )
        for k in range(1, DP):
            pl.semaphore_signal(
                barrier, inc=1, device_id={"dp": lax.rem(d + k, DP)}, device_id_type=MESH
            )
        pl.semaphore_signal(barrier, inc=1, device_id={"section": other}, device_id_type=MESH)
        pl.semaphore_wait(barrier, T + DP - 1)

        def to_other(src, dst, ssem, rsem):
            return pltpu.make_async_remote_copy(
                src_ref=src, dst_ref=dst, send_sem=ssem, recv_sem=rsem,
                device_id={"section": other}, device_id_type=MESH,
            )

        def gathered(index, layer, owner):
            return (wq, wup, wout, wdn)[index].at[layer, pl.ds(pl.multiple_of(owner * DR, DR), DR)]

        def weight_copy(index, way, hop, owner):
            place = gathered(index, s, owner)
            return pltpu.make_async_remote_copy(
                src_ref=place, dst_ref=place,
                send_sem=w_ss.at[index, way, hop], recv_sem=w_rs.at[index, way, hop],
                device_id={"dp": d + 1 if way == 0 else d - 1}, device_id_type=MESH,
            )

        def weight_over(index, layer, owner):
            place = gathered(index, layer, owner)
            return to_other(place, place, v_ss.at[index, owner], v_rs.at[index, owner])

        has_next = (d < DP - 1, d > 0)

        def holds(way, hop):
            return d >= hop + 1 if way == 0 else d + hop + 1 <= DP - 1

        def owner_of(way, hop):
            return d - hop - 1 if way == 0 else d + hop + 1

        def weight_local(index):
            place = gathered(index, s, d)
            if index == 0:
                return [
                    pltpu.make_async_copy(
                        wq_in.at[part], place.at[:, part * QC:(part + 1) * QC], w_ls.at[part]
                    )
                    for part in range(3)
                ]
            stage = (None, place, wout_raw, wdn_raw)[index]
            return [pltpu.make_async_copy((None, wup_in, wout_in, wdn_in)[index], stage, w_ls.at[2 + index])]

        def weights_own(indices):
            for index in indices:
                for copy in weight_local(index):
                    copy.wait()
                rows = pl.ds(pl.multiple_of(d * DR, DR), DR)
                if index == 2:
                    wout[s, rows, :] = wout_raw[...].T
                if index == 3:
                    wdn[s, rows, :] = wdn_raw[...].T

        def weights_start(indices):
            for index in indices:
                for way in range(2):
                    @pl.when(has_next[way])
                    def _(index=index, way=way):
                        weight_copy(index, way, 0, d).start()
                weight_over(index, s, d).start()

        def weights_hop(indices, hop):
            for index in indices:
                for way in range(2):
                    @pl.when(holds(way, hop))
                    def _(index=index, way=way):
                        owner = owner_of(way, hop)
                        weight_copy(index, way, hop, owner).wait_recv()

                        @pl.when(has_next[way])
                        def _():
                            weight_copy(index, way, hop + 1, owner).start()

                        weight_over(index, s, owner).start()

        def weights_pass(indices, first, last):
            if last > first:
                def step(hop, carry):
                    weights_hop(indices, hop)
                    return carry

                lax.fori_loop(first, last, step, 0)

        def weights_sent():
            for index in range(4):
                for way in range(2):
                    @pl.when(has_next[way])
                    def _(index=index, way=way):
                        weight_copy(index, way, 0, d).wait_send()

            def step(hop, carry):
                for index in range(4):
                    for way in range(2):
                        @pl.when(jnp.logical_and(has_next[way], holds(way, hop)))
                        def _(index=index, way=way):
                            weight_copy(index, way, hop + 1, owner_of(way, hop)).wait_send()
                return carry

            lax.fori_loop(0, DP - 1, step, 0)

        def weights_from_other(indices, layer):
            def step(owner, carry):
                for index in indices:
                    weight_over(index, layer, owner).wait_recv()
                return carry

            lax.fori_loop(0, DP, step, 0)

        for index in range(4):
            for copy in weight_local(index):
                copy.start()

        factors = (
            (aq_in, dk.at[0], aq, 1.0), (au_in, dk.at[1], au, 1.0),
            (ad_in, dv.at[0], ad, 1.0), (ao_in, dv.at[1, 0:QC], ao, 1.0),
            (None, xw.at[1, 0:RANK, 0:3 * QC], bq, ADAPTER_SCALE), (bu_in, xw.at[1, RANK:2 * RANK, 0:FFL], bu, ADAPTER_SCALE),
            (bo_in, dqt.at[0:RANK, 0:D], bo, ADAPTER_SCALE), (bd_in, dqt.at[RANK:2 * RANK, 0:D], bd, ADAPTER_SCALE),
        )

        def factor_load(index):
            source, stage, _, _ = factors[index]
            if index == 4:
                return [
                    pltpu.make_async_copy(
                        bq_in.at[part], xw.at[1, 0:RANK, part * QC:(part + 1) * QC], f_s.at[7 + part if part else 4]
                    )
                    for part in range(3)
                ]
            return [pltpu.make_async_copy(source, stage, f_s.at[index])]

        def factor_over(index, layer):
            place = norms.at[layer] if index == 8 else factors[index][2].at[layer]
            return to_other(place, place, c_ss.at[index], c_rs.at[index])

        def factors_give():
            norms[s, 0:2, :] = gain_in[...]
            norms[s, 2:4, :] = bias_in[...]
            factor_over(8, s).start()
            for index, (_, stage, place, scale) in enumerate(factors):
                for copy in factor_load(index):
                    copy.wait()
                v = stage[...]
                place[s] = (v if scale == 1.0 else v * scale).astype(BF)
                factor_over(index, s).start()

        for index in range(8):
            for copy in factor_load(index):
                copy.start()

        def across(c):
            return lax.rem(t + c, 2) + 2 * lax.rem(t // 2 + c // 2, 2)

        def block(i):
            return pl.ds(pl.multiple_of(i * R, R), R)

        def half(i, low):
            return pl.ds(pl.multiple_of(i * R + (B if low else 0), B), B)

        def rows_copy(buf, m, kind, ssem, rsem):
            if kind < 2:
                place = buf.at[m, block(t)]
            elif kind == 2:
                place = buf.at[m, half(across(1), False)]
            else:
                place = buf.at[m, half(across(2), True)]
            return pltpu.make_async_remote_copy(
                src_ref=place, dst_ref=place,
                send_sem=ssem.at[m * 4 + kind], recv_sem=rsem.at[m * 4 + kind],
                device_id={"tensor": across((1, 2, 2, 1)[kind])}, device_id_type=MESH,
            )

        def rows_wait(buf, m, kind, ssem, rsem):
            if kind < 2:
                place = buf.at[m, block(across(1 + kind))]
            else:
                place = buf.at[m, half(across(3), kind == 3)]
            pltpu.make_async_remote_copy(
                src_ref=place, dst_ref=place,
                send_sem=ssem.at[m * 4 + kind], recv_sem=rsem.at[m * 4 + kind],
                device_id={"tensor": across(1)}, device_id_type=MESH,
            ).wait_recv()

        def rows_start(buf, m, ssem, rsem):
            for kind in range(2):
                rows_copy(buf, m, kind, ssem, rsem).start()

        def rows_next(buf, m, c, ssem, rsem):
            @pl.when(c == 1)
            def _():
                for kind in range(2):
                    rows_wait(buf, m, kind, ssem, rsem)
                    rows_copy(buf, m, 2 + kind, ssem, rsem).start()

            @pl.when(c == 3)
            def _():
                for kind in range(2, 4):
                    rows_wait(buf, m, kind, ssem, rsem)

        def rows_sent(buf, m, ssem, rsem):
            for kind in range(4):
                rows_copy(buf, m, kind, ssem, rsem).wait_send()

        def to_peer(axis, size, me, k, src, dst, ssem, rsem):
            return pltpu.make_async_remote_copy(
                src_ref=src, dst_ref=dst, send_sem=ssem, recv_sem=rsem,
                device_id={axis: lax.rem(me + k, size)}, device_id_type=MESH,
            )

        def block_copy(phase, kind):
            place = (
                sbuf.at[across(1), 0:B], sbuf.at[across(3), 0:B],
                sbuf.at[across(2), B:R], sbuf.at[across(3), B:R],
                sbuf.at[across(2), 0:B], sbuf.at[across(1), B:R],
            )[kind]
            return pltpu.make_async_remote_copy(
                src_ref=place, dst_ref=rbuf.at[lax.rem(phase, 2) * 6 + kind],
                send_sem=r_ss.at[kind], recv_sem=r_rs.at[phase * 6 + kind],
                device_id={"tensor": across((1, 1, 2, 2, 2, 1)[kind])}, device_id_type=MESH,
            )

        def blocks_next(phase, c):
            @pl.when(c == 3)
            def _():
                block_copy(phase, 1).start()
                block_copy(phase, 3).start()

            @pl.when(c == 2)
            def _():
                block_copy(phase, 2).start()

            @pl.when(c == 1)
            def _():
                block_copy(phase, 0).start()
                block_copy(phase, 1).wait_recv()
                place = across(2)
                sbuf[place, 0:B] = (
                    sbuf[place, 0:B].astype(F32) + rbuf[lax.rem(phase, 2) * 6 + 1].astype(F32)
                ).astype(BF)
                block_copy(phase, 4).start()
                block_copy(phase, 3).wait_recv()
                place = across(1)
                sbuf[place, B:R] = (
                    sbuf[place, B:R].astype(F32) + rbuf[lax.rem(phase, 2) * 6 + 3].astype(F32)
                ).astype(BF)
                block_copy(phase, 5).start()

        def block_sum(phase, low):
            base = lax.rem(phase, 2) * 6
            if low:
                own, first, second = sbuf[t, B:R], rbuf[base + 2], rbuf[base + 5]
            else:
                own, first, second = sbuf[t, 0:B], rbuf[base], rbuf[base + 4]
            return own.astype(F32) + (first.astype(F32) + second.astype(F32))

        def blocks_arrive(phase):
            for kind in (0, 2, 4, 5):
                block_copy(phase, kind).wait_recv()

        def blocks_sent(phase):
            for kind in range(6):
                block_copy(phase, kind).wait_send()

        def rows_out(src, out, layer, index):
            class Out:
                def start(self):
                    @pl.when(s == layer)
                    def _():
                        local_copy(src, out.at[s], 3 + index).start()

                    @pl.when(s != layer)
                    def _():
                        to_other(src, out.at[s], c_ss.at[9 + index], c_rs.at[9 + index]).start()

                def sent(self):
                    @pl.when(s == layer)
                    def _():
                        local_copy(src, out.at[s], 3 + index).wait()

                    @pl.when(s != layer)
                    def _():
                        to_other(src, out.at[s], c_ss.at[9 + index], c_rs.at[9 + index]).wait_send()

                def arrive(self):
                    @pl.when(s == layer)
                    def _():
                        to_other(src, out.at[other], c_ss.at[9 + index], c_rs.at[9 + index]).wait_recv()

            return Out()

        def act_out(layer):
            return rows_out(yw if layer else xw.at[1], act, layer, layer)

        def ig_out(layer):
            return rows_out(yw, ig, layer, 2 + layer)

        def local_copy(src, dst, index):
            return pltpu.make_async_copy(src, dst, l_s.at[index])

        def norm_parts(x):
            mean = jnp.mean(x, axis=-1, keepdims=True)
            centred = x - mean
            spread = jnp.mean(centred * centred, axis=-1, keepdims=True)
            rstd = lax.rsqrt(spread + EPSILON)
            return centred * rstd, rstd

        def send_normed(layer):
            xhat, _ = norm_parts(xw[layer])
            xh[layer, block(t)] = xhat.astype(BF)
            rows_start(xh, layer, x_ss, x_rs)

        lane = lax.broadcasted_iota(jnp.int32, (R, 128), 1)
        in_first = lax.rem(lane, HEAD) < ROT // 2
        head_low = lane < HEAD

        def turn(v, cosine, sine):
            swapped = jnp.where(in_first, pltpu.roll(v, 128 - ROT // 2, 1), pltpu.roll(v, ROT // 2, 1))
            return v * cosine + swapped * sine

        def rope_of(chunk):
            again = jnp.where(chunk * R >= HALF, chunk * R - HALF, chunk * R)
            plain = rope[pl.ds(pl.multiple_of(chunk * R, R), R), :]
            restarted = rope[pl.ds(pl.multiple_of(again, R), R), :]
            table = jnp.where(split[s] > 0, restarted, plain)
            crossed = pltpu.roll(table, HEAD, 1)
            return jnp.where(head_low, table, crossed), jnp.where(head_low, crossed, table)

        def head_part(v, hh):
            zero = jnp.zeros_like(v)
            return jnp.where(head_low, v, zero) if hh == 0 else jnp.where(head_low, zero, v)

        causal = lax.broadcasted_iota(jnp.int32, (R, R), 0) <= lax.broadcasted_iota(
            jnp.int32, (R, R), 1
        )

        def scores_t(m, p, i, j, q):
            keys = kp[m * PAIRS + p, j * R:(j + 1) * R, :]
            sc = nt(keys, q)
            if j == i:
                sc = jnp.where(causal, sc, MASKED)
            if i * R >= HALF and j * R < HALF:
                sc = sc + MASKED * split[s].astype(F32)
            return sc

        loads = [local_copy(x_in.at[s], xw.at[0], 0), local_copy(ct_in.at[s], yw, 1)]
        for copy in loads:
            copy.start()

        weights_own((0, 1))

        @pl.when(s == 0)
        def _():
            weights_start((0, 1))

        loads[0].wait()
        send_normed(0)
        loads[1].wait()
        dz[1, block(t)] = yw[...].astype(BF)
        rows_start(dz, 1, z_ss, z_rs)
        factors_give()
        weights_own((2, 3))
        gb[...] = jnp.zeros_like(gb)

        @pl.when(s == 0)
        def _():
            weights_pass((0, 1), 0, DP - 2)
            weights_start((2, 3))
            weights_pass((0, 1), DP - 2, DP - 1)

        for index in range(9):
            factor_over(index, other).wait_recv()
        def gain_of(layer, j, cols=slice(None)):
            return norms[layer, j:j + 1, cols]

        def bias_of(layer, j):
            return norms[layer, 2 + j:3 + j, :]

        def normed_to_hidden(m):
            @pl.when(s != m)
            def _():
                weights_from_other((0, 1), m)

            @pl.when(m > 0)
            def _():
                local_copy(hw, h_hbm, 1).wait()
                local_copy(dg, dg_hbm, 2).wait()

            def chunk(c, carry):
                src = across(c)
                rows_next(xh, m, c, x_ss, x_rs)

                @pl.when(jnp.logical_and(c == 2, s == m))
                def _():
                    weights_hop((2, 3), 0)

                rows = block(src)
                xhc = xh[m, rows, :].astype(F32)
                n1 = (xhc * gain_of(m, 0) + bias_of(m, 0)).astype(BF)
                n2 = (xhc * gain_of(m, 1) + bias_of(m, 1)).astype(BF)
                t1 = nn(n1, aq[m]).astype(BF)
                t2 = nn(n2, au[m]).astype(BF)
                t12t[m, 0:RANK, rows] = t1.T
                t12t[m, RANK:2 * RANK, rows] = t2.T
                cosine, sine = rope_of(src)
                for part in range(3):
                    cols = slice(part * QC, (part + 1) * QC)
                    val = nn(n1, wq[m, :, cols]) + nn(t1, bq[m, :, cols])
                    if part == 2:
                        vb = val.astype(BF)
                        for p in range(PAIRS):
                            vp[m * PAIRS + p, rows, :] = vb[:, p * 128:(p + 1) * 128]
                        vT[:, rows] = vb.T
                    else:
                        for p in range(PAIRS):
                            v = turn(val[:, p * 128:(p + 1) * 128], cosine, sine)
                            if part == 0:
                                qp[m * PAIRS + p, rows, :] = (v * 0.125).astype(BF)
                            else:
                                vb = v.astype(BF)
                                kp[m * PAIRS + p, rows, :] = vb
                                kT[m, p * 128:(p + 1) * 128, rows] = vb.T
                for n0 in range(0, FFL, TILE):
                    cols = slice(n0, n0 + TILE)
                    u = nn(n2, wup[m, :, cols]) + nn(t2, bu[m, :, cols])
                    phi = 0.5 * (1.0 + lax.erf(u * 0.7071067811865476))
                    hw[rows, cols] = (u * phi).astype(BF)
                    dg[rows, cols] = (
                        phi + u * (0.3989422804014327 * jnp.exp(-0.5 * u * u))
                    ).astype(BF)
                return carry

            lax.fori_loop(0, T, chunk, 0)
            @pl.when(m == 0)
            def _():
                local_copy(hw, h_hbm, 1).start()
                local_copy(dg, dg_hbm, 2).start()

        def attend(m, i):
                icols = slice(i * R, (i + 1) * R)

                def pair(p, carry, i=i, icols=icols):
                    for hh in range(2):
                        h = 2 * p + hh
                        q = head_part(qp[m * PAIRS + p, icols, :], hh)
                        hrows = pl.ds(pl.multiple_of(h * HEAD, HEAD), HEAD)
                        blocks = [scores_t(m, p, i, j, q) for j in range(i + 1)]
                        top = functools.reduce(
                            jnp.maximum, [jnp.max(b, axis=0, keepdims=True) for b in blocks]
                        )
                        total = jnp.zeros_like(top)
                        acc = jnp.zeros((HEAD, R), F32)
                        for j in range(i + 1):
                            e = jnp.exp(blocks[j] - top)
                            total = total + jnp.sum(e, axis=0, keepdims=True)
                            acc = acc + nn(vT[hrows, j * R:(j + 1) * R], e.astype(BF))
                        oT[m, hrows, icols] = (acc * (1.0 / total)).astype(BF)
                        lse[pl.ds(m * HEADS + h, 1), icols] = top + jnp.log(total)
                    return carry

                lax.fori_loop(0, PAIRS, pair, 0)

        def project(m, c):
                i = across(c)
                rows = block(i)
                o = oT[m, :, rows].T
                hrow = hw[rows, :]
                to = nn(o, ao[m]).astype(BF)
                td = nn(hrow, ad[m]).astype(BF)
                todt[m, 0:RANK, rows] = to.T
                todt[m, RANK:2 * RANK, rows] = td.T
                for n0 in range(0, D, TILE):
                    cols = slice(n0, n0 + TILE)
                    sbuf[i, :, cols] = (
                        nt(o, wout[m, cols, :]) + nt(hrow, wdn[m, cols, :])
                        + nn(to, bo[m, :, cols]) + nn(td, bd[m, :, cols])
                    ).astype(BF)
                blocks_next(m, c)

        def attend_and_project(m):
            def step(n, carry):
                c = T - 1 - lax.rem(n, T)
                now = n // T
                for i in range(T):
                    @pl.when(jnp.logical_and(across(c) == i, now == m))
                    def _(i=i):
                        attend(m, i)

                @pl.when(n == T)
                def _():
                    last_weights(m)

                @pl.when(now == 1)
                def _():
                    project(m, c)
                return carry

            lax.fori_loop(0, 2 * T, step, 0)

        def finish_forward(m):
            blocks_arrive(m)
            for low in range(2):
                rows = slice(low * B, (low + 1) * B)
                y = xw[m, rows, :] + block_sum(m, low)

                @pl.when(m == 0)
                def _(y=y, rows=rows):
                    xw[1, rows, :] = y

                @pl.when(m == 1)
                def _(y=y, rows=rows):
                    yw[rows, :] = y

            @pl.when(m == 0)
            def _():
                send_normed(1)
                act_out(0).start()

            @pl.when(m == 1)
            def _():
                act_out(1).start()

            rows_sent(xh, m, x_ss, x_rs)
            blocks_sent(m)

        def last_weights(m):
            @pl.when(s == m)
            def _():
                weights_pass((2, 3), max(1, DP - 2), DP - 1)
                weights_sent()

            @pl.when(jnp.logical_and(s == 0, m == 0))
            def _():
                pl.semaphore_signal(go, inc=1, device_id={"section": other}, device_id_type=MESH)

            @pl.when(jnp.logical_and(s == 1, m == 0))
            def _():
                pl.semaphore_wait(go, 1)
                weights_start((0, 1))

            @pl.when(s != m)
            def _():
                weights_from_other((2, 3), m)

        def forward(m, carry):
            normed_to_hidden(m)

            @pl.when(s == m)
            def _():
                weights_pass((2, 3), 1, DP - 2)

            attend_and_project(m)

            @pl.when(jnp.logical_and(s == 1, m == 0))
            def _():
                weights_pass((0, 1), 0, DP - 2)
                weights_start((2, 3))

            finish_forward(m)

            @pl.when(jnp.logical_and(s == 1, m == 0))
            def _():
                weights_pass((0, 1), DP - 2, DP - 1)
            return carry

        lax.fori_loop(0, 2, forward, 0)

        def gradient_to_hidden(m, meanwhile):
            @pl.when(m == 0)
            def _():
                local_copy(dg_hbm, dg, 2).wait()

            def chunk(c, carry):
                src = across(c)
                meanwhile(c)
                rows_next(dz, m, c, z_ss, z_rs)
                rows = block(src)
                full = dz[m, rows, :]
                eo = nt(full, bo[m]).astype(BF)
                ed = nt(full, bd[m]).astype(BF)
                edot[0:RANK, rows] = eo.T
                edot[RANK:2 * RANK, rows] = ed.T
                do = nt(eo, ao[m]) + nn(full, wout[m])
                dob = do.astype(BF)
                for p in range(PAIRS):
                    v = dob[:, p * 128:(p + 1) * 128]
                    dop[p, rows, :] = v
                prod = dob.T.astype(F32) * oT[m, :, rows].astype(F32)
                for h in range(HEADS):
                    delta[h:h + 1, rows] = jnp.sum(
                        prod[h * HEAD:(h + 1) * HEAD], axis=0, keepdims=True
                    )
                for n0 in range(0, FFL, TILE):
                    cols = slice(n0, n0 + TILE)
                    v = nt(ed, ad[m, cols, :]) + nn(full, wdn[m, :, cols])
                    dg[rows, cols] = (v * dg[rows, cols].astype(F32)).astype(BF)
                vT[0:RANK, rows] = nt(dg[rows, :], bu[m]).astype(BF).T
                return carry

            lax.fori_loop(0, T, chunk, 0)

        def attention_back(m, meanwhile):
            dk[...] = jnp.zeros_like(dk)
            dv[...] = jnp.zeros_like(dv)
            for i in range(T):
                icols = slice(i * R, (i + 1) * R)

                def pair(p, carry, i=i, icols=icols):
                    for hh in range(2):
                        h = 2 * p + hh
                        q = head_part(qp[m * PAIRS + p, icols, :], hh)
                        do = head_part(dop[p, icols, :], hh)
                        hrows = pl.ds(pl.multiple_of(h * HEAD, HEAD), HEAD)
                        low = lse[pl.ds(m * HEADS + h, 1), icols]
                        dlt = delta[pl.ds(h, 1), icols]
                        acc = jnp.zeros((HEAD, R), F32)
                        for j in range(i + 1):
                            jrows = slice(j * R, (j + 1) * R)
                            prob = jnp.exp(scores_t(m, p, i, j, q) - low)
                            dp_t = nt(vp[m * PAIRS + p, jrows, :], do)
                            ds_t = (prob * (dp_t - dlt)).astype(BF)
                            dv[p, jrows, :] += nn(prob.astype(BF), do)
                            dk[p, jrows, :] += nn(ds_t, q)
                            acc = acc + nn(kT[m, hrows, jrows], ds_t)
                        dqt[hrows, icols] = acc
                    return carry

                lax.fori_loop(0, PAIRS, pair, 0)
                meanwhile(i)

        def turn_back(m):
            def step(i, carry):
                rows = block(i)
                cosine, sine = rope_of(i)
                sine = -sine
                dq = dqt[:, rows].T * 0.125
                for p in range(PAIRS):
                    lanes = slice(p * 128, (p + 1) * 128)
                    dqkv[rows, p * 128:(p + 1) * 128] = turn(dq[:, lanes], cosine, sine).astype(BF)
                    dqkv[rows, QC + p * 128:QC + (p + 1) * 128] = turn(
                        dk[p, rows, :], cosine, sine
                    ).astype(BF)
                    dqkv[rows, 2 * QC + p * 128:2 * QC + (p + 1) * 128] = dv[p, rows, :].astype(BF)
                dop[0, rows, :] = nt(dqkv[rows, :], bq[m]).astype(BF)
                return carry

            lax.fori_loop(0, T, step, 0)

        def project_back(m):
            def tail(n, carry):
                c = T - 1 - n
                i = across(c)
                rows = block(i)
                dj = dqkv[rows, :]
                du = dg[rows, :]
                e1 = dop[0, rows, :]
                e2 = vT[0:RANK, rows].T
                for n0 in range(0, D, TILE):
                    cols = slice(n0, n0 + TILE)
                    dn1 = nt(dj, wq[m, cols, :]) + nt(e1, aq[m, cols, :])
                    dn2 = nt(du, wup[m, cols, :]) + nt(e2, au[m, cols, :])
                    xhc = xh[m, rows, cols].astype(F32)
                    gb[0:1, cols] += jnp.sum(dn1 * xhc, axis=0, keepdims=True)
                    gb[1:2, cols] += jnp.sum(dn2 * xhc, axis=0, keepdims=True)
                    gb[2:3, cols] += jnp.sum(dn1, axis=0, keepdims=True)
                    gb[3:4, cols] += jnp.sum(dn2, axis=0, keepdims=True)
                    sbuf[i, :, cols] = (dn1 * gain_of(m, 0, cols) + dn2 * gain_of(m, 1, cols)).astype(BF)
                blocks_next(3 - m, c)
                return carry

            lax.fori_loop(0, T, tail, 0)

            @pl.when(m == 1)
            def _():
                act_out(1).sent()
                local_copy(ct_in.at[s], yw, 0).start()

        def put(buf, base, width, col, value):
            lo = 0
            while lo < value.shape[1]:
                j, at = divmod(col + lo, width)
                n = min(width - at, value.shape[1] - lo)
                buf[base + j, :, at:at + n] = value[:, lo:lo + n].astype(BF)
                lo += n

        def pad(buf, base, width, total):
            spare = -total % width
            if spare > 0:
                put(buf, base, width, total, jnp.zeros((RANK, spare), F32))

        def summed_rows(m, j, left):
            acc[...] = jnp.zeros((RANK, D), F32)

            def step(i, carry):
                rows = block(i)
                n = (xh[m, rows, :].astype(F32) * gain_of(m, j) + bias_of(m, j)).astype(BF)
                acc[...] += nn(left(rows), n)
                return carry

            lax.fori_loop(0, T, step, 0)
            return acc[...]

        def early_gradients(m):
            put(pa_e, 0, EARLY.PW, 0, ADAPTER_SCALE * nn(t12t[m, RANK:2 * RANK, :], dg[...]))
            put(pa_e, 0, EARLY.PW, FFL, nt(edot[0:RANK, :], oT[m]))
            put(pa_e, 0, EARLY.PW, FFL + QC, nn(edot[RANK:2 * RANK, :], hw[...]))
            pad(pa_e, 0, EARLY.PW, EARLY.alone)
            put(pt_e, 0, EARLY.GRW, D, ADAPTER_SCALE * nn(todt[m, 0:RANK, :], dz[m]))
            put(pt_e, 0, EARLY.GRW, 2 * D, ADAPTER_SCALE * nn(todt[m, RANK:2 * RANK, :], dz[m]))
            put(pt_e, 0, EARLY.GRW, 0, summed_rows(m, 1, lambda rows: vT[0:RANK, rows]))

        def late_gradients(m):
            put(pa_l, 0, LATE.PW, 0, ADAPTER_SCALE * nn(t12t[m, 0:RANK, :], dqkv[...]))
            pad(pa_l, 0, LATE.PW, LATE.alone)
            put(pt_l, 0, LATE.GRW, 0, summed_rows(m, 0, lambda rows: dop[0, rows, :].T))

        def finish_backward(m):
            @pl.when(m == 1)
            def _():
                local_copy(ct_in.at[s], yw, 0).wait()

            @pl.when(m == 0)
            def _():
                ig_out(1).sent()

            blocks_arrive(3 - m)
            for low in range(2):
                rows = slice(low * B, (low + 1) * B)
                xhat, rstd = norm_parts(xw[m, rows, :])
                g = block_sum(3 - m, low)
                mean_g = jnp.mean(g, axis=1, keepdims=True)
                mean_gx = jnp.mean(g * xhat, axis=1, keepdims=True)
                v = yw[rows, :] + (g - mean_g - xhat * mean_gx) * rstd
                yw[rows, :] = v

                @pl.when(m == 1)
                def _(v=v, low=low):
                    dz[0, half(t, low == 1)] = v.astype(BF)

            @pl.when(m == 1)
            def _():
                rows_start(dz, 0, z_ss, z_rs)
                ig_out(1).start()

            @pl.when(m == 0)
            def _():
                ig_out(0).start()

            rows_sent(dz, m, z_ss, z_rs)
            blocks_sent(3 - m)

        def guarded(full, condition, action):
            if full:
                action()
            else:
                pl.when(condition)(action)

        class Exchange:
            def __init__(self, index, k, pieces, gather, source, landing):
                self.args = index, k, source, landing
                self.full = pieces >= DP
                to, come = lax.rem(d + k, DP), lax.rem(d - k + DP, DP)
                self.sends = d < pieces if gather else to < pieces
                self.hears = come < pieces if gather else d < pieces

            def copy(self):
                index, k, source, landing = self.args
                return to_peer("dp", DP, d, k, source(lax.rem(d + k, DP)), landing(k - 1),
                               ad_ss.at[index, k - 1], ad_rs.at[index, k - 1])

            def start(self):
                guarded(self.full, self.sends, lambda: self.copy().start())

            def wait_send(self):
                guarded(self.full, self.sends, lambda: self.copy().wait_send())

            def wait_recv(self):
                guarded(self.full, self.hears, lambda: self.copy().wait_recv())

        def over_dp(index, source, landing, pieces=DP, gather=False):
            for k in range(1, DP):
                yield Exchange(index, k, pieces, gather, source, landing)

        def over_tensor(index, source, landing):
            for k in range(1, T):
                yield to_peer("tensor", T, t, k, source(lax.rem(t + k, T)), landing(k - 1),
                              at_ss.at[index, k - 1], at_rs.at[index, k - 1])

        def gb_over():
            return to_other(gb, gb_x, c_ss.at[17], c_rs.at[17])

        def gb_tensor():
            return over_tensor(4, lambda j: gb, lambda k: gb_t.at[k])

        def gb_dp():
            return over_dp(8, lambda j: gb_sum, lambda k: gb_d.at[k])

        def start_all(copies):
            for copy in copies:
                copy.start()

        def arrive_all(copies):
            for copy in copies:
                copy.wait_recv()

        def sent_all(copies):
            for copy in copies:
                copy.wait_send()

        class Sums:
            def __init__(self, group, size, refs, ga_out, gr_out):
                self.g, self.z = group, size
                (self.pa, self.pa_x, self.pa_in, self.pa_sum, self.pt, self.pt_x, self.pt_in,
                 self.pb, self.pb_in, self.pb_all) = refs
                self.ga_out, self.gr_out = ga_out, gr_out

            def over(self):
                yield to_other(self.pt, self.pt_x, c_ss.at[13 + 2 * self.g], c_rs.at[13 + 2 * self.g])
                yield to_other(self.pa, self.pa_x, c_ss.at[14 + 2 * self.g], c_rs.at[14 + 2 * self.g])

            def pa_scatter(self):
                return over_dp(4 * self.g, lambda j: self.pa.at[lax.rem(j, self.z.NA)], lambda k: self.pa_in.at[k], self.z.NA)

            def pa_gather(self):
                return over_dp(4 * self.g + 1, lambda j: self.pa_sum, lambda k: self.ga_place(), self.z.NA, True)

            def pb_scatter(self):
                return over_dp(4 * self.g + 2, lambda j: self.pb.at[lax.rem(j, self.z.NB)], lambda k: self.pb_in.at[k], self.z.NB)

            def pb_gather(self):
                return over_dp(
                    4 * self.g + 3, lambda j: self.pb_all.at[lax.rem(d, self.z.NB)], lambda k: self.pb_all.at[lax.rem(d, self.z.NB)], self.z.NB, True
                )

            def pt_scatter(self):
                return over_tensor(2 * self.g, lambda j: self.pt.at[j], lambda k: self.pt_in.at[k])

            def pt_gather(self):
                return over_tensor(2 * self.g + 1, lambda j: self.pt.at[t], lambda k: self.gr_place())

            def ga_place(self):
                return self.ga_out.at[:, pl.ds(pl.multiple_of(lax.rem(d, self.z.NA) * self.z.PW, 128), self.z.PW)]

            def gr_place(self):
                return self.gr_out.at[:, pl.ds(pl.multiple_of(t * self.z.GRW, 128), self.z.GRW)]

            def ga_store(self):
                return pltpu.make_async_copy(self.pa_sum, self.ga_place(), f_s.at[2 * self.g])

            def gr_store(self):
                return pltpu.make_async_copy(self.pt.at[t], self.gr_place(), f_s.at[2 * self.g + 1])

            def give(self):
                start_all(self.over())

            def given(self):
                sent_all(self.over())

            def begin(self):
                arrive_all(self.over())
                for j in range(T):
                    self.pt[j] = (self.pt[j].astype(F32) + self.pt_x[j].astype(F32)).astype(BF)
                start_all(self.pt_scatter())
                for j in range(self.z.NA):
                    self.pa[j] = (self.pa[j].astype(F32) + self.pa_x[j].astype(F32)).astype(BF)
                start_all(self.pa_scatter())

            def pass_on(self):
                arrive_all(self.pt_scatter())
                v = self.pt[t].astype(F32)
                for k in range(T - 1):
                    v = v + self.pt_in[k].astype(F32)
                put(self.pb, 0, self.z.SW, 0, v)
                pad(self.pb, 0, self.z.SW, self.z.GRW)
                start_all(self.pb_scatter())
                arrive_all(self.pa_scatter())

                def add():
                    v = self.pa[d].astype(F32)
                    for k in range(DP - 1):
                        v = v + self.pa_in[k].astype(F32)
                    self.pa_sum[...] = v.astype(BF)
                    self.ga_store().start()

                guarded(self.z.NA >= DP, d < self.z.NA, add)
                start_all(self.pa_gather())

            def add(self):
                arrive_all(self.pb_scatter())

                def add():
                    v = self.pb[d].astype(F32)
                    for k in range(DP - 1):
                        v = v + self.pb_in[k].astype(F32)
                    self.pb_all[d] = v.astype(BF)

                guarded(self.z.NB >= DP, d < self.z.NB, add)
                start_all(self.pb_gather())

            def spread(self):
                arrive_all(self.pb_gather())
                for j in range(self.z.NB):
                    lo, hi = j * self.z.SW, min((j + 1) * self.z.SW, self.z.GRW)
                    self.pt[t, :, lo:hi] = self.pb_all[j, :, 0:hi - lo]
                start_all(self.pt_gather())
                self.gr_store().start()

            def end(self):
                for copies in (self.pa_gather(), self.pt_gather()):
                    arrive_all(copies)
                for copies in (self.pa_scatter(), self.pa_gather(), self.pt_scatter(), self.pt_gather(),
                               self.pb_scatter(), self.pb_gather()):
                    sent_all(copies)
                guarded(self.z.NA >= DP, d < self.z.NA, lambda: self.ga_store().wait())
                self.gr_store().wait()

        early = Sums(0, EARLY, (pa_e, pa_x_e, pa_in_e, pa_sum_e, pt_e, pt_x_e, pt_in_e, pb_e, pb_in_e, pb_all_e), ga_early, gr_early)
        late = Sums(1, LATE, (pa_l, pa_x_l, pa_in_l, pa_sum_l, pt_l, pt_x_l, pt_in_l, pb_l, pb_in_l, pb_all_l), ga_late, gr_late)

        def gb_store():
            return pltpu.make_async_copy(gb, gb_out, f_s.at[4])

        def gb_begin():
            gb_over().wait_recv()
            gb[...] = gb[...] + gb_x[...]
            start_all(gb_tensor())

        def gb_pass_on():
            arrive_all(gb_tensor())
            total = gb[...]
            for k in range(T - 1):
                total = total + gb_t[k]
            gb_sum[...] = total
            start_all(gb_dp())

        def gb_end():
            arrive_all(gb_dp())
            sent_all(gb_tensor())
            total = gb_sum[...]
            for k in range(DP - 1):
                total = total + gb_d[k]
            gb[...] = total
            gb_store().start()
            sent_all(gb_dp())
            gb_store().wait()

        def on_core(core, *actions):
            @pl.when(s == core)
            def _():
                for action in actions:
                    action()

        gradient_to_hidden(1, lambda c: None)
        attention_back(1, lambda i: None)
        turn_back(1)
        project_back(1)
        on_core(0, gb_over().start)
        early_gradients(1)
        on_core(0, early.give)
        late_gradients(1)
        on_core(0, late.give)
        local_copy(h_hbm, hw, 1).start()
        local_copy(dg_hbm, dg, 2).start()
        on_core(1, early.begin)
        finish_backward(1)
        on_core(1, late.begin, gb_begin, early.pass_on)

        def meanwhile(c):
            for when, actions in ((1, (early.add, late.pass_on)), (2, (early.spread, gb_pass_on)), (3, (late.add,))):
                @pl.when(jnp.logical_and(s == 1, c == when))
                def _(actions=actions):
                    for action in actions:
                        action()

        def in_attention(i):
            if i == 1:
                on_core(0, early.begin)

        gradient_to_hidden(0, meanwhile)
        on_core(1, late.spread, early.end)
        on_core(0, early.given)
        local_copy(h_hbm, hw, 1).wait()
        early_gradients(0)
        on_core(1, early.give)
        attention_back(0, in_attention)
        on_core(1, late.end, gb_end)
        on_core(0, late.given, gb_over().wait_send)
        turn_back(0)
        late_gradients(0)
        on_core(1, late.give)
        on_core(0, early.pass_on, late.begin)
        gb[...] = jnp.zeros_like(gb)
        project_back(0)
        on_core(1, gb_over().start)
        on_core(0, early.add, late.pass_on, gb_begin, early.spread)
        finish_backward(0)
        on_core(0, late.add, gb_pass_on, late.spread, gb_end, early.end, late.end)
        on_core(1, early.given, late.given, gb_over().wait_send)

        ig_out(0).sent()
        act_out(0).sent()
        for layer in range(2):
            act_out(layer).arrive()
            ig_out(layer).arrive()
        for index in range(9):
            factor_over(index, s).wait_send()
        for index in range(4):
            for owner in range(DP):
                weight_over(index, s, owner).wait_send()

    def sums_scratch(z):
        return [
            pltpu.VMEM((z.NA, RANK, z.PW), BF),
            pltpu.VMEM((z.NA, RANK, z.PW), BF),
            pltpu.VMEM((DP - 1, RANK, z.PW), BF),
            pltpu.VMEM((RANK, z.PW), BF),
            pltpu.VMEM((T, RANK, z.GRW), BF),
            pltpu.VMEM((T, RANK, z.GRW), BF),
            pltpu.VMEM((T - 1, RANK, z.GRW), BF),
            pltpu.VMEM((z.NB, RANK, z.SW), BF),
            pltpu.VMEM((DP - 1, RANK, z.SW), BF),
            pltpu.VMEM((z.NB, RANK, z.SW), BF),
        ]

    any_spec = pl.BlockSpec(memory_space=pl.ANY)
    vmem_spec = pl.BlockSpec(memory_space=pltpu.VMEM)
    smem_spec = pl.BlockSpec(memory_space=pltpu.SMEM)
    shapes = jax.ShapeDtypeStruct
    return pl.pallas_call(
        kernel,
        out_shape=(
            shapes((M, R, D), F32), shapes((M, R, D), F32),
            shapes((8, D), F32),
            shapes((L, FFL), BF), shapes((L, FFL), BF),
            shapes((RANK, EARLY.NA * EARLY.PW), BF), shapes((RANK, EARLY.both), BF),
            shapes((RANK, LATE.NA * LATE.PW), BF), shapes((RANK, LATE.both), BF),
        ),
        in_specs=[any_spec] * 14 + [vmem_spec] * 3 + [smem_spec],
        out_specs=(any_spec,) * 9,
        scratch_shapes=[
            pltpu.VMEM((2, D, RANK), BF), pltpu.VMEM((2, RANK, 3 * QC), BF),
            pltpu.VMEM((2, QC, RANK), BF), pltpu.VMEM((2, RANK, D), BF),
            pltpu.VMEM((2, D, RANK), BF), pltpu.VMEM((2, RANK, FFL), BF),
            pltpu.VMEM((2, FFL, RANK), BF), pltpu.VMEM((2, RANK, D), BF),
            pltpu.VMEM((2, 8, D), F32),
            pltpu.VMEM((QC, DR), BF), pltpu.VMEM((FFL, DR), BF),
            pltpu.VMEM((2, D, 3 * QC), BF), pltpu.VMEM((2, D, FFL), BF),
            pltpu.VMEM((2, D, QC), BF), pltpu.VMEM((2, D, FFL), BF),
            pltpu.VMEM((M, L, D), BF),
            pltpu.VMEM((M, 2 * RANK, L), BF),
            pltpu.VMEM((M * PAIRS, L, 128), BF),
            pltpu.VMEM((M * PAIRS, L, 128), BF),
            pltpu.VMEM((M * PAIRS, L, 128), BF),
            pltpu.VMEM((M, QC, L), BF),
            pltpu.VMEM((QC, L), BF),
            pltpu.VMEM((M, QC, L), BF),
            pltpu.VMEM((M * HEADS, L), F32),
            pltpu.VMEM((L, FFL), BF),
            pltpu.VMEM((L, FFL), BF),
            pltpu.VMEM((M, 2 * RANK, L), BF),
            pltpu.VMEM((T, R, D), BF),
            pltpu.VMEM((2 * 6, B, D), BF),
            pltpu.VMEM((M, L, D), BF),
            pltpu.VMEM((PAIRS, L, 128), BF),
            pltpu.VMEM((8, L), F32),
            pltpu.VMEM((2 * RANK, L), BF),
            pltpu.VMEM((PAIRS, L, 128), F32),
            pltpu.VMEM((PAIRS, L, 128), F32),
            pltpu.VMEM((QC, L), F32),
            pltpu.VMEM((L, 3 * QC), BF),
            pltpu.VMEM((RANK, D), F32),
            pltpu.VMEM((8, D), F32),
            pltpu.VMEM((M, R, D), F32),
            pltpu.VMEM((R, D), F32),
            pltpu.VMEM((8, D), F32),
            pltpu.VMEM((8, D), F32),
            pltpu.VMEM((T - 1, 8, D), F32),
            pltpu.VMEM((DP - 1, 8, D), F32),
            *sums_scratch(EARLY), *sums_scratch(LATE),
            pltpu.SemaphoreType.DMA((6,)),
            pltpu.SemaphoreType.DMA((4, 2, DP)),
            pltpu.SemaphoreType.DMA((4, 2, DP)),
            pltpu.SemaphoreType.DMA((4, DP)),
            pltpu.SemaphoreType.DMA((4, DP)),
            pltpu.SemaphoreType.DMA((2 * 4,)),
            pltpu.SemaphoreType.DMA((2 * 4,)),
            pltpu.SemaphoreType.DMA((6,)),
            pltpu.SemaphoreType.DMA((4 * 6,)),
            pltpu.SemaphoreType.DMA((2 * 4,)),
            pltpu.SemaphoreType.DMA((2 * 4,)),
            pltpu.SemaphoreType.DMA((18,)),
            pltpu.SemaphoreType.DMA((18,)),
            pltpu.SemaphoreType.DMA((7,)),
            pltpu.SemaphoreType.DMA((10,)),
            pltpu.SemaphoreType.REGULAR,
            pltpu.SemaphoreType.DMA((5, T - 1)),
            pltpu.SemaphoreType.DMA((5, T - 1)),
            pltpu.SemaphoreType.DMA((9, DP - 1)),
            pltpu.SemaphoreType.DMA((9, DP - 1)),
        ],
        compiler_params=pltpu.CompilerParams(
            collective_id=0, has_side_effects=True, vmem_limit_bytes=63 * 2**20
        ),
    )


def make_finish(T, DP, M, R, D, QC, FFL, RANK):
    DR = D // DP
    EARLY, LATE = group_sizes(T, DP, D, QC, FFL)
    sliced = DR % 128 != 0
    loaded = (
        ((RANK, EARLY.NA * EARLY.PW), BF), ((RANK, EARLY.both), BF),
        ((RANK, LATE.NA * LATE.PW), BF), ((RANK, LATE.both), BF),
        ((DR, RANK), F32), ((3, RANK, QC), F32), ((3, DR, QC), BF),
        ((DR, RANK), F32), ((RANK, FFL), F32), ((DR, FFL), BF),
        ((FFL, RANK), F32), ((RANK, DR), F32), ((FFL, DR), BF),
        ((QC, RANK), F32), ((RANK, DR), F32), ((QC, DR), BF),
        ((M, R, D), F32), ((M, R, D), F32), ((8, D), F32),
    )
    made = (
        (RANK, FFL), (QC, RANK), (FFL, RANK), (D, RANK), (RANK, D), (RANK, D),
        (3, RANK, QC), (D, RANK), (3, DR, QC), (DR, FFL), (FFL, DR), (QC, DR),
    )
    n_in, n_made = len(loaded), len(made)

    def kernel(*refs):
        sources = list(refs[:n_in])
        results = refs[n_in:n_in + n_made + 2]
        gains, biases = refs[n_in + n_made + 2:n_in + n_made + 4]
        held = refs[n_in + n_made + 4:2 * n_in + n_made + 4]
        stage = refs[2 * n_in + n_made + 4:2 * n_in + 2 * n_made + 4]
        in_sem, out_sem = refs[-2:]
        d = lax.axis_index("dp")
        for index in (4, 7):
            sources[index] = sources[index].at[pl.ds(pl.multiple_of(d * DR, DR), DR)]
        if not sliced:
            for index in (11, 14):
                sources[index] = sources[index].at[:, pl.ds(pl.multiple_of(d * DR, 128), DR)]
        loads = [pltpu.make_async_copy(sources[n], held[n], in_sem.at[n]) for n in range(n_in)]
        for copy in loads:
            copy.start()
        stores = []

        def take(*indices):
            for index in indices:
                loads[index].wait()

        def store(index, source):
            copy = pltpu.make_async_copy(source, results[index], out_sem.at[index])
            copy.start()
            stores.append(copy)

        def give(index, value):
            stage[index][...] = value
            store(index, stage[index])

        def factor(ref):
            return (ADAPTER_SCALE * ref).astype(BF)

        take(0)
        ga = held[0]
        give(0, ga[:, 0:FFL].astype(F32))
        give(1, ga[:, FFL:FFL + QC].astype(F32).T)
        give(2, ga[:, FFL + QC:2 * FFL + QC].astype(F32).T)
        take(1)
        gr = held[1]
        give(3, gr[:, 0:D].astype(F32).T)
        give(4, gr[:, D:2 * D].astype(F32))
        give(5, gr[:, 2 * D:3 * D].astype(F32))
        take(2, 3)
        for part in range(3):
            stage[6][part] = held[2][:, part * QC:(part + 1) * QC].astype(F32)
        store(6, stage[6])
        give(7, held[3][...].astype(F32).T)
        take(4, 5, 6)
        for part in range(3):
            stage[8][part] = held[6][part].astype(F32) + nn(held[4][...].astype(BF), factor(held[5][part]))
        store(8, stage[8])
        take(7, 8, 9)
        give(9, held[9][...].astype(F32) + nn(held[7][...].astype(BF), factor(held[8][...])))
        take(10, 11, 12)
        give(10, held[12][...].astype(F32) + nn(held[10][...].astype(BF), factor(held[11][...])))
        take(13, 14, 15)
        give(11, held[15][...].astype(F32) + nn(held[13][...].astype(BF), factor(held[14][...])))
        for index in range(2):
            take(16 + index)
            store(12 + index, held[16 + index])
        take(18)
        gains[...] = held[18][0:2]
        biases[...] = held[18][2:4]
        for copy in stores:
            copy.wait()

    any_spec = pl.BlockSpec(memory_space=pl.ANY)
    rows = ((M, R, D),) * 2
    vmem_spec = pl.BlockSpec(memory_space=pltpu.VMEM)
    return pl.pallas_call(
        kernel,
        out_shape=tuple(jax.ShapeDtypeStruct(shape, F32) for shape in made + rows + ((2, D),) * 2),
        in_specs=[any_spec] * n_in,
        out_specs=(any_spec,) * (n_made + 2) + (vmem_spec,) * 2,
        scratch_shapes=[
            *(pltpu.VMEM(shape, dtype) for shape, dtype in loaded),
            *(pltpu.VMEM(shape, F32) for shape in made),
            pltpu.SemaphoreType.DMA((n_in,)), pltpu.SemaphoreType.DMA((n_made + 2,)),
        ],
        compiler_params=pltpu.CompilerParams(vmem_limit_bytes=63 * 2**20),
    )


def rope_table(length):
    half = ROT // 2
    inverse = np.float32(10000.0) ** (-np.arange(half, dtype=np.float32) * np.float32(2.0 / ROT))
    angles = np.arange(length, dtype=np.float32)[:, None] * inverse[None, :]
    cosine, sine = np.cos(angles.astype(np.float64)), np.sin(angles.astype(np.float64))
    rest = np.zeros((length, HEAD - ROT))
    return np.concatenate(
        [cosine, cosine, rest + 1.0, -sine, sine, rest], axis=-1
    ).astype(np.float32)


def solution(mesh):
    T = mesh.shape["tensor"]
    DP = mesh.shape["dp"]

    def per_device(
        inputs, cotangent, split,
        query_key_value_weight, output_weight, up_weight, down_weight,
        qkv_adapter_input, qkv_adapter_output, out_adapter_input, out_adapter_output,
        up_adapter_input, up_adapter_output, down_adapter_input, down_adapter_output,
        ln_gain, ln_bias,
    ):
        M, R, D = inputs.shape
        QC = output_weight.shape[1]
        FFL = up_weight.shape[2]
        RANK = qkv_adapter_input.shape[2]
        L = R * T
        wq = query_key_value_weight[0].transpose(1, 0, 2)
        bq = qkv_adapter_output[0].transpose(1, 0, 2)
        DR = D // DP
        kernel = make_kernel(T, DP, M, R, D, QC, FFL, RANK)
        act, ig, gb, _, _, ga_early, gr_early, ga_late, gr_late = kernel(
            inputs, cotangent, wq, up_weight[0], output_weight[0], down_weight[0],
            qkv_adapter_input[0], bq,
            out_adapter_input[0], out_adapter_output[0],
            up_adapter_input[0], up_adapter_output[0],
            down_adapter_input[0], down_adapter_output[0],
            ln_gain[0], ln_bias[0], jnp.asarray(rope_table(L)), split[:, 0],
        )
        out_factor, down_factor = out_adapter_output[0], down_adapter_output[0]
        if DR % 128 != 0:
            start = lax.axis_index("dp") * DR
            out_factor = lax.dynamic_slice_in_dim(out_factor, start, DR, 1)
            down_factor = lax.dynamic_slice_in_dim(down_factor, start, DR, 1)
        (
            b_up, a_out, a_down, a_up, b_out, b_down, b_qkv, a_qkv, c_qkv, c_up, c_down, c_out, act, ig,
            grad_gain, grad_bias,
        ) = make_finish(T, DP, M, R, D, QC, FFL, RANK)(
            ga_early, gr_early, ga_late, gr_late,
            qkv_adapter_input[0], bq, wq,
            up_adapter_input[0], up_adapter_output[0], up_weight[0],
            down_adapter_input[0], down_factor, down_weight[0],
            out_adapter_input[0], out_factor, output_weight[0],
            act, ig, gb,
        )
        return (
            act[None], ig[None],
            a_qkv[None], b_qkv.transpose(1, 0, 2)[None],
            a_out[None], b_out[None], a_up[None], b_up[None], a_down[None], b_down[None],
            grad_gain[None], grad_bias[None],
            c_qkv.transpose(1, 0, 2)[None], c_out[None], c_up[None], c_down[None],
        )

    rows = P(None, ("dp", "tensor"), None)
    whole = P("section", None, None)
    in_specs = (
        rows, rows, P(None, "dp"),
        P("section", "dp", None, "tensor"), P("section", "tensor", "dp"),
        P("section", "dp", "tensor"), P("section", "tensor", "dp"),
        whole, P("section", None, None, "tensor"), P("section", "tensor", None), whole,
        whole, P("section", None, "tensor"), P("section", "tensor", None), whole,
        whole, whole,
    )
    layer_rows = P("section", None, ("dp", "tensor"), None)
    out_specs = (
        layer_rows, layer_rows,
        whole, P("section", None, None, "tensor"), P("section", "tensor", None), whole,
        whole, P("section", None, "tensor"), P("section", "tensor", None), whole,
        whole, whole,
        P("section", "dp", None, "tensor"), P("section", "tensor", "dp"),
        P("section", "dp", "tensor"), P("section", "tensor", "dp"),
    )
    return jax.shard_map(
        per_device, mesh=mesh, in_specs=in_specs, out_specs=out_specs, check_vma=False
    )
```

```python
import functools

import jax
import jax.numpy as jnp
import numpy as np
from jax import lax
from jax.experimental import pallas as pl
from jax.experimental.pallas import tpu as pltpu
from jax.sharding import PartitionSpec as P

HEAD = 64
ROT = 16
ADAPTER_SCALE = 0.25
EPSILON = 1e-05
MASKED = -1e30
BF = jnp.bfloat16
F32 = jnp.float32
MESH = pl.DeviceIdType.MESH


def nn(a, b):
    return lax.dot_general(a, b, (((1,), (0,)), ((), ())), preferred_element_type=F32)


def nt(a, b):
    return lax.dot_general(a, b, (((1,), (1,)), ((), ())), preferred_element_type=F32)


class Sizes:
    def __init__(self, T, DP, alone, both):
        self.alone, self.both = alone, both
        self.PW = -(-alone // (DP * 128)) * 128
        self.GRW = both // T
        self.SW = -(-self.GRW // (DP * 128)) * 128
        self.NA, self.NB = -(-alone // self.PW), -(-self.GRW // self.SW)


def group_sizes(T, DP, D, QC, FFL):
    return Sizes(T, DP, QC + 2 * FFL, 3 * D), Sizes(T, DP, 3 * QC, D)


def make_kernel(T, DP, M, R, D, QC, FFL, RANK):
    L = R * T
    DR = D // DP
    B = R // 2
    PAIRS = QC // 128
    HEADS = QC // HEAD
    TILE = 256
    HALF = L // 2
    EARLY, LATE = group_sizes(T, DP, D, QC, FFL)

    def kernel(
        x_in, ct_in, wq_in, wup_in, wout_in, wdn_in,
        aq_in, bq_in, ao_in, bo_in, au_in, bu_in, ad_in, bd_in, gain_in, bias_in, rope, split,
        act, ig, gb_out, h_hbm, dg_hbm, ga_early, gr_early, ga_late, gr_late,
        aq, bq, ao, bo, au, bu, ad, bd, norms, wout_raw, wdn_raw,
        wq, wup, wout, wdn, xh, t12t, qp, kp, vp, kT, vT, oT, lse, hw, dg,
        todt, sbuf, rbuf, dz, dop, delta, edot, dk, dv, dqt, dqkv,
        acc, gb, xw, yw, gb_x, gb_sum, gb_t, gb_d,
        pa_e, pa_x_e, pa_in_e, pa_sum_e, pt_e, pt_x_e, pt_in_e, pb_e, pb_in_e, pb_all_e,
        pa_l, pa_x_l, pa_in_l, pa_sum_l, pt_l, pt_x_l, pt_in_l, pb_l, pb_in_l, pb_all_l,
        w_ls, w_ss, w_rs, v_ss, v_rs, x_ss, x_rs, r_ss, r_rs, z_ss, z_rs, c_ss, c_rs, l_s, f_s,
        go, at_ss, at_rs, ad_ss, ad_rs,
    ):
        s = lax.axis_index("section")
        d = lax.axis_index("dp")
        t = lax.axis_index("tensor")
        other = 1 - s

        barrier = pltpu.get_barrier_semaphore()
        for k in range(1, T):
            pl.semaphore_signal(
                barrier, inc=1, device_id={"tensor": lax.rem(t + k, T)}, device_id_type=MESH
            )
        for k in range(1, DP):
            pl.semaphore_signal(
                barrier, inc=1, device_id={"dp": lax.rem(d + k, DP)}, device_id_type=MESH
            )
        pl.semaphore_signal(barrier, inc=1, device_id={"section": other}, device_id_type=MESH)
        pl.semaphore_wait(barrier, T + DP - 1)

        def to_other(src, dst, ssem, rsem):
            return pltpu.make_async_remote_copy(
                src_ref=src, dst_ref=dst, send_sem=ssem, recv_sem=rsem,
                device_id={"section": other}, device_id_type=MESH,
            )

        def gathered(index, layer, owner):
            return (wq, wup, wout, wdn)[index].at[layer, pl.ds(pl.multiple_of(owner * DR, DR), DR)]

        def weight_copy(index, way, hop, owner):
            place = gathered(index, s, owner)
            return pltpu.make_async_remote_copy(
                src_ref=place, dst_ref=place,
                send_sem=w_ss.at[index, way, hop], recv_sem=w_rs.at[index, way, hop],
                device_id={"dp": d + 1 if way == 0 else d - 1}, device_id_type=MESH,
            )

        def weight_over(index, layer, owner):
            place = gathered(index, layer, owner)
            return to_other(place, place, v_ss.at[index, owner], v_rs.at[index, owner])

        has_next = (d < DP - 1, d > 0)

        def holds(way, hop):
            return d >= hop + 1 if way == 0 else d + hop + 1 <= DP - 1

        def owner_of(way, hop):
            return d - hop - 1 if way == 0 else d + hop + 1

        def weight_local(index):
            place = gathered(index, s, d)
            if index == 0:
                return [
                    pltpu.make_async_copy(
                        wq_in.at[part], place.at[:, part * QC:(part + 1) * QC], w_ls.at[part]
                    )
                    for part in range(3)
                ]
            stage = (None, place, wout_raw, wdn_raw)[index]
            return [pltpu.make_async_copy((None, wup_in, wout_in, wdn_in)[index], stage, w_ls.at[2 + index])]

        def weights_own(indices):
            for index in indices:
                for copy in weight_local(index):
                    copy.wait()
                rows = pl.ds(pl.multiple_of(d * DR, DR), DR)
                if index == 2:
                    wout[s, rows, :] = wout_raw[...].T
                if index == 3:
                    wdn[s, rows, :] = wdn_raw[...].T

        def weights_start(indices):
            for index in indices:
                for way in range(2):
                    @pl.when(has_next[way])
                    def _(index=index, way=way):
                        weight_copy(index, way, 0, d).start()
                weight_over(index, s, d).start()

        def weights_hop(indices, hop):
            for index in indices:
                for way in range(2):
                    @pl.when(holds(way, hop))
                    def _(index=index, way=way):
                        owner = owner_of(way, hop)
                        weight_copy(index, way, hop, owner).wait_recv()

                        @pl.when(has_next[way])
                        def _():
                            weight_copy(index, way, hop + 1, owner).start()

                        weight_over(index, s, owner).start()

        def weights_pass(indices, first, last):
            if last > first:
                def step(hop, carry):
                    weights_hop(indices, hop)
                    return carry

                lax.fori_loop(first, last, step, 0)

        def weights_sent():
            for index in range(4):
                for way in range(2):
                    @pl.when(has_next[way])
                    def _(index=index, way=way):
                        weight_copy(index, way, 0, d).wait_send()

            def step(hop, carry):
                for index in range(4):
                    for way in range(2):
                        @pl.when(jnp.logical_and(has_next[way], holds(way, hop)))
                        def _(index=index, way=way):
                            weight_copy(index, way, hop + 1, owner_of(way, hop)).wait_send()
                return carry

            lax.fori_loop(0, DP - 1, step, 0)

        def weights_from_other(indices, layer):
            def step(owner, carry):
                for index in indices:
                    weight_over(index, layer, owner).wait_recv()
                return carry

            lax.fori_loop(0, DP, step, 0)

        for index in range(4):
            for copy in weight_local(index):
                copy.start()

        factors = (
            (aq_in, dk.at[0], aq, 1.0), (au_in, dk.at[1], au, 1.0),
            (ad_in, dv.at[0], ad, 1.0), (ao_in, dv.at[1, 0:QC], ao, 1.0),
            (None, xw.at[1, 0:RANK, 0:3 * QC], bq, ADAPTER_SCALE), (bu_in, xw.at[1, RANK:2 * RANK, 0:FFL], bu, ADAPTER_SCALE),
            (bo_in, dqt.at[0:RANK, 0:D], bo, ADAPTER_SCALE), (bd_in, dqt.at[RANK:2 * RANK, 0:D], bd, ADAPTER_SCALE),
        )

        def factor_load(index):
            source, stage, _, _ = factors[index]
            if index == 4:
                return [
                    pltpu.make_async_copy(
                        bq_in.at[part], xw.at[1, 0:RANK, part * QC:(part + 1) * QC], f_s.at[7 + part if part else 4]
                    )
                    for part in range(3)
                ]
            return [pltpu.make_async_copy(source, stage, f_s.at[index])]

        def factor_over(index, layer):
            place = norms.at[layer] if index == 8 else factors[index][2].at[layer]
            return to_other(place, place, c_ss.at[index], c_rs.at[index])

        def factors_give():
            norms[s, 0:2, :] = gain_in[...]
            norms[s, 2:4, :] = bias_in[...]
            factor_over(8, s).start()
            for index, (_, stage, place, scale) in enumerate(factors):
                for copy in factor_load(index):
                    copy.wait()
                v = stage[...]
                place[s] = (v if scale == 1.0 else v * scale).astype(BF)
                factor_over(index, s).start()

        for index in range(8):
            for copy in factor_load(index):
                copy.start()

        def across(c):
            return lax.rem(t + c, 2) + 2 * lax.rem(t // 2 + c // 2, 2)

        def block(i):
            return pl.ds(pl.multiple_of(i * R, R), R)

        def half(i, low):
            return pl.ds(pl.multiple_of(i * R + (B if low else 0), B), B)

        def rows_copy(buf, m, kind, ssem, rsem):
            if kind < 2:
                place = buf.at[m, block(t)]
            elif kind == 2:
                place = buf.at[m, half(across(1), False)]
            else:
                place = buf.at[m, half(across(2), True)]
            return pltpu.make_async_remote_copy(
                src_ref=place, dst_ref=place,
                send_sem=ssem.at[m * 4 + kind], recv_sem=rsem.at[m * 4 + kind],
                device_id={"tensor": across((1, 2, 2, 1)[kind])}, device_id_type=MESH,
            )

        def rows_wait(buf, m, kind, ssem, rsem):
            if kind < 2:
                place = buf.at[m, block(across(1 + kind))]
            else:
                place = buf.at[m, half(across(3), kind == 3)]
            pltpu.make_async_remote_copy(
                src_ref=place, dst_ref=place,
                send_sem=ssem.at[m * 4 + kind], recv_sem=rsem.at[m * 4 + kind],
                device_id={"tensor": across(1)}, device_id_type=MESH,
            ).wait_recv()

        def rows_start(buf, m, ssem, rsem):
            for kind in range(2):
                rows_copy(buf, m, kind, ssem, rsem).start()

        def rows_next(buf, m, c, ssem, rsem):
            @pl.when(c == 1)
            def _():
                for kind in range(2):
                    rows_wait(buf, m, kind, ssem, rsem)
                    rows_copy(buf, m, 2 + kind, ssem, rsem).start()

            @pl.when(c == 3)
            def _():
                for kind in range(2, 4):
                    rows_wait(buf, m, kind, ssem, rsem)

        def rows_sent(buf, m, ssem, rsem):
            for kind in range(4):
                rows_copy(buf, m, kind, ssem, rsem).wait_send()

        def to_peer(axis, size, me, k, src, dst, ssem, rsem):
            return pltpu.make_async_remote_copy(
                src_ref=src, dst_ref=dst, send_sem=ssem, recv_sem=rsem,
                device_id={axis: lax.rem(me + k, size)}, device_id_type=MESH,
            )

        def block_copy(phase, kind):
            place = (
                sbuf.at[across(1), 0:B], sbuf.at[across(3), 0:B],
                sbuf.at[across(2), B:R], sbuf.at[across(3), B:R],
                sbuf.at[across(2), 0:B], sbuf.at[across(1), B:R],
            )[kind]
            return pltpu.make_async_remote_copy(
                src_ref=place, dst_ref=rbuf.at[lax.rem(phase, 2) * 6 + kind],
                send_sem=r_ss.at[kind], recv_sem=r_rs.at[phase * 6 + kind],
                device_id={"tensor": across((1, 1, 2, 2, 2, 1)[kind])}, device_id_type=MESH,
            )

        def blocks_next(phase, c):
            @pl.when(c == 3)
            def _():
                block_copy(phase, 1).start()
                block_copy(phase, 3).start()

            @pl.when(c == 2)
            def _():
                block_copy(phase, 2).start()

            @pl.when(c == 1)
            def _():
                block_copy(phase, 0).start()
                block_copy(phase, 1).wait_recv()
                place = across(2)
                sbuf[place, 0:B] = (
                    sbuf[place, 0:B].astype(F32) + rbuf[lax.rem(phase, 2) * 6 + 1].astype(F32)
                ).astype(BF)
                block_copy(phase, 4).start()
                block_copy(phase, 3).wait_recv()
                place = across(1)
                sbuf[place, B:R] = (
                    sbuf[place, B:R].astype(F32) + rbuf[lax.rem(phase, 2) * 6 + 3].astype(F32)
                ).astype(BF)
                block_copy(phase, 5).start()

        def block_sum(phase, low):
            base = lax.rem(phase, 2) * 6
            if low:
                own, first, second = sbuf[t, B:R], rbuf[base + 2], rbuf[base + 5]
            else:
                own, first, second = sbuf[t, 0:B], rbuf[base], rbuf[base + 4]
            return own.astype(F32) + (first.astype(F32) + second.astype(F32))

        def blocks_arrive(phase):
            for kind in (0, 2, 4, 5):
                block_copy(phase, kind).wait_recv()

        def blocks_sent(phase):
            for kind in range(6):
                block_copy(phase, kind).wait_send()

        def rows_out(src, out, layer, index):
            class Out:
                def start(self):
                    @pl.when(s == layer)
                    def _():
                        local_copy(src, out.at[s], 3 + index).start()

                    @pl.when(s != layer)
                    def _():
                        to_other(src, out.at[s], c_ss.at[9 + index], c_rs.at[9 + index]).start()

                def sent(self):
                    @pl.when(s == layer)
                    def _():
                        local_copy(src, out.at[s], 3 + index).wait()

                    @pl.when(s != layer)
                    def _():
                        to_other(src, out.at[s], c_ss.at[9 + index], c_rs.at[9 + index]).wait_send()

                def arrive(self):
                    @pl.when(s == layer)
                    def _():
                        to_other(src, out.at[other], c_ss.at[9 + index], c_rs.at[9 + index]).wait_recv()

            return Out()

        def act_out(layer):
            return rows_out(yw if layer else xw.at[1], act, layer, layer)

        def ig_out(layer):
            return rows_out(yw, ig, layer, 2 + layer)

        def local_copy(src, dst, index):
            return pltpu.make_async_copy(src, dst, l_s.at[index])

        def norm_parts(x):
            mean = jnp.mean(x, axis=-1, keepdims=True)
            centred = x - mean
            spread = jnp.mean(centred * centred, axis=-1, keepdims=True)
            rstd = lax.rsqrt(spread + EPSILON)
            return centred * rstd, rstd

        def send_normed(layer):
            xhat, _ = norm_parts(xw[layer])
            xh[layer, block(t)] = xhat.astype(BF)
            rows_start(xh, layer, x_ss, x_rs)

        lane = lax.broadcasted_iota(jnp.int32, (R, 128), 1)
        in_first = lax.rem(lane, HEAD) < ROT // 2
        head_low = lane < HEAD

        def turn(v, cosine, sine):
            swapped = jnp.where(in_first, pltpu.roll(v, 128 - ROT // 2, 1), pltpu.roll(v, ROT // 2, 1))
            return v * cosine + swapped * sine

        def rope_of(chunk):
            again = jnp.where(chunk * R >= HALF, chunk * R - HALF, chunk * R)
            plain = rope[pl.ds(pl.multiple_of(chunk * R, R), R), :]
            restarted = rope[pl.ds(pl.multiple_of(again, R), R), :]
            table = jnp.where(split[s] > 0, restarted, plain)
            crossed = pltpu.roll(table, HEAD, 1)
            return jnp.where(head_low, table, crossed), jnp.where(head_low, crossed, table)

        def head_part(v, hh):
            zero = jnp.zeros_like(v)
            return jnp.where(head_low, v, zero) if hh == 0 else jnp.where(head_low, zero, v)

        causal = lax.broadcasted_iota(jnp.int32, (R, R), 0) <= lax.broadcasted_iota(
            jnp.int32, (R, R), 1
        )

        def scores_t(m, p, i, j, q):
            keys = kp[m * PAIRS + p, j * R:(j + 1) * R, :]
            sc = nt(keys, q)
            if j == i:
                sc = jnp.where(causal, sc, MASKED)
            if i * R >= HALF and j * R < HALF:
                sc = sc + MASKED * split[s].astype(F32)
            return sc

        loads = [local_copy(x_in.at[s], xw.at[0], 0), local_copy(ct_in.at[s], yw, 1)]
        for copy in loads:
            copy.start()

        weights_own((0, 1))

        @pl.when(s == 0)
        def _():
            weights_start((0, 1))

        loads[0].wait()
        send_normed(0)
        loads[1].wait()
        dz[1, block(t)] = yw[...].astype(BF)
        rows_start(dz, 1, z_ss, z_rs)
        factors_give()
        weights_own((2, 3))
        gb[...] = jnp.zeros_like(gb)

        @pl.when(s == 0)
        def _():
            weights_pass((0, 1), 0, DP - 2)
            weights_start((2, 3))
            weights_pass((0, 1), DP - 2, DP - 1)

        for index in range(9):
            factor_over(index, other).wait_recv()
        def gain_of(layer, j, cols=slice(None)):
            return norms[layer, j:j + 1, cols]

        def bias_of(layer, j):
            return norms[layer, 2 + j:3 + j, :]

        def normed_to_hidden(m):
            @pl.when(s != m)
            def _():
                weights_from_other((0, 1), m)

            @pl.when(m > 0)
            def _():
                local_copy(hw, h_hbm, 1).wait()
                local_copy(dg, dg_hbm, 2).wait()

            def chunk(c, carry):
                src = across(c)
                rows_next(xh, m, c, x_ss, x_rs)

                @pl.when(jnp.logical_and(c == 2, s == m))
                def _():
                    weights_hop((2, 3), 0)

                rows = block(src)
                xhc = xh[m, rows, :].astype(F32)
                n1 = (xhc * gain_of(m, 0) + bias_of(m, 0)).astype(BF)
                n2 = (xhc * gain_of(m, 1) + bias_of(m, 1)).astype(BF)
                t1 = nn(n1, aq[m]).astype(BF)
                t2 = nn(n2, au[m]).astype(BF)
                t12t[m, 0:RANK, rows] = t1.T
                t12t[m, RANK:2 * RANK, rows] = t2.T
                cosine, sine = rope_of(src)
                for part in range(3):
                    cols = slice(part * QC, (part + 1) * QC)
                    val = nn(n1, wq[m, :, cols]) + nn(t1, bq[m, :, cols])
                    if part == 2:
                        vb = val.astype(BF)
                        for p in range(PAIRS):
                            vp[m * PAIRS + p, rows, :] = vb[:, p * 128:(p + 1) * 128]
                        vT[:, rows] = vb.T
                    else:
                        for p in range(PAIRS):
                            v = turn(val[:, p * 128:(p + 1) * 128], cosine, sine)
                            if part == 0:
                                qp[m * PAIRS + p, rows, :] = (v * 0.125).astype(BF)
                            else:
                                vb = v.astype(BF)
                                kp[m * PAIRS + p, rows, :] = vb
                                kT[m, p * 128:(p + 1) * 128, rows] = vb.T
                for n0 in range(0, FFL, TILE):
                    cols = slice(n0, n0 + TILE)
                    u = nn(n2, wup[m, :, cols]) + nn(t2, bu[m, :, cols])
                    phi = 0.5 * (1.0 + lax.erf(u * 0.7071067811865476))
                    hw[rows, cols] = (u * phi).astype(BF)
                    dg[rows, cols] = (
                        phi + u * (0.3989422804014327 * jnp.exp(-0.5 * u * u))
                    ).astype(BF)
                return carry

            lax.fori_loop(0, T, chunk, 0)
            @pl.when(m == 0)
            def _():
                local_copy(hw, h_hbm, 1).start()
                local_copy(dg, dg_hbm, 2).start()

        def attend(m, i):
                icols = slice(i * R, (i + 1) * R)

                def pair(p, carry, i=i, icols=icols):
                    for hh in range(2):
                        h = 2 * p + hh
                        q = head_part(qp[m * PAIRS + p, icols, :], hh)
                        hrows = pl.ds(pl.multiple_of(h * HEAD, HEAD), HEAD)
                        blocks = [scores_t(m, p, i, j, q) for j in range(i + 1)]
                        top = functools.reduce(
                            jnp.maximum, [jnp.max(b, axis=0, keepdims=True) for b in blocks]
                        )
                        total = jnp.zeros_like(top)
                        acc = jnp.zeros((HEAD, R), F32)
                        for j in range(i + 1):
                            e = jnp.exp(blocks[j] - top)
                            total = total + jnp.sum(e, axis=0, keepdims=True)
                            acc = acc + nn(vT[hrows, j * R:(j + 1) * R], e.astype(BF))
                        oT[m, hrows, icols] = (acc * (1.0 / total)).astype(BF)
                        lse[pl.ds(m * HEADS + h, 1), icols] = top + jnp.log(total)
                    return carry

                lax.fori_loop(0, PAIRS, pair, 0)

        def project(m, c):
                i = across(c)
                rows = block(i)
                o = oT[m, :, rows].T
                hrow = hw[rows, :]
                to = nn(o, ao[m]).astype(BF)
                td = nn(hrow, ad[m]).astype(BF)
                todt[m, 0:RANK, rows] = to.T
                todt[m, RANK:2 * RANK, rows] = td.T
                for n0 in range(0, D, TILE):
                    cols = slice(n0, n0 + TILE)
                    sbuf[i, :, cols] = (
                        nt(o, wout[m, cols, :]) + nt(hrow, wdn[m, cols, :])
                        + nn(to, bo[m, :, cols]) + nn(td, bd[m, :, cols])
                    ).astype(BF)
                blocks_next(m, c)

        def attend_and_project(m):
            def step(n, carry):
                c = T - 1 - lax.rem(n, T)
                now = n // T
                for i in range(T):
                    @pl.when(jnp.logical_and(across(c) == i, now == m))
                    def _(i=i):
                        attend(m, i)

                @pl.when(n == T)
                def _():
                    last_weights(m)

                @pl.when(now == 1)
                def _():
                    project(m, c)
                return carry

            lax.fori_loop(0, 2 * T, step, 0)

        def finish_forward(m):
            blocks_arrive(m)
            for low in range(2):
                rows = slice(low * B, (low + 1) * B)
                y = xw[m, rows, :] + block_sum(m, low)

                @pl.when(m == 0)
                def _(y=y, rows=rows):
                    xw[1, rows, :] = y

                @pl.when(m == 1)
                def _(y=y, rows=rows):
                    yw[rows, :] = y

            @pl.when(m == 0)
            def _():
                send_normed(1)
                act_out(0).start()

            @pl.when(m == 1)
            def _():
                act_out(1).start()

            rows_sent(xh, m, x_ss, x_rs)
            blocks_sent(m)

        def last_weights(m):
            @pl.when(s == m)
            def _():
                weights_pass((2, 3), max(1, DP - 2), DP - 1)
                weights_sent()

            @pl.when(jnp.logical_and(s == 0, m == 0))
            def _():
                pl.semaphore_signal(go, inc=1, device_id={"section": other}, device_id_type=MESH)

            @pl.when(jnp.logical_and(s == 1, m == 0))
            def _():
                pl.semaphore_wait(go, 1)
                weights_start((0, 1))

            @pl.when(s != m)
            def _():
                weights_from_other((2, 3), m)

        def forward(m, carry):
            normed_to_hidden(m)

            @pl.when(s == m)
            def _():
                weights_pass((2, 3), 1, DP - 2)

            attend_and_project(m)

            @pl.when(jnp.logical_and(s == 1, m == 0))
            def _():
                weights_pass((0, 1), 0, DP - 2)
                weights_start((2, 3))

            finish_forward(m)

            @pl.when(jnp.logical_and(s == 1, m == 0))
            def _():
                weights_pass((0, 1), DP - 2, DP - 1)
            return carry

        lax.fori_loop(0, 2, forward, 0)

        def gradient_to_hidden(m, meanwhile):
            @pl.when(m == 0)
            def _():
                local_copy(dg_hbm, dg, 2).wait()

            def chunk(c, carry):
                src = across(c)
                meanwhile(c)
                rows_next(dz, m, c, z_ss, z_rs)
                rows = block(src)
                full = dz[m, rows, :]
                eo = nt(full, bo[m]).astype(BF)
                ed = nt(full, bd[m]).astype(BF)
                edot[0:RANK, rows] = eo.T
                edot[RANK:2 * RANK, rows] = ed.T
                do = nt(eo, ao[m]) + nn(full, wout[m])
                dob = do.astype(BF)
                for p in range(PAIRS):
                    v = dob[:, p * 128:(p + 1) * 128]
                    dop[p, rows, :] = v
                prod = dob.T.astype(F32) * oT[m, :, rows].astype(F32)
                for h in range(HEADS):
                    delta[h:h + 1, rows] = jnp.sum(
                        prod[h * HEAD:(h + 1) * HEAD], axis=0, keepdims=True
                    )
                for n0 in range(0, FFL, TILE):
                    cols = slice(n0, n0 + TILE)
                    v = nt(ed, ad[m, cols, :]) + nn(full, wdn[m, :, cols])
                    dg[rows, cols] = (v * dg[rows, cols].astype(F32)).astype(BF)
                vT[0:RANK, rows] = nt(dg[rows, :], bu[m]).astype(BF).T
                return carry

            lax.fori_loop(0, T, chunk, 0)

        def attention_back(m, meanwhile):
            dk[...] = jnp.zeros_like(dk)
            dv[...] = jnp.zeros_like(dv)
            for i in range(T):
                icols = slice(i * R, (i + 1) * R)

                def pair(p, carry, i=i, icols=icols):
                    for hh in range(2):
                        h = 2 * p + hh
                        q = head_part(qp[m * PAIRS + p, icols, :], hh)
                        do = head_part(dop[p, icols, :], hh)
                        hrows = pl.ds(pl.multiple_of(h * HEAD, HEAD), HEAD)
                        low = lse[pl.ds(m * HEADS + h, 1), icols]
                        dlt = delta[pl.ds(h, 1), icols]
                        acc = jnp.zeros((HEAD, R), F32)
                        for j in range(i + 1):
                            jrows = slice(j * R, (j + 1) * R)
                            prob = jnp.exp(scores_t(m, p, i, j, q) - low)
                            dp_t = nt(vp[m * PAIRS + p, jrows, :], do)
                            ds_t = (prob * (dp_t - dlt)).astype(BF)
                            dv[p, jrows, :] += nn(prob.astype(BF), do)
                            dk[p, jrows, :] += nn(ds_t, q)
                            acc = acc + nn(kT[m, hrows, jrows], ds_t)
                        dqt[hrows, icols] = acc
                    return carry

                lax.fori_loop(0, PAIRS, pair, 0)
                meanwhile(i)

        def turn_back(m):
            def step(i, carry):
                rows = block(i)
                cosine, sine = rope_of(i)
                sine = -sine
                dq = dqt[:, rows].T * 0.125
                for p in range(PAIRS):
                    lanes = slice(p * 128, (p + 1) * 128)
                    dqkv[rows, p * 128:(p + 1) * 128] = turn(dq[:, lanes], cosine, sine).astype(BF)
                    dqkv[rows, QC + p * 128:QC + (p + 1) * 128] = turn(
                        dk[p, rows, :], cosine, sine
                    ).astype(BF)
                    dqkv[rows, 2 * QC + p * 128:2 * QC + (p + 1) * 128] = dv[p, rows, :].astype(BF)
                dop[0, rows, :] = nt(dqkv[rows, :], bq[m]).astype(BF)
                return carry

            lax.fori_loop(0, T, step, 0)

        def project_back(m):
            def tail(n, carry):
                c = T - 1 - n
                i = across(c)
                rows = block(i)
                dj = dqkv[rows, :]
                du = dg[rows, :]
                e1 = dop[0, rows, :]
                e2 = vT[0:RANK, rows].T
                for n0 in range(0, D, TILE):
                    cols = slice(n0, n0 + TILE)
                    dn1 = nt(dj, wq[m, cols, :]) + nt(e1, aq[m, cols, :])
                    dn2 = nt(du, wup[m, cols, :]) + nt(e2, au[m, cols, :])
                    xhc = xh[m, rows, cols].astype(F32)
                    gb[0:1, cols] += jnp.sum(dn1 * xhc, axis=0, keepdims=True)
                    gb[1:2, cols] += jnp.sum(dn2 * xhc, axis=0, keepdims=True)
                    gb[2:3, cols] += jnp.sum(dn1, axis=0, keepdims=True)
                    gb[3:4, cols] += jnp.sum(dn2, axis=0, keepdims=True)
                    sbuf[i, :, cols] = (dn1 * gain_of(m, 0, cols) + dn2 * gain_of(m, 1, cols)).astype(BF)
                blocks_next(3 - m, c)
                return carry

            lax.fori_loop(0, T, tail, 0)

            @pl.when(m == 1)
            def _():
                act_out(1).sent()
                local_copy(ct_in.at[s], yw, 0).start()

        def put(buf, base, width, col, value):
            lo = 0
            while lo < value.shape[1]:
                j, at = divmod(col + lo, width)
                n = min(width - at, value.shape[1] - lo)
                buf[base + j, :, at:at + n] = value[:, lo:lo + n].astype(BF)
                lo += n

        def pad(buf, base, width, total):
            spare = -total % width
            if spare > 0:
                put(buf, base, width, total, jnp.zeros((RANK, spare), F32))

        def summed_rows(m, j, left):
            acc[...] = jnp.zeros((RANK, D), F32)

            def step(i, carry):
                rows = block(i)
                n = (xh[m, rows, :].astype(F32) * gain_of(m, j) + bias_of(m, j)).astype(BF)
                acc[...] += nn(left(rows), n)
                return carry

            lax.fori_loop(0, T, step, 0)
            return acc[...]

        def early_gradients(m):
            put(pa_e, 0, EARLY.PW, 0, ADAPTER_SCALE * nn(t12t[m, RANK:2 * RANK, :], dg[...]))
            put(pa_e, 0, EARLY.PW, FFL, nt(edot[0:RANK, :], oT[m]))
            put(pa_e, 0, EARLY.PW, FFL + QC, nn(edot[RANK:2 * RANK, :], hw[...]))
            pad(pa_e, 0, EARLY.PW, EARLY.alone)
            put(pt_e, 0, EARLY.GRW, D, ADAPTER_SCALE * nn(todt[m, 0:RANK, :], dz[m]))
            put(pt_e, 0, EARLY.GRW, 2 * D, ADAPTER_SCALE * nn(todt[m, RANK:2 * RANK, :], dz[m]))
            put(pt_e, 0, EARLY.GRW, 0, summed_rows(m, 1, lambda rows: vT[0:RANK, rows]))

        def late_gradients(m):
            put(pa_l, 0, LATE.PW, 0, ADAPTER_SCALE * nn(t12t[m, 0:RANK, :], dqkv[...]))
            pad(pa_l, 0, LATE.PW, LATE.alone)
            put(pt_l, 0, LATE.GRW, 0, summed_rows(m, 0, lambda rows: dop[0, rows, :].T))

        def finish_backward(m):
            @pl.when(m == 1)
            def _():
                local_copy(ct_in.at[s], yw, 0).wait()

            @pl.when(m == 0)
            def _():
                ig_out(1).sent()

            blocks_arrive(3 - m)
            for low in range(2):
                rows = slice(low * B, (low + 1) * B)
                xhat, rstd = norm_parts(xw[m, rows, :])
                g = block_sum(3 - m, low)
                mean_g = jnp.mean(g, axis=1, keepdims=True)
                mean_gx = jnp.mean(g * xhat, axis=1, keepdims=True)
                v = yw[rows, :] + (g - mean_g - xhat * mean_gx) * rstd
                yw[rows, :] = v

                @pl.when(m == 1)
                def _(v=v, low=low):
                    dz[0, half(t, low == 1)] = v.astype(BF)

            @pl.when(m == 1)
            def _():
                rows_start(dz, 0, z_ss, z_rs)
                ig_out(1).start()

            @pl.when(m == 0)
            def _():
                ig_out(0).start()

            rows_sent(dz, m, z_ss, z_rs)
            blocks_sent(3 - m)

        def guarded(full, condition, action):
            if full:
                action()
            else:
                pl.when(condition)(action)

        class Exchange:
            def __init__(self, index, k, pieces, gather, source, landing):
                self.args = index, k, source, landing
                self.full = pieces >= DP
                to, come = lax.rem(d + k, DP), lax.rem(d - k + DP, DP)
                self.sends = d < pieces if gather else to < pieces
                self.hears = come < pieces if gather else d < pieces

            def copy(self):
                index, k, source, landing = self.args
                return to_peer("dp", DP, d, k, source(lax.rem(d + k, DP)), landing(k - 1),
                               ad_ss.at[index, k - 1], ad_rs.at[index, k - 1])

            def start(self):
                guarded(self.full, self.sends, lambda: self.copy().start())

            def wait_send(self):
                guarded(self.full, self.sends, lambda: self.copy().wait_send())

            def wait_recv(self):
                guarded(self.full, self.hears, lambda: self.copy().wait_recv())

        def over_dp(index, source, landing, pieces=DP, gather=False):
            for k in range(1, DP):
                yield Exchange(index, k, pieces, gather, source, landing)

        def over_tensor(index, source, landing):
            for k in range(1, T):
                yield to_peer("tensor", T, t, k, source(lax.rem(t + k, T)), landing(k - 1),
                              at_ss.at[index, k - 1], at_rs.at[index, k - 1])

        def gb_over():
            return to_other(gb, gb_x, c_ss.at[17], c_rs.at[17])

        def gb_tensor():
            return over_tensor(4, lambda j: gb, lambda k: gb_t.at[k])

        def gb_dp():
            return over_dp(8, lambda j: gb_sum, lambda k: gb_d.at[k])

        def start_all(copies):
            for copy in copies:
                copy.start()

        def arrive_all(copies):
            for copy in copies:
                copy.wait_recv()

        def sent_all(copies):
            for copy in copies:
                copy.wait_send()

        class Sums:
            def __init__(self, group, size, refs, ga_out, gr_out):
                self.g, self.z = group, size
                (self.pa, self.pa_x, self.pa_in, self.pa_sum, self.pt, self.pt_x, self.pt_in,
                 self.pb, self.pb_in, self.pb_all) = refs
                self.ga_out, self.gr_out = ga_out, gr_out

            def over(self):
                yield to_other(self.pt, self.pt_x, c_ss.at[13 + 2 * self.g], c_rs.at[13 + 2 * self.g])
                yield to_other(self.pa, self.pa_x, c_ss.at[14 + 2 * self.g], c_rs.at[14 + 2 * self.g])

            def pa_scatter(self):
                return over_dp(4 * self.g, lambda j: self.pa.at[lax.rem(j, self.z.NA)], lambda k: self.pa_in.at[k], self.z.NA)

            def pa_gather(self):
                return over_dp(4 * self.g + 1, lambda j: self.pa_sum, lambda k: self.ga_place(), self.z.NA, True)

            def pb_scatter(self):
                return over_dp(4 * self.g + 2, lambda j: self.pb.at[lax.rem(j, self.z.NB)], lambda k: self.pb_in.at[k], self.z.NB)

            def pb_gather(self):
                return over_dp(
                    4 * self.g + 3, lambda j: self.pb_all.at[lax.rem(d, self.z.NB)], lambda k: self.pb_all.at[lax.rem(d, self.z.NB)], self.z.NB, True
                )

            def pt_scatter(self):
                return over_tensor(2 * self.g, lambda j: self.pt.at[j], lambda k: self.pt_in.at[k])

            def pt_gather(self):
                return over_tensor(2 * self.g + 1, lambda j: self.pt.at[t], lambda k: self.gr_place())

            def ga_place(self):
                return self.ga_out.at[:, pl.ds(pl.multiple_of(lax.rem(d, self.z.NA) * self.z.PW, 128), self.z.PW)]

            def gr_place(self):
                return self.gr_out.at[:, pl.ds(pl.multiple_of(t * self.z.GRW, 128), self.z.GRW)]

            def ga_store(self):
                return pltpu.make_async_copy(self.pa_sum, self.ga_place(), f_s.at[2 * self.g])

            def gr_store(self):
                return pltpu.make_async_copy(self.pt.at[t], self.gr_place(), f_s.at[2 * self.g + 1])

            def give(self):
                start_all(self.over())

            def given(self):
                sent_all(self.over())

            def begin(self):
                arrive_all(self.over())
                for j in range(T):
                    self.pt[j] = (self.pt[j].astype(F32) + self.pt_x[j].astype(F32)).astype(BF)
                start_all(self.pt_scatter())
                for j in range(self.z.NA):
                    self.pa[j] = (self.pa[j].astype(F32) + self.pa_x[j].astype(F32)).astype(BF)
                start_all(self.pa_scatter())

            def pass_on(self):
                arrive_all(self.pt_scatter())
                v = self.pt[t].astype(F32)
                for k in range(T - 1):
                    v = v + self.pt_in[k].astype(F32)
                put(self.pb, 0, self.z.SW, 0, v)
                pad(self.pb, 0, self.z.SW, self.z.GRW)
                start_all(self.pb_scatter())
                arrive_all(self.pa_scatter())

                def add():
                    v = self.pa[d].astype(F32)
                    for k in range(DP - 1):
                        v = v + self.pa_in[k].astype(F32)
                    self.pa_sum[...] = v.astype(BF)
                    self.ga_store().start()

                guarded(self.z.NA >= DP, d < self.z.NA, add)
                start_all(self.pa_gather())

            def add(self):
                arrive_all(self.pb_scatter())

                def add():
                    v = self.pb[d].astype(F32)
                    for k in range(DP - 1):
                        v = v + self.pb_in[k].astype(F32)
                    self.pb_all[d] = v.astype(BF)

                guarded(self.z.NB >= DP, d < self.z.NB, add)
                start_all(self.pb_gather())

            def spread(self):
                arrive_all(self.pb_gather())
                for j in range(self.z.NB):
                    lo, hi = j * self.z.SW, min((j + 1) * self.z.SW, self.z.GRW)
                    self.pt[t, :, lo:hi] = self.pb_all[j, :, 0:hi - lo]
                start_all(self.pt_gather())
                self.gr_store().start()

            def end(self):
                for copies in (self.pa_gather(), self.pt_gather()):
                    arrive_all(copies)
                for copies in (self.pa_scatter(), self.pa_gather(), self.pt_scatter(), self.pt_gather(),
                               self.pb_scatter(), self.pb_gather()):
                    sent_all(copies)
                guarded(self.z.NA >= DP, d < self.z.NA, lambda: self.ga_store().wait())
                self.gr_store().wait()

        early = Sums(0, EARLY, (pa_e, pa_x_e, pa_in_e, pa_sum_e, pt_e, pt_x_e, pt_in_e, pb_e, pb_in_e, pb_all_e), ga_early, gr_early)
        late = Sums(1, LATE, (pa_l, pa_x_l, pa_in_l, pa_sum_l, pt_l, pt_x_l, pt_in_l, pb_l, pb_in_l, pb_all_l), ga_late, gr_late)

        def gb_store():
            return pltpu.make_async_copy(gb, gb_out, f_s.at[4])

        def gb_begin():
            gb_over().wait_recv()
            gb[...] = gb[...] + gb_x[...]
            start_all(gb_tensor())

        def gb_pass_on():
            arrive_all(gb_tensor())
            total = gb[...]
            for k in range(T - 1):
                total = total + gb_t[k]
            gb_sum[...] = total
            start_all(gb_dp())

        def gb_end():
            arrive_all(gb_dp())
            sent_all(gb_tensor())
            total = gb_sum[...]
            for k in range(DP - 1):
                total = total + gb_d[k]
            gb[...] = total
            gb_store().start()
            sent_all(gb_dp())
            gb_store().wait()

        def on_core(core, *actions):
            @pl.when(s == core)
            def _():
                for action in actions:
                    action()

        gradient_to_hidden(1, lambda c: None)
        attention_back(1, lambda i: None)
        turn_back(1)
        project_back(1)
        on_core(0, gb_over().start)
        early_gradients(1)
        on_core(0, early.give)
        late_gradients(1)
        on_core(0, late.give)
        local_copy(h_hbm, hw, 1).start()
        local_copy(dg_hbm, dg, 2).start()
        on_core(1, early.begin)
        finish_backward(1)
        on_core(1, late.begin, gb_begin, early.pass_on)

        def meanwhile(c):
            for when, actions in ((1, (early.add, late.pass_on)), (2, (early.spread, gb_pass_on)), (3, (late.add,))):
                @pl.when(jnp.logical_and(s == 1, c == when))
                def _(actions=actions):
                    for action in actions:
                        action()

        def in_attention(i):
            if i == 1:
                on_core(0, early.begin)

        gradient_to_hidden(0, meanwhile)
        on_core(1, late.spread, early.end)
        on_core(0, early.given)
        local_copy(h_hbm, hw, 1).wait()
        early_gradients(0)
        on_core(1, early.give)
        attention_back(0, in_attention)
        on_core(1, late.end, gb_end)
        on_core(0, late.given, gb_over().wait_send)
        turn_back(0)
        late_gradients(0)
        on_core(1, late.give)
        on_core(0, early.pass_on, late.begin)
        gb[...] = jnp.zeros_like(gb)
        project_back(0)
        on_core(1, gb_over().start)
        on_core(0, early.add, late.pass_on, gb_begin, early.spread)
        finish_backward(0)
        on_core(0, late.add, gb_pass_on, late.spread, gb_end, early.end, late.end)
        on_core(1, early.given, late.given, gb_over().wait_send)

        ig_out(0).sent()
        act_out(0).sent()
        for layer in range(2):
            act_out(layer).arrive()
            ig_out(layer).arrive()
        for index in range(9):
            factor_over(index, s).wait_send()
        for index in range(4):
            for owner in range(DP):
                weight_over(index, s, owner).wait_send()

    def sums_scratch(z):
        return [
            pltpu.VMEM((z.NA, RANK, z.PW), BF),
            pltpu.VMEM((z.NA, RANK, z.PW), BF),
            pltpu.VMEM((DP - 1, RANK, z.PW), BF),
            pltpu.VMEM((RANK, z.PW), BF),
            pltpu.VMEM((T, RANK, z.GRW), BF),
            pltpu.VMEM((T, RANK, z.GRW), BF),
            pltpu.VMEM((T - 1, RANK, z.GRW), BF),
            pltpu.VMEM((z.NB, RANK, z.SW), BF),
            pltpu.VMEM((DP - 1, RANK, z.SW), BF),
            pltpu.VMEM((z.NB, RANK, z.SW), BF),
        ]

    any_spec = pl.BlockSpec(memory_space=pl.ANY)
    vmem_spec = pl.BlockSpec(memory_space=pltpu.VMEM)
    smem_spec = pl.BlockSpec(memory_space=pltpu.SMEM)
    shapes = jax.ShapeDtypeStruct
    return pl.pallas_call(
        kernel,
        out_shape=(
            shapes((M, R, D), F32), shapes((M, R, D), F32),
            shapes((8, D), F32),
            shapes((L, FFL), BF), shapes((L, FFL), BF),
            shapes((RANK, EARLY.NA * EARLY.PW), BF), shapes((RANK, EARLY.both), BF),
            shapes((RANK, LATE.NA * LATE.PW), BF), shapes((RANK, LATE.both), BF),
        ),
        in_specs=[any_spec] * 14 + [vmem_spec] * 3 + [smem_spec],
        out_specs=(any_spec,) * 9,
        scratch_shapes=[
            pltpu.VMEM((2, D, RANK), BF), pltpu.VMEM((2, RANK, 3 * QC), BF),
            pltpu.VMEM((2, QC, RANK), BF), pltpu.VMEM((2, RANK, D), BF),
            pltpu.VMEM((2, D, RANK), BF), pltpu.VMEM((2, RANK, FFL), BF),
            pltpu.VMEM((2, FFL, RANK), BF), pltpu.VMEM((2, RANK, D), BF),
            pltpu.VMEM((2, 8, D), F32),
            pltpu.VMEM((QC, DR), BF), pltpu.VMEM((FFL, DR), BF),
            pltpu.VMEM((2, D, 3 * QC), BF), pltpu.VMEM((2, D, FFL), BF),
            pltpu.VMEM((2, D, QC), BF), pltpu.VMEM((2, D, FFL), BF),
            pltpu.VMEM((M, L, D), BF),
            pltpu.VMEM((M, 2 * RANK, L), BF),
            pltpu.VMEM((M * PAIRS, L, 128), BF),
            pltpu.VMEM((M * PAIRS, L, 128), BF),
            pltpu.VMEM((M * PAIRS, L, 128), BF),
            pltpu.VMEM((M, QC, L), BF),
            pltpu.VMEM((QC, L), BF),
            pltpu.VMEM((M, QC, L), BF),
            pltpu.VMEM((M * HEADS, L), F32),
            pltpu.VMEM((L, FFL), BF),
            pltpu.VMEM((L, FFL), BF),
            pltpu.VMEM((M, 2 * RANK, L), BF),
            pltpu.VMEM((T, R, D), BF),
            pltpu.VMEM((2 * 6, B, D), BF),
            pltpu.VMEM((M, L, D), BF),
            pltpu.VMEM((PAIRS, L, 128), BF),
            pltpu.VMEM((8, L), F32),
            pltpu.VMEM((2 * RANK, L), BF),
            pltpu.VMEM((PAIRS, L, 128), F32),
            pltpu.VMEM((PAIRS, L, 128), F32),
            pltpu.VMEM((QC, L), F32),
            pltpu.VMEM((L, 3 * QC), BF),
            pltpu.VMEM((RANK, D), F32),
            pltpu.VMEM((8, D), F32),
            pltpu.VMEM((M, R, D), F32),
            pltpu.VMEM((R, D), F32),
            pltpu.VMEM((8, D), F32),
            pltpu.VMEM((8, D), F32),
            pltpu.VMEM((T - 1, 8, D), F32),
            pltpu.VMEM((DP - 1, 8, D), F32),
            *sums_scratch(EARLY), *sums_scratch(LATE),
            pltpu.SemaphoreType.DMA((6,)),
            pltpu.SemaphoreType.DMA((4, 2, DP)),
            pltpu.SemaphoreType.DMA((4, 2, DP)),
            pltpu.SemaphoreType.DMA((4, DP)),
            pltpu.SemaphoreType.DMA((4, DP)),
            pltpu.SemaphoreType.DMA((2 * 4,)),
            pltpu.SemaphoreType.DMA((2 * 4,)),
            pltpu.SemaphoreType.DMA((6,)),
            pltpu.SemaphoreType.DMA((4 * 6,)),
            pltpu.SemaphoreType.DMA((2 * 4,)),
            pltpu.SemaphoreType.DMA((2 * 4,)),
            pltpu.SemaphoreType.DMA((18,)),
            pltpu.SemaphoreType.DMA((18,)),
            pltpu.SemaphoreType.DMA((7,)),
            pltpu.SemaphoreType.DMA((10,)),
            pltpu.SemaphoreType.REGULAR,
            pltpu.SemaphoreType.DMA((5, T - 1)),
            pltpu.SemaphoreType.DMA((5, T - 1)),
            pltpu.SemaphoreType.DMA((9, DP - 1)),
            pltpu.SemaphoreType.DMA((9, DP - 1)),
        ],
        compiler_params=pltpu.CompilerParams(
            collective_id=0, has_side_effects=True, vmem_limit_bytes=63 * 2**20
        ),
    )


def make_finish(T, DP, M, R, D, QC, FFL, RANK):
    DR = D // DP
    EARLY, LATE = group_sizes(T, DP, D, QC, FFL)
    sliced = DR % 128 != 0
    loaded = (
        ((RANK, EARLY.NA * EARLY.PW), BF), ((RANK, EARLY.both), BF),
        ((RANK, LATE.NA * LATE.PW), BF), ((RANK, LATE.both), BF),
        ((DR, RANK), F32), ((3, RANK, QC), F32), ((3, DR, QC), BF),
        ((DR, RANK), F32), ((RANK, FFL), F32), ((DR, FFL), BF),
        ((FFL, RANK), F32), ((RANK, DR), F32), ((FFL, DR), BF),
        ((QC, RANK), F32), ((RANK, DR), F32), ((QC, DR), BF),
        ((M, R, D), F32), ((M, R, D), F32), ((8, D), F32),
    )
    made = (
        (RANK, FFL), (QC, RANK), (FFL, RANK), (D, RANK), (RANK, D), (RANK, D),
        (3, RANK, QC), (D, RANK), (3, DR, QC), (DR, FFL), (FFL, DR), (QC, DR),
    )
    n_in, n_made = len(loaded), len(made)

    def kernel(*refs):
        sources = list(refs[:n_in])
        results = refs[n_in:n_in + n_made + 2]
        gains, biases = refs[n_in + n_made + 2:n_in + n_made + 4]
        held = refs[n_in + n_made + 4:2 * n_in + n_made + 4]
        stage = refs[2 * n_in + n_made + 4:2 * n_in + 2 * n_made + 4]
        in_sem, out_sem = refs[-2:]
        d = lax.axis_index("dp")
        for index in (4, 7):
            sources[index] = sources[index].at[pl.ds(pl.multiple_of(d * DR, DR), DR)]
        if not sliced:
            for index in (11, 14):
                sources[index] = sources[index].at[:, pl.ds(pl.multiple_of(d * DR, 128), DR)]
        loads = [pltpu.make_async_copy(sources[n], held[n], in_sem.at[n]) for n in range(n_in)]
        for index in (0, 16, 17, *range(1, 16), 18):
            loads[index].start()
        stores = []

        def take(*indices):
            for index in indices:
                loads[index].wait()

        def store(index, source):
            copy = pltpu.make_async_copy(source, results[index], out_sem.at[index])
            copy.start()
            stores.append(copy)

        def give(index, value):
            stage[index][...] = value
            store(index, stage[index])

        def factor(ref):
            return (ADAPTER_SCALE * ref).astype(BF)

        take(0)
        ga = held[0]
        give(0, ga[:, 0:FFL].astype(F32))
        give(1, ga[:, FFL:FFL + QC].astype(F32).T)
        give(2, ga[:, FFL + QC:2 * FFL + QC].astype(F32).T)
        for index in range(2):
            take(16 + index)
            store(12 + index, held[16 + index])
        take(1)
        gr = held[1]
        give(3, gr[:, 0:D].astype(F32).T)
        give(4, gr[:, D:2 * D].astype(F32))
        give(5, gr[:, 2 * D:3 * D].astype(F32))
        take(2, 3)
        for part in range(3):
            stage[6][part] = held[2][:, part * QC:(part + 1) * QC].astype(F32)
        store(6, stage[6])
        give(7, held[3][...].astype(F32).T)
        take(4, 5, 6)
        for part in range(3):
            stage[8][part] = held[6][part].astype(F32) + nn(held[4][...].astype(BF), factor(held[5][part]))
        store(8, stage[8])
        take(7, 8, 9)
        give(9, held[9][...].astype(F32) + nn(held[7][...].astype(BF), factor(held[8][...])))
        take(10, 11, 12)
        give(10, held[12][...].astype(F32) + nn(held[10][...].astype(BF), factor(held[11][...])))
        take(13, 14, 15)
        give(11, held[15][...].astype(F32) + nn(held[13][...].astype(BF), factor(held[14][...])))
        take(18)
        gains[...] = held[18][0:2]
        biases[...] = held[18][2:4]
        for copy in stores:
            copy.wait()

    any_spec = pl.BlockSpec(memory_space=pl.ANY)
    rows = ((M, R, D),) * 2
    vmem_spec = pl.BlockSpec(memory_space=pltpu.VMEM)
    return pl.pallas_call(
        kernel,
        out_shape=tuple(jax.ShapeDtypeStruct(shape, F32) for shape in made + rows + ((2, D),) * 2),
        in_specs=[any_spec] * n_in,
        out_specs=(any_spec,) * (n_made + 2) + (vmem_spec,) * 2,
        scratch_shapes=[
            *(pltpu.VMEM(shape, dtype) for shape, dtype in loaded),
            *(pltpu.VMEM(shape, F32) for shape in made),
            pltpu.SemaphoreType.DMA((n_in,)), pltpu.SemaphoreType.DMA((n_made + 2,)),
        ],
        compiler_params=pltpu.CompilerParams(vmem_limit_bytes=63 * 2**20),
    )


def rope_table(length):
    half = ROT // 2
    inverse = np.float32(10000.0) ** (-np.arange(half, dtype=np.float32) * np.float32(2.0 / ROT))
    angles = np.arange(length, dtype=np.float32)[:, None] * inverse[None, :]
    cosine, sine = np.cos(angles.astype(np.float64)), np.sin(angles.astype(np.float64))
    rest = np.zeros((length, HEAD - ROT))
    return np.concatenate(
        [cosine, cosine, rest + 1.0, -sine, sine, rest], axis=-1
    ).astype(np.float32)


def solution(mesh):
    T = mesh.shape["tensor"]
    DP = mesh.shape["dp"]

    def per_device(
        inputs, cotangent, split,
        query_key_value_weight, output_weight, up_weight, down_weight,
        qkv_adapter_input, qkv_adapter_output, out_adapter_input, out_adapter_output,
        up_adapter_input, up_adapter_output, down_adapter_input, down_adapter_output,
        ln_gain, ln_bias,
    ):
        M, R, D = inputs.shape
        QC = output_weight.shape[1]
        FFL = up_weight.shape[2]
        RANK = qkv_adapter_input.shape[2]
        L = R * T
        wq = query_key_value_weight[0].transpose(1, 0, 2)
        bq = qkv_adapter_output[0].transpose(1, 0, 2)
        DR = D // DP
        kernel = make_kernel(T, DP, M, R, D, QC, FFL, RANK)
        act, ig, gb, _, _, ga_early, gr_early, ga_late, gr_late = kernel(
            inputs, cotangent, wq, up_weight[0], output_weight[0], down_weight[0],
            qkv_adapter_input[0], bq,
            out_adapter_input[0], out_adapter_output[0],
            up_adapter_input[0], up_adapter_output[0],
            down_adapter_input[0], down_adapter_output[0],
            ln_gain[0], ln_bias[0], jnp.asarray(rope_table(L)), split[:, 0],
        )
        out_factor, down_factor = out_adapter_output[0], down_adapter_output[0]
        if DR % 128 != 0:
            start = lax.axis_index("dp") * DR
            out_factor = lax.dynamic_slice_in_dim(out_factor, start, DR, 1)
            down_factor = lax.dynamic_slice_in_dim(down_factor, start, DR, 1)
        (
            b_up, a_out, a_down, a_up, b_out, b_down, b_qkv, a_qkv, c_qkv, c_up, c_down, c_out, act, ig,
            grad_gain, grad_bias,
        ) = make_finish(T, DP, M, R, D, QC, FFL, RANK)(
            ga_early, gr_early, ga_late, gr_late,
            qkv_adapter_input[0], bq, wq,
            up_adapter_input[0], up_adapter_output[0], up_weight[0],
            down_adapter_input[0], down_factor, down_weight[0],
            out_adapter_input[0], out_factor, output_weight[0],
            act, ig, gb,
        )
        return (
            act[None], ig[None],
            a_qkv[None], b_qkv.transpose(1, 0, 2)[None],
            a_out[None], b_out[None], a_up[None], b_up[None], a_down[None], b_down[None],
            grad_gain[None], grad_bias[None],
            c_qkv.transpose(1, 0, 2)[None], c_out[None], c_up[None], c_down[None],
        )

    rows = P(None, ("dp", "tensor"), None)
    whole = P("section", None, None)
    in_specs = (
        rows, rows, P(None, "dp"),
        P("section", "dp", None, "tensor"), P("section", "tensor", "dp"),
        P("section", "dp", "tensor"), P("section", "tensor", "dp"),
        whole, P("section", None, None, "tensor"), P("section", "tensor", None), whole,
        whole, P("section", None, "tensor"), P("section", "tensor", None), whole,
        whole, whole,
    )
    layer_rows = P("section", None, ("dp", "tensor"), None)
    out_specs = (
        layer_rows, layer_rows,
        whole, P("section", None, None, "tensor"), P("section", "tensor", None), whole,
        whole, P("section", None, "tensor"), P("section", "tensor", None), whole,
        whole, whole,
        P("section", "dp", None, "tensor"), P("section", "tensor", "dp"),
        P("section", "dp", "tensor"), P("section", "tensor", "dp"),
    )
    return jax.shard_map(
        per_device, mesh=mesh, in_specs=in_specs, out_specs=out_specs, check_vma=False
    )
```
